128 devices in a mesh: px: 8 (over x, core), py: 16 (over z, y).
Axes of the slice: x: 4, y: 4, z: 4, core: 2. Of those that a mesh axis runs over, the one named last changes fastest.
Arguments:
- residual: float32 [32, 64, 8, 8, 8, 128], P('px', 'py'), may hold values from -4 to 4
- element_stiffness_scale: float32 [32, 64, 128], P('px', 'py'), may hold values from 0.25 to 4
- fine_basis: float32 [3, 10, 10], replicated, may hold values from -2 to 2
- fine_eigen: float32 [3, 10], replicated, may hold values from 0.3 to 3
- middle_basis: float32 [3, 6, 6], replicated, may hold values from -2.5 to 2.5
- middle_eigen: float32 [3, 6], replicated, may hold values from 0.3 to 3
Outputs:
- correction: float32 [32, 64, 8, 8, 8, 128], P('px', 'py')
The draws below stay inside these ranges and needn't reach their ends.
All inputs are finite; a program needn't handle non-finite values.
Results may differ from the reference program's by a relative error of at most 0.000098.
Values sent between devices are 32-bit elements; how exact they have to be, the bound alone decides.
No kernel may reach another device: no remote copies, remote signals or barrier semaphores. Data moves between devices by JAX's collectives and lax.ppermute only.
A program may use at most 128 MiB of HBM per device.

```python
import math
import jax
import jax.numpy as jnp
from jax import lax

FINE_NODE_COUNT = 8
NODES_MID = 4
ELEMENTS_Z = 128
ELEMENTS_X = 32
ELEMENTS_Y = 64


def draw_residual(key, part):
    key = jax.random.fold_in(key, 11)
    complete_shape = (ELEMENTS_X, ELEMENTS_Y, FINE_NODE_COUNT, FINE_NODE_COUNT, FINE_NODE_COUNT, ELEMENTS_Z)
    return jnp.clip(jax.random.normal(key, complete_shape, jnp.float32), -4.0, 4.0)


def steps_of(own_key, extent, split, smallest, top_value):
    def one(position, shards_of):
        draws = jax.random.uniform(jax.random.fold_in(jax.random.fold_in(own_key, 6), position), (shards_of,), jnp.float32, smallest / len(split), top_value / len(split))
        return jnp.repeat(jnp.exp(draws), extent[position] // shards_of).reshape((-1,) + (1,) * (len(extent) - position - 1))

    loudness = one(*split[0])
    for cut in split[1:]:
        loudness = loudness * one(*cut)
    return loudness


def scatter_about(stream_key, shape, deviation, most, kind=jnp.bfloat16):
    values = jax.random.normal(stream_key, shape, jnp.float32) * deviation
    return jnp.minimum(jnp.maximum(values, -most), most).astype(kind)


def setup_inputs(seed: int = 0) -> dict:
    streams_of = jax.random.split(jax.random.key(seed), 7)
    residual = draw_residual(jax.random.fold_in(streams_of[6], 71), 0)
    element_stiffness_scale = jnp.clip(jnp.exp(math.log(4.0) - 2.7725887 * jax.random.uniform(streams_of[1], (ELEMENTS_X, ELEMENTS_Y, ELEMENTS_Z), jnp.float32) ** steps_of(streams_of[1], (ELEMENTS_X, ELEMENTS_Y, ELEMENTS_Z), ((0, 8), (1, 16)), -0.2, 0.2)), 0.25, 4.0)
    fine_basis = scatter_about(streams_of[2], (3, FINE_NODE_COUNT + 2, FINE_NODE_COUNT + 2), (FINE_NODE_COUNT + 2) ** -0.5, 2.0, jnp.float32)
    fine_eigen = jnp.clip(jnp.exp(jax.random.uniform(streams_of[3], (3, FINE_NODE_COUNT + 2), jnp.float32, math.log(0.3), math.log(3.0))), 0.3, 3.0)
    middle_basis = scatter_about(streams_of[4], (3, NODES_MID + 2, NODES_MID + 2), (NODES_MID + 2) ** -0.5, 2.5, jnp.float32)
    middle_eigen = jnp.clip(jnp.exp(jax.random.uniform(streams_of[5], (3, NODES_MID + 2), jnp.float32, math.log(0.3), math.log(3.0))), 0.3, 3.0)
    return dict(residual=residual, element_stiffness_scale=element_stiffness_scale, fine_basis=fine_basis, fine_eigen=fine_eigen, middle_basis=middle_basis, middle_eigen=middle_eigen)


HIGHEST = lax.Precision.HIGHEST
coarse_stiff = 24.0
coarse_mass = 0.5


def lobatto(node_count):
    positions = jnp.arange(node_count, dtype=jnp.int32).astype(jnp.float32)
    return -jnp.cos(positions * (math.pi / (node_count - 1)))


def interpolation(fine_count, coarse_count):
    fine_points = lobatto(fine_count)
    coarse_points = lobatto(coarse_count)
    numerator = fine_points[:, None, None] - coarse_points[None, None, :]
    distance = coarse_points[None, :, None] - coarse_points[None, None, :]
    same_node = jnp.eye(coarse_count, dtype=bool)[None]
    factors = jnp.where(same_node, jnp.float32(1.0), numerator / jnp.where(same_node, jnp.float32(1.0), distance))
    return jnp.prod(factors, axis=2)


def inverse_multiplicity(node_count):
    positions = jnp.arange(node_count, dtype=jnp.int32)
    line_weight = jnp.where((positions == 0) | (positions == node_count - 1), 0.5, 1.0).astype(jnp.float32)
    return (line_weight[:, None, None] * line_weight[None, :, None] * line_weight[None, None, :])[..., None]


def hartley(node_count):
    positions = jnp.arange(node_count, dtype=jnp.int32)
    phase = (positions[:, None] * positions[None, :]) % node_count
    angle = phase.astype(jnp.float32) * (2.0 * math.pi / node_count)
    return jnp.cos(angle) + jnp.sin(angle)


def line_eigen(positions, node_count):
    return 2.0 - 2.0 * jnp.cos(positions.astype(jnp.float32) * (2.0 * math.pi / node_count))


def coarse_denominator(line_x, line_y, line_z):
    return coarse_stiff * (line_x[:, None, None] + line_y[None, :, None] + line_z[None, None, :]) + coarse_mass


def coarse_solve(vertex):
    count_x, count_y, count_z = vertex.shape
    spectrum = jnp.einsum('kx,xyz->kyz', hartley(count_x), vertex, precision=HIGHEST)
    spectrum = jnp.einsum('ky,xyz->xkz', hartley(count_y), spectrum, precision=HIGHEST)
    spectrum = jnp.einsum('kz,xyz->xyk', hartley(count_z), spectrum, precision=HIGHEST)
    denominator = coarse_denominator(
        line_eigen(jnp.arange(count_x, dtype=jnp.int32), count_x),
        line_eigen(jnp.arange(count_y, dtype=jnp.int32), count_y),
        line_eigen(jnp.arange(count_z, dtype=jnp.int32), count_z))
    spectrum = spectrum / denominator
    spectrum = jnp.einsum('kx,xyz->kyz', hartley(count_x), spectrum, precision=HIGHEST)
    spectrum = jnp.einsum('ky,xyz->xkz', hartley(count_y), spectrum, precision=HIGHEST)
    spectrum = jnp.einsum('kz,xyz->xyk', hartley(count_z), spectrum, precision=HIGHEST)
    return spectrum / float(count_x * count_y * count_z)


def corner_values(block):
    size_x = block.shape[0] - 1
    size_y = block.shape[1] - 1
    planes = []
    for step_a in (0, 1):
        for step_b in (0, 1):
            for step_c in (0, 1):
                shifted = block[step_a:step_a + size_x, step_b:step_b + size_y]
                planes.append(jnp.roll(shifted, -step_c, axis=2))
    stacked = jnp.stack(planes, axis=2)
    return stacked.reshape(size_x, size_y, 2, 2, 2, block.shape[2])


def restrict(values, interp):
    values = jnp.einsum('fi,...fghz->...ighz', interp, values, precision=HIGHEST)
    values = jnp.einsum('gj,...ighz->...ijhz', interp, values, precision=HIGHEST)
    return jnp.einsum('hk,...ijhz->...ijkz', interp, values, precision=HIGHEST)


def prolong(values, interp):
    values = jnp.einsum('fi,...ighz->...fghz', interp, values, precision=HIGHEST)
    values = jnp.einsum('gj,...fjhz->...fghz', interp, values, precision=HIGHEST)
    return jnp.einsum('hk,...fgkz->...fghz', interp, values, precision=HIGHEST)


def local_solve(extended, elem_scale, eigen_basis, eigen_values):
    spectrum = jnp.einsum('ai,...abcz->...ibcz', eigen_basis[0], extended, precision=HIGHEST)
    spectrum = jnp.einsum('bj,...ibcz->...ijcz', eigen_basis[1], spectrum, precision=HIGHEST)
    spectrum = jnp.einsum('ck,...ijcz->...ijkz', eigen_basis[2], spectrum, precision=HIGHEST)
    total = eigen_values[0][:, None, None] + eigen_values[1][None, :, None] + eigen_values[2][None, None, :]
    spectrum = spectrum / (elem_scale[..., None, None, None, :] * total[..., None])
    result = jnp.einsum('ai,...ijkz->...ajkz', eigen_basis[0], spectrum, precision=HIGHEST)
    result = jnp.einsum('bj,...ajkz->...abkz', eigen_basis[1], result, precision=HIGHEST)
    return jnp.einsum('ck,...abkz->...abcz', eigen_basis[2], result, precision=HIGHEST)


def face_sum(values):
    last_node = values.shape[2] - 1
    low_side = values[:, :, :, 0]
    high_side = values[:, :, :, last_node]
    values = values.at[:, :, :, 0].set(low_side + jnp.roll(high_side, 1, axis=1))
    values = values.at[:, :, :, last_node].set(high_side + jnp.roll(low_side, -1, axis=1))
    low_side = values[:, :, :, :, 0]
    high_side = values[:, :, :, :, last_node]
    values = values.at[:, :, :, :, 0].set(low_side + jnp.roll(high_side, 1, axis=4))
    values = values.at[:, :, :, :, last_node].set(high_side + jnp.roll(low_side, -1, axis=4))
    low_side = values[:, :, 0]
    high_side = values[:, :, last_node]
    values = values.at[:, :, 0].set(low_side + jnp.roll(high_side, 1, axis=0))
    values = values.at[:, :, last_node].set(high_side + jnp.roll(low_side, -1, axis=0))
    return values


def extend_slice(layer_slab, low_face, high_face):
    node_count = layer_slab.shape[1]
    inner_node = node_count - 2
    extended = jnp.zeros((layer_slab.shape[0], node_count + 2, node_count + 2, node_count + 2, layer_slab.shape[4]), layer_slab.dtype)
    extended = extended.at[:, 1:-1, 1:-1, 1:-1].set(layer_slab)
    extended = extended.at[:, 0, 1:-1, 1:-1].set(low_face)
    extended = extended.at[:, -1, 1:-1, 1:-1].set(high_face)
    extended = extended.at[:, 1:-1, 0, 1:-1].set(jnp.roll(layer_slab[:, :, inner_node], 1, axis=0))
    extended = extended.at[:, 1:-1, -1, 1:-1].set(jnp.roll(layer_slab[:, :, 1], -1, axis=0))
    extended = extended.at[:, 1:-1, 1:-1, 0].set(jnp.roll(layer_slab[:, :, :, inner_node], 1, axis=3))
    extended = extended.at[:, 1:-1, 1:-1, -1].set(jnp.roll(layer_slab[:, :, :, 1], -1, axis=3))
    return extended


def schwarz(values, element_stiffness_scale, eigen_basis, eigen_values):
    node_count = values.shape[2]
    low_faces = jnp.roll(values[:, :, node_count - 2], 1, axis=0)
    high_faces = jnp.roll(values[:, :, 1], -1, axis=0)

    def one_slab(pieces):
        layer_slab, low_face, high_face, slab_scale = pieces
        extended = extend_slice(layer_slab, low_face, high_face)
        return local_solve(extended, slab_scale, eigen_basis, eigen_values)[:, 1:-1, 1:-1, 1:-1]

    return lax.map(one_slab, (values, low_faces, high_faces, element_stiffness_scale))


def reference(residual, element_stiffness_scale, fine_basis, fine_eigen, middle_basis, middle_eigen):
    fine_count = residual.shape[2]
    middle_count = middle_basis.shape[1] - 2
    interp_fine = interpolation(fine_count, middle_count)
    interp_mid = interpolation(middle_count, 2)
    fine_weight = inverse_multiplicity(fine_count)
    middle_weight = inverse_multiplicity(middle_count)
    fine_rhs = face_sum(residual)
    fine_part = fine_weight * face_sum(schwarz(fine_rhs, element_stiffness_scale, fine_basis, fine_eigen))
    middle_rhs = face_sum(restrict(fine_weight * fine_rhs, interp_fine))
    middle_part = middle_weight * face_sum(schwarz(middle_rhs, element_stiffness_scale, middle_basis, middle_eigen))
    coarse_rhs = face_sum(restrict(middle_weight * middle_rhs, interp_mid))
    vertex = coarse_rhs[:, :, 0, 0, 0]
    solution = coarse_solve(vertex)
    wrapped = jnp.concatenate([solution, solution[:1]], axis=0)
    wrapped = jnp.concatenate([wrapped, wrapped[:, :1]], axis=1)
    corner = corner_values(wrapped)
    return fine_part + prolong(middle_part + prolong(corner, interp_mid), interp_fine)
```

```python
import functools
import math

import jax
import jax.numpy as jnp
import ml_dtypes
import numpy as np
from jax import lax
from jax.experimental import pallas as pl
from jax.experimental.pallas import tpu as pltpu
from jax.sharding import PartitionSpec as P

F32, BF16 = jnp.float32, jnp.bfloat16
HIGHEST = lax.Precision.HIGHEST
LANES = 128
EX = EY = 4
VMEM_LIMIT = 56 * 1024 * 1024


def lobatto(count):
    return -np.cos(np.arange(count) * (np.pi / (count - 1)))


def interpolation(fine_count, coarse_count):
    fine, coarse = lobatto(fine_count), lobatto(coarse_count)
    out = np.ones((fine_count, coarse_count))
    for j in range(coarse_count):
        for m in range(coarse_count):
            if m != j:
                out[:, j] *= (fine - coarse[m]) / (coarse[j] - coarse[m])
    return out


def hartley(count):
    phase = np.outer(np.arange(count), np.arange(count)) % count
    angle = phase * (2.0 * np.pi / count)
    return np.cos(angle) + np.sin(angle)


def line_eigen(count):
    return 2.0 - 2.0 * np.cos(np.arange(count) * (2.0 * np.pi / count))


def split_np(values):
    values = np.asarray(values, np.float32)
    high = values.astype(ml_dtypes.bfloat16)
    low = (values - high.astype(np.float32)).astype(ml_dtypes.bfloat16)
    return high, low


def split(values):
    high = values.astype(BF16)
    return high, (values - high.astype(F32)).astype(BF16)


def dot(left, right):
    return jnp.dot(left, right, preferred_element_type=F32)


def exact_dot(left, right, contract=((1,), (0,))):
    return lax.dot_general(
        left, right, (contract, ((), ())), precision=HIGHEST, preferred_element_type=F32
    )


INTERP_FINE = interpolation(8, 4)
INTERP_MID = interpolation(4, 2)
INTERP_ALL = INTERP_FINE @ INTERP_MID


def kron3(m):
    return np.kron(np.kron(m, m), m)


def restrict_matrix():
    rows = np.zeros((80, 512))
    rows[:64] = kron3(INTERP_FINE).T
    rows[64:72] = kron3(INTERP_ALL).T
    high, low = split_np(rows)
    return np.concatenate([high, low], axis=0)


def prolong_matrix():
    fine = kron3(INTERP_FINE)
    coarse = np.zeros((512, 16))
    coarse[:, :8] = kron3(INTERP_ALL)
    fine_high, fine_low = split_np(fine)
    coarse_high, coarse_low = split_np(coarse)
    return np.concatenate(
        [fine_high, fine_high, fine_low, coarse_high, coarse_high, coarse_low], axis=1
    )


def vertex_matrices():
    out = np.zeros((2, 32, 128), np.float32)
    for ex in range(EX):
        for ey in range(EY):
            for i in (0, 1):
                for j in (0, 1):
                    for k in (0, 1):
                        column = (ex * EY + ey) * 8 + i * 4 + j * 2 + k
                        out[k, (ex + i) * 5 + ey + j, column] = 1.0
    return out


class Level:
    def __init__(self, n):
        self.n = n
        self.wide = n + 2
        self.core = n * n
        self.rim = 4 * n
        self.depth = self.core + self.rim
        self.modes = -(-(self.wide * self.wide) // 16) * 16
        self.planes = EX * n + 4

    def tables(self):
        n, wide = self.n, self.wide
        first = np.zeros((2 * self.modes, wide), np.float32)
        second = np.zeros((2 * self.modes, wide), np.float32)
        for half in (0, 1):
            for j in range(wide):
                for k in range(wide):
                    first[half * self.modes + j * wide + k, j] = 1.0
                    second[half * self.modes + j * wide + k, k] = 1.0
        inner = list(range(1, n + 1))
        points = [(b, c) for b in inner for c in inner]
        points += [(0, c) for c in inner] + [(n + 1, c) for c in inner]
        points += [(b, 0) for b in inner] + [(b, n + 1) for b in inner]
        pick_b = np.zeros((wide, 2 * self.depth), np.float32)
        pick_c = np.zeros((wide, 2 * self.depth), np.float32)
        for half in (0, 1):
            for column, (b, c) in enumerate(points):
                pick_b[b, half * self.depth + column] = 1.0
                pick_c[c, half * self.depth + column] = 1.0
        return (
            first,
            second,
            pick_b,
            pick_c,
            np.ascontiguousarray(pick_b[:, : self.core].T),
            np.ascontiguousarray(pick_c[:, : self.core].T),
        )


FINE, MID = Level(8), Level(4)

HALO_ROWS = 640
DIAG_ROWS = 40
FACE_ROWS = 320
EDGE_ROWS = 16


def pack_kernel(
    residual,
    restrict,
    vertex_pick,
    hartley_z,
    x_up,
    x_down,
    y_up,
    y_down,
    d_uu,
    d_ud,
    d_du,
    d_dd,
    middle,
    vertex,
    field,
    corners,
    sems,
):
    copies = []
    for ex in range(EX):
        copy = pltpu.make_async_copy(residual.at[ex], field.at[ex], sems.at[ex])
        copy.start()
        copies.append(copy)
    for ex in range(EX):
        copies[ex].wait()
        for pair in range(EY // 2):
            ey = 2 * pair
            values = jnp.concatenate(
                [field[ex, ey].reshape(512, LANES), field[ex, ey + 1].reshape(512, LANES)], axis=1
            )
            high, low = split(values)
            upper = dot(restrict[...], high)
            lower = dot(restrict[0:80, :], low)
            total = upper[0:80] + upper[80:160] + lower
            for h in (0, 1):
                part = total[:, h * LANES : (h + 1) * LANES]
                for i in range(4):
                    middle[ex, ey + h, i] = part[16 * i : 16 * i + 16]
                column = ex * EY + ey + h
                corners[8 * column : 8 * column + 8] = part[64:72]
    for out, ex, nodes, mids in ((x_up, EX - 1, (7, 6), (3, 2)), (x_down, 0, (0, 1), (0, 1))):
        for layer in (0, 1):
            for ey in range(EY):
                row = (layer * EY + ey) * 64
                out[row : row + 64] = field[ex, ey, nodes[layer]]
                row = 512 + (layer * EY + ey) * 16
                out[row : row + 16] = middle[ex, ey, mids[layer]]
    for out, ey, nodes, mids in ((y_up, EY - 1, (7, 6), (3, 2)), (y_down, 0, (0, 1), (0, 1))):
        for layer in (0, 1):
            for ex in range(EX):
                for a in range(8):
                    row = (layer * EX + ex) * 64 + a * 8
                    line = nodes[layer] * 8
                    out[row : row + 8] = field[ex, ey, a, line : line + 8]
                for a in range(4):
                    row = 512 + (layer * EX + ex) * 16 + a * 4
                    line = mids[layer] * 4
                    out[row : row + 4] = middle[ex, ey, a, line : line + 4]
    for out, up_x, up_y in ((d_uu, 1, 1), (d_ud, 1, 0), (d_du, 0, 1), (d_dd, 0, 0)):
        ex, ey = (EX - 1) * up_x, (EY - 1) * up_y
        out[32:40] = jnp.zeros((8, LANES), F32)
        for n, source, base in ((8, field, 0), (4, middle, 24)):
            face_a, inner_a = (n - 1, n - 2) if up_x else (0, 1)
            face_b, inner_b = (n - 1, n - 2) if up_y else (0, 1)
            for line, (a, b) in enumerate(((face_a, face_b), (face_a, inner_b), (inner_a, face_b))):
                out[base + line * n : base + line * n + n] = source[ex, ey, a, b * n : b * n + n]
    values = corners[...]
    low = exact_dot(vertex_pick[0], values)
    high = exact_dot(vertex_pick[1], values)
    total = low + pltpu.roll(high, 1, 1)
    vertex[...] = exact_dot(total, hartley_z[...])


def pack(residual):
    halo = jax.ShapeDtypeStruct((HALO_ROWS, LANES), F32)
    diag = jax.ShapeDtypeStruct((DIAG_ROWS, LANES), F32)
    vmem = pl.BlockSpec(memory_space=pltpu.VMEM)
    return pl.pallas_call(
        pack_kernel,
        out_shape=[halo] * 4
        + [diag] * 4
        + [
            jax.ShapeDtypeStruct((EX, EY, 4, 16, LANES), F32),
            jax.ShapeDtypeStruct((32, LANES), F32),
        ],
        in_specs=[pl.BlockSpec(memory_space=pl.ANY)] + [vmem] * 3,
        out_specs=[vmem] * 10,
        scratch_shapes=[
            pltpu.VMEM((EX, EY, 8, 64, LANES), F32),
            pltpu.VMEM((128, LANES), F32),
            pltpu.SemaphoreType.DMA((EX,)),
        ],
        compiler_params=pltpu.CompilerParams(vmem_limit_bytes=VMEM_LIMIT),
        cost_estimate=pl.CostEstimate(flops=10**9, bytes_accessed=8 * 10**6, transcendentals=0),
        name="pack",
    )(
        residual,
        jnp.asarray(restrict_matrix()),
        jnp.asarray(vertex_matrices()),
        jnp.asarray(hartley(128), F32),
    )


def sum_lines(ref, lead, n, scale=None):
    count = ref.shape[-2] // n
    low_rows = lead + (pl.ds(0, count, stride=n), slice(None))
    high_rows = lead + (pl.ds(n - 1, count, stride=n), slice(None))
    low, high = ref[low_rows], ref[high_rows]
    new_low = low + pltpu.roll(high, 1, 1)
    new_high = high + pltpu.roll(low, LANES - 1, 1)
    if scale is not None:
        new_low, new_high = new_low * scale, new_high * scale
    ref[low_rows] = new_low
    ref[high_rows] = new_high


def halo_lines(level, halo, layer, plane):
    n = level.n
    start = layer * EX * n * n + plane * n + (0 if n == 8 else 512)
    return halo[start : start + n]


def diag_line(level, diag, line):
    n = level.n
    start = line * n + (0 if n == 8 else 24)
    return diag[start : start + n]


def assemble(level, planes, rims, sides, x_low, x_high, y_low, y_high, diags):
    n, core = level.n, level.core
    last = EX * n + 3
    base = 0 if n == 8 else 512
    for ey in range(EY):
        row = base + ey * core
        planes[ey, 2] += x_low[row : row + core]
        planes[ey, last - 2] += x_high[row : row + core]
        for ex in range(EX - 1):
            left = 2 + ex * n + n - 1
            total = planes[ey, left] + planes[ey, left + 1]
            planes[ey, left] = total
            planes[ey, left + 1] = total
        row = base + (EY + ey) * core
        planes[ey, 0] = x_low[row : row + core]
        planes[ey, last] = x_high[row : row + core]
    for side, halo in ((0, y_low), (1, y_high)):
        for layer in (0, 1):
            kind = 2 * side + layer
            start = base + layer * EX * core
            sides[kind] = halo[start : start + EX * core]
            sides[kind, 0:n] += diag_line(level, diags[0][side], layer)
            sides[kind, EX * core - n : EX * core] += diag_line(level, diags[1][side], layer)
            for ex in range(EX - 1):
                row = ex * core + core
                total = sides[kind, row - n : row] + sides[kind, row : row + n]
                sides[kind, row - n : row] = total
                sides[kind, row : row + n] = total
    for plane in range(EX * n):
        row = plane * n
        planes[0, 2 + plane, 0:n] += sides[0, row : row + n]
        planes[EY - 1, 2 + plane, core - n : core] += sides[2, row : row + n]
    for plane, diag in ((0, diags[0]), (last, diags[1])):
        planes[0, plane, 0:n] += diag_line(level, diag[0], 2)
        planes[EY - 1, plane, core - n : core] += diag_line(level, diag[1], 2)
    for ey in range(EY - 1):
        for plane in [0, last] + list(range(2, 2 + EX * n)):
            total = planes[ey, plane, core - n : core] + planes[ey + 1, plane, 0:n]
            planes[ey, plane, core - n : core] = total
            planes[ey + 1, plane, 0:n] = total
    for ey in range(EY):
        for plane in [0, last] + list(range(2, 2 + EX * n)):
            sum_lines(planes, (ey, plane), n)
    for kind in (1, 3):
        sum_lines(sides, (kind,), n)
    for ey in range(EY):
        for plane in range(EX * n):
            at = 2 + plane
            row = plane * n
            low = planes[ey - 1, at, core - 2 * n : core - n] if ey else sides[1, row : row + n]
            high = planes[ey + 1, at, n : 2 * n] if ey < EY - 1 else sides[3, row : row + n]
            rims[ey, plane, 0:n] = low
            rims[ey, plane, n : 2 * n] = high
            rims[ey, plane, 2 * n : 3 * n] = pltpu.roll(
                planes[ey, at, pl.ds(n - 2, n, stride=n), :], 1, 1
            )
            rims[ey, plane, 3 * n : 4 * n] = pltpu.roll(
                planes[ey, at, pl.ds(1, n, stride=n), :], LANES - 1, 1
            )


def build_tables(level, tables, basis, eigen, forward, backward, inverse):
    first, second, pick_b, pick_c, core_b, core_c = tables
    modes, depth = level.modes, level.depth
    rows_b = exact_dot(first[0:modes], basis[1], ((1,), (1,)))
    rows_c = exact_dot(second[0:modes], basis[2], ((1,), (1,)))
    matrix = exact_dot(rows_b, pick_b[...]) * exact_dot(rows_c, pick_c[...])
    high, low = split(matrix)
    keep = lax.broadcasted_iota(jnp.int32, matrix.shape, 1) < depth
    forward[0:modes] = high
    forward[modes : 2 * modes] = jnp.where(keep, low.astype(F32), 0.0).astype(BF16)
    out_b = exact_dot(exact_dot(core_b[...], basis[1]), first[...], ((1,), (1,)))
    out_c = exact_dot(exact_dot(core_c[...], basis[2]), second[...], ((1,), (1,)))
    matrix = out_b * out_c
    high, low = split(matrix)
    keep = lax.broadcasted_iota(jnp.int32, matrix.shape, 1) < modes
    backward[0 : level.core] = high
    backward[level.core : 2 * level.core] = jnp.where(keep, low.astype(F32), 0.0).astype(BF16)
    wide = level.wide
    spread_b = jnp.broadcast_to(eigen[1:2, :], (LANES, wide))
    spread_c = jnp.broadcast_to(eigen[2:3, :], (LANES, wide))
    lines = exact_dot(first[0:modes], spread_b, ((1,), (1,)))
    lines += exact_dot(second[0:modes], spread_c, ((1,), (1,)))
    for i in range(wide):
        inverse[i] = 1.0 / (lines + eigen[0:1, i : i + 1])


def solve_pair(level, q, planes, rims, coeff, forward, backward, inverse, scale, spectrum, hats, out):
    n, wide, core, modes, depth = level.n, level.wide, level.core, level.modes, level.depth
    ex = q // 2
    ey = (q % 2) * 2
    base = ex * n
    offsets = [0] + [2 + a for a in range(n)] + [n + 3]

    def contract(load, nodes, row):
        held = [[load(h, e) for h in (0, 1)] for e in nodes]
        for i in range(wide):
            for h in (0, 1):
                total = coeff[nodes[0], i] * held[0][h]
                for position in range(1, len(nodes)):
                    total += coeff[nodes[position], i] * held[position][h]
                high, low = split(total)
                lanes = slice(h * LANES, (h + 1) * LANES)
                spectrum[i, row : row + 16, lanes] = high
                spectrum[i, depth + row : depth + row + 16, lanes] = low

    for row in range(0, core, 16):
        contract(
            lambda h, e, row=row: planes[ey + h, base + offsets[e], row : row + 16],
            list(range(wide)),
            row,
        )
    for row in range(0, level.rim, 16):
        contract(
            lambda h, e, row=row: rims[ey + h, base + e - 1, row : row + 16],
            list(range(1, n + 1)),
            core + row,
        )
    for i in range(wide):
        both = dot(forward[...], spectrum[i])
        damp = inverse[i]
        hat = (both[0:modes] + both[modes : 2 * modes]) * jnp.concatenate([damp, damp], axis=1)
        high, low = split(hat)
        both = dot(backward[...], jnp.concatenate([high, low], axis=0))
        hats[i] = both[0:core] + both[core : 2 * core]
    for h in (0, 1):
        inv = 1.0 / scale[ex, pl.ds(ey + h, 1), :]
        lanes = slice(h * LANES, (h + 1) * LANES)
        for row in range(0, core, 16):
            held = [hats[i, row : row + 16, lanes] for i in range(wide)]
            for a in range(n):
                total = coeff[a + 1, 0] * held[0]
                for i in range(1, wide):
                    total += coeff[a + 1, i] * held[i]
                out[q, h, a, row : row + 16] = total * inv


def schwarz_kernel(
    residual,
    middle,
    scale,
    fine_basis,
    fine_coeff,
    fine_eigen,
    middle_basis,
    middle_coeff,
    middle_eigen,
    *refs,
):
    halos, refs = refs[:8], refs[8:]
    fine_tables, refs = refs[:6], refs[6:]
    middle_tables, refs = refs[:6], refs[6:]
    fine_out, middle_out, refs = refs[0], refs[1], refs[2:]
    sends, refs = refs[:8], refs[8:]
    (
        planes,
        rims,
        sides,
        forward,
        backward,
        inverse,
        spectrum,
        hats,
        planes_m,
        rims_m,
        sides_m,
        forward_m,
        backward_m,
        inverse_m,
        spectrum_m,
        hats_m,
        solved,
        in_sems,
        out_sems,
    ) = refs
    x_low, x_high, y_low, y_high, d_ll, d_lh, d_hl, d_hh = halos
    diags = ((d_ll, d_lh), (d_hl, d_hh))
    copies = []
    for ex in range(EX):
        for ey in range(EY):
            copy = pltpu.make_async_copy(
                residual.at[ex, ey], planes.at[ey, pl.ds(2 + 8 * ex, 8)], in_sems.at[ex * EY + ey]
            )
            copy.start()
            copies.append(copy)
    for ex in range(EX):
        for ey in range(EY):
            planes_m[ey, 2 + 4 * ex : 6 + 4 * ex] = middle[ex, ey]
    build_tables(FINE, fine_tables, fine_basis, fine_eigen, forward, backward, inverse)
    build_tables(MID, middle_tables, middle_basis, middle_eigen, forward_m, backward_m, inverse_m)
    assemble(MID, planes_m, rims_m, sides_m, x_low, x_high, y_low, y_high, diags)

    def middle_step(q, carry):
        solve_pair(
            MID, q, planes_m, rims_m, middle_coeff, forward_m, backward_m, inverse_m, scale,
            spectrum_m, hats_m, middle_out,
        )
        return carry

    lax.fori_loop(0, 8, middle_step, 0)
    for copy in copies:
        copy.wait()
    assemble(FINE, planes, rims, sides, x_low, x_high, y_low, y_high, diags)

    def fine_step(q, carry):
        solve_pair(
            FINE, q, planes, rims, fine_coeff, forward, backward, inverse, scale,
            spectrum, hats, solved,
        )
        pltpu.make_async_copy(solved.at[q], fine_out.at[q], out_sems.at[q]).start()
        return carry

    lax.fori_loop(0, 8, fine_step, 0)

    x_up, x_down, y_up, y_down, d_uu, d_ud, d_du, d_dd = sends
    for n, source, base in ((8, solved, 0), (4, middle_out, 256)):
        core = n * n
        for out, ex, node in ((x_up, EX - 1, n - 1), (x_down, 0, 0)):
            for ey in range(EY):
                row = base + ey * core
                out[row : row + core] = source[2 * ex + ey // 2, ey % 2, node]
        for out, ey, node in ((y_up, EY - 1, n - 1), (y_down, 0, 0)):
            for ex in range(EX):
                for a in range(n):
                    row = base + (ex * n + a) * n
                    out[row : row + n] = source[
                        2 * ex + ey // 2, ey % 2, a, node * n : node * n + n
                    ]
    for out, up_x, up_y in ((d_uu, 1, 1), (d_ud, 1, 0), (d_du, 0, 1), (d_dd, 0, 0)):
        out[8:16] = jnp.zeros((8, LANES), F32)
        for n, source, base in ((8, solved, 0), (4, middle_out, 8)):
            a, b = (n - 1) * up_x, (n - 1) * up_y
            q, h = 2 * (EX - 1) * up_x + up_y, up_y
            out[base : base + n] = source[q, h, a, b * n : b * n + n]
    for q in range(8):
        pltpu.make_async_copy(solved.at[q], fine_out.at[q], out_sems.at[q]).wait()


def schwarz(residual, middle, scale, fine_basis, fine_eigen, middle_basis, middle_eigen, halos):
    vmem = pl.BlockSpec(memory_space=pltpu.VMEM)
    smem = pl.BlockSpec(memory_space=pltpu.SMEM)
    hbm = pl.BlockSpec(memory_space=pl.ANY)
    tables = [jnp.asarray(t) for level in (FINE, MID) for t in level.tables()]
    face = jax.ShapeDtypeStruct((FACE_ROWS, LANES), F32)
    edge = jax.ShapeDtypeStruct((EDGE_ROWS, LANES), F32)

    def scratch(level):
        return [
            pltpu.VMEM((EY, level.planes, level.core, LANES), F32),
            pltpu.VMEM((EY, EX * level.n, level.rim, LANES), F32),
            pltpu.VMEM((4, EX * level.core, LANES), F32),
            pltpu.VMEM((2 * level.modes, 2 * level.depth), BF16),
            pltpu.VMEM((2 * level.core, 2 * level.modes), BF16),
            pltpu.VMEM((level.wide, level.modes, LANES), F32),
            pltpu.VMEM((level.wide, 2 * level.depth, 2 * LANES), BF16),
            pltpu.VMEM((level.wide, level.core, 2 * LANES), F32),
        ]

    return pl.pallas_call(
        schwarz_kernel,
        out_shape=[
            jax.ShapeDtypeStruct((8, 2, 8, 64, LANES), F32),
            jax.ShapeDtypeStruct((8, 2, 4, 16, LANES), F32),
        ]
        + [face] * 4
        + [edge] * 4,
        in_specs=[hbm, vmem, vmem, vmem, smem, vmem, vmem, smem, vmem] + [vmem] * 20,
        out_specs=[hbm] + [vmem] * 9,
        scratch_shapes=scratch(FINE)
        + scratch(MID)
        + [
            pltpu.VMEM((8, 2, 8, 64, LANES), F32),
            pltpu.SemaphoreType.DMA((16,)),
            pltpu.SemaphoreType.DMA((8,)),
        ],
        compiler_params=pltpu.CompilerParams(vmem_limit_bytes=VMEM_LIMIT),
        cost_estimate=pl.CostEstimate(
            flops=8 * 10**9, bytes_accessed=12 * 10**6, transcendentals=0
        ),
        name="schwarz",
    )(
        residual, middle, scale, fine_basis, fine_basis[0], fine_eigen,
        middle_basis, middle_basis[0], middle_eigen, *halos, *tables,
    )


def coarse_kernel(place, rows_x, gathered, forward_y, back_y, hartley_z, lines, out, held, part):
    own_x, own_y = place[0], place[1]

    def y_step(p, carry):
        before = lax.rem(p + 7, 8)
        slabs = []
        for lx in range(4):
            pieces = []
            for ly in range(5):
                piece = gathered[pl.ds(p * 512 + lx * 5 + ly, 16, stride=32), :]
                if lx == 0:
                    piece += gathered[pl.ds(before * 512 + 20 + ly, 16, stride=32), :]
                pieces.append(piece)
            slabs.append(jnp.concatenate(pieces, axis=0))
        for half in (0, 2):
            high, low = split(jnp.concatenate([slabs[half], slabs[half + 1]], axis=1))
            both = dot(forward_y[...], jnp.concatenate([high, low], axis=0))
            total = both[0:64] + both[64:128]
            held[4 * p + half] = total[:, 0:LANES]
            held[4 * p + half + 1] = total[:, LANES : 2 * LANES]
        return carry

    lax.fori_loop(0, 8, y_step, 0)
    angle = 2.0 * np.pi / 32
    eigen_x = line_eigen(32)

    def x_step(chunk, carry):
        rows = pl.ds(pl.multiple_of(chunk * 8, 8), 8)
        values = [held[x, rows, :] for x in range(32)]
        even = [values[0]] + [values[x] + values[32 - x] for x in range(1, 16)] + [values[16]]
        odd = [None] + [values[x] - values[32 - x] for x in range(1, 16)]
        base = lines[rows, :]
        totals = [None] * 5
        for k in range(17):
            cosine = even[0]
            for x in range(1, 17):
                cosine = cosine + float(np.cos(angle * (k * x % 32))) * even[x]
            modes = [(k, cosine)]
            if 0 < k < 16:
                sine = float(np.sin(angle * k)) * odd[1]
                for x in range(2, 16):
                    sine = sine + float(np.sin(angle * (k * x % 32))) * odd[x]
                modes = [(k, cosine + sine), (32 - k, cosine - sine)]
            damp = 1.0 / (base + float(24.0 * eigen_x[k]))
            for kx, value in modes:
                value = value * damp
                for lx in range(5):
                    term = rows_x[lax.rem(own_x * 4 + lx, 32), kx] * value
                    totals[lx] = term if totals[lx] is None else totals[lx] + term
        for lx in range(5):
            part[lx, rows, :] = totals[lx]
        return carry

    lax.fori_loop(0, 8, x_step, 0)
    own_rows = back_y[own_y]
    solved = jnp.concatenate([exact_dot(own_rows, part[lx]) for lx in range(5)], axis=0)
    out[...] = exact_dot(solved, hartley_z[...]) * (1.0 / (32 * 64 * 128))


def coarse(gathered):
    vmem = pl.BlockSpec(memory_space=pltpu.VMEM)
    smem = pl.BlockSpec(memory_space=pltpu.SMEM)
    place = jnp.stack([lax.axis_index("px"), lax.axis_index("py")]).astype(jnp.int32)
    table_y = hartley(64)
    forward = np.zeros((64, 160), np.float32)
    back = np.zeros((16, 8, 64), np.float32)
    for q in range(16):
        for ly in range(5):
            forward[:, ly * 16 + q] = table_y[:, (4 * q + ly) % 64]
            back[q, ly] = table_y[(4 * q + ly) % 64]
    forward[:, 80:] = forward[:, :80]
    high, low = split_np(forward)
    low[:, 80:] = 0
    lines = 24.0 * (line_eigen(64)[:, None] + line_eigen(128)[None, :]) + 0.5
    return pl.pallas_call(
        coarse_kernel,
        out_shape=jax.ShapeDtypeStruct((40, LANES), F32),
        in_specs=[smem, smem] + [vmem] * 5,
        out_specs=vmem,
        scratch_shapes=[
            pltpu.VMEM((32, 64, LANES), F32),
            pltpu.VMEM((5, 64, LANES), F32),
        ],
        compiler_params=pltpu.CompilerParams(vmem_limit_bytes=VMEM_LIMIT),
        cost_estimate=pl.CostEstimate(
            flops=2 * 10**9, bytes_accessed=4 * 10**6, transcendentals=0
        ),
        name="coarse",
    )(
        place,
        jnp.asarray(hartley(32), F32),
        gathered,
        jnp.asarray(np.concatenate([high, low], axis=0)),
        jnp.asarray(back),
        jnp.asarray(hartley(128), F32),
        jnp.asarray(lines, F32),
    )


def average_faces(level, field, sides, x_low, x_high, y_low, y_high, diags):
    n, core = level.n, level.core
    base = 0 if n == 8 else 256
    edge = 0 if n == 8 else 8

    def at(ex, ey):
        return 2 * ex + ey // 2, ey % 2

    for ey in range(EY):
        row = base + ey * core
        q, h = at(0, ey)
        field[q, h, 0] = 0.5 * (field[q, h, 0] + x_low[row : row + core])
        q, h = at(EX - 1, ey)
        field[q, h, n - 1] = 0.5 * (field[q, h, n - 1] + x_high[row : row + core])
        for ex in range(EX - 1):
            q, h = at(ex, ey)
            total = 0.5 * (field[q, h, n - 1] + field[q + 2, h, 0])
            field[q, h, n - 1] = total
            field[q + 2, h, 0] = total
    for side, halo in ((0, y_low), (1, y_high)):
        sides[side] = halo[base : base + EX * core]
        low = diags[0][side][edge : edge + n]
        high = diags[1][side][edge : edge + n]
        end = EX * core
        sides[side, 0:n] = 0.5 * (sides[side, 0:n] + low)
        sides[side, end - n : end] = 0.5 * (sides[side, end - n : end] + high)
        for ex in range(EX - 1):
            row = ex * core + core
            total = 0.5 * (sides[side, row - n : row] + sides[side, row : row + n])
            sides[side, row - n : row] = total
            sides[side, row : row + n] = total
    for ex in range(EX):
        for a in range(n):
            row = (ex * n + a) * n
            q, h = at(ex, 0)
            field[q, h, a, 0:n] = 0.5 * (field[q, h, a, 0:n] + sides[0, row : row + n])
            q, h = at(ex, EY - 1)
            field[q, h, a, core - n : core] = 0.5 * (
                field[q, h, a, core - n : core] + sides[1, row : row + n]
            )
            for ey in range(EY - 1):
                q, h = at(ex, ey)
                p, g = at(ex, ey + 1)
                total = 0.5 * (field[q, h, a, core - n : core] + field[p, g, a, 0:n])
                field[q, h, a, core - n : core] = total
                field[p, g, a, 0:n] = total


def finish_kernel(
    fine, middle, coarse_part, prolong, x_low, x_high, y_low, y_high, d_ll, d_lh, d_hl, d_hh,
    out, field, sides, field_m, sides_m, corner, result, in_sems, out_sems,
):
    copies = []
    for q in range(8):
        copy = pltpu.make_async_copy(fine.at[q], field.at[q], in_sems.at[q])
        copy.start()
        copies.append(copy)
    diags = ((d_ll, d_lh), (d_hl, d_hh))
    field_m[...] = middle[...]
    average_faces(MID, field_m, sides_m, x_low, x_high, y_low, y_high, diags)
    near = coarse_part[...]
    far = pltpu.roll(near, LANES - 1, 1)
    for q in range(8):
        for h in (0, 1):
            ex, ey = q // 2, (q % 2) * 2 + h
            corner[q, h, 8:16] = jnp.zeros((8, LANES), F32)
            for i in (0, 1):
                for j in (0, 1):
                    row = (ex + i) * 8 + ey + j
                    place = i * 4 + j * 2
                    corner[q, h, place : place + 1] = near[row : row + 1]
                    corner[q, h, place + 1 : place + 2] = far[row : row + 1]
    for copy in copies:
        copy.wait()
    average_faces(FINE, field, sides, x_low, x_high, y_low, y_high, diags)

    def step(q, carry):
        for h in (0, 1):
            for a in range(4):
                sum_lines(field_m, (q, h, a), 4, 0.5)
            for a in range(8):
                sum_lines(field, (q, h, a), 8, 0.5)
        level = jnp.concatenate(
            [field_m[q, 0].reshape(64, LANES), field_m[q, 1].reshape(64, LANES)], axis=1
        )
        high, low = split(level)
        ends = jnp.concatenate([corner[q, 0], corner[q, 1]], axis=1)
        ends_high, ends_low = split(ends)
        stacked = jnp.concatenate([high, low, high, ends_high, ends_low, ends_high], axis=0)
        total = dot(prolong[...], stacked)
        for h in (0, 1):
            part = total[:, h * LANES : (h + 1) * LANES]
            result[q, h] = field[q, h] + part.reshape(8, 64, LANES)
        pltpu.make_async_copy(result.at[q], out.at[q], out_sems.at[q]).start()
        return carry

    lax.fori_loop(0, 8, step, 0)
    for q in range(8):
        pltpu.make_async_copy(result.at[q], out.at[q], out_sems.at[q]).wait()


def finish(fine, middle, coarse_part, halos):
    vmem = pl.BlockSpec(memory_space=pltpu.VMEM)
    hbm = pl.BlockSpec(memory_space=pl.ANY)
    return pl.pallas_call(
        finish_kernel,
        out_shape=jax.ShapeDtypeStruct((8, 2, 8, 64, LANES), F32),
        in_specs=[hbm] + [vmem] * 11,
        out_specs=hbm,
        scratch_shapes=[
            pltpu.VMEM((8, 2, 8, 64, LANES), F32),
            pltpu.VMEM((2, EX * 64, LANES), F32),
            pltpu.VMEM((8, 2, 4, 16, LANES), F32),
            pltpu.VMEM((2, EX * 16, LANES), F32),
            pltpu.VMEM((8, 2, 16, LANES), F32),
            pltpu.VMEM((8, 2, 8, 64, LANES), F32),
            pltpu.SemaphoreType.DMA((8,)),
            pltpu.SemaphoreType.DMA((8,)),
        ],
        compiler_params=pltpu.CompilerParams(vmem_limit_bytes=VMEM_LIMIT),
        cost_estimate=pl.CostEstimate(
            flops=2 * 10**9, bytes_accessed=8 * 10**6, transcendentals=0
        ),
        name="finish",
    )(fine, middle, coarse_part, jnp.asarray(prolong_matrix()), *halos)


def shift(values, axis, step):
    count = lax.axis_size(axis)
    return lax.ppermute(values, axis, [(i, (i + step) % count) for i in range(count)])


def shift_both(values, step_x, step_y):
    count_x, count_y = lax.axis_size("px"), lax.axis_size("py")
    pairs = [
        (i * count_y + j, (i + step_x) % count_x * count_y + (j + step_y) % count_y)
        for i in range(count_x)
        for j in range(count_y)
    ]
    return lax.ppermute(values, ("px", "py"), pairs)


def exchange(sends):
    x_up, x_down, y_up, y_down, d_uu, d_ud, d_du, d_dd = sends
    return (
        shift(x_up, "px", 1),
        shift(x_down, "px", -1),
        shift(y_up, "py", 1),
        shift(y_down, "py", -1),
        shift_both(d_uu, 1, 1),
        shift_both(d_ud, 1, -1),
        shift_both(d_du, -1, 1),
        shift_both(d_dd, -1, -1),
    )


def on_device(residual, scale, fine_basis, fine_eigen, middle_basis, middle_eigen):
    shape = residual.shape
    residual = residual.reshape(EX, EY, 8, 64, LANES)
    packed = pack(residual)
    sends, middle, vertex = packed[:8], packed[8], packed[9]
    halos = exchange(sends)
    devices = lax.axis_size("px") * lax.axis_size("py")
    copies = jnp.broadcast_to(vertex[None], (devices, 32, LANES))
    gathered = lax.all_to_all(copies, ("px", "py"), 0, 0).reshape(devices * 32, LANES)
    solved = schwarz(
        residual, middle, scale, fine_basis, fine_eigen, middle_basis, middle_eigen, halos
    )
    fine_solved, middle_solved, faces = solved[0], solved[1], solved[2:]
    faces = exchange(faces)
    coarse_part = coarse(gathered)
    return finish(fine_solved, middle_solved, coarse_part, faces).reshape(shape)


def solution(mesh):
    placed = (P("px", "py", None, None, None, None), P("px", "py", None), P(), P(), P(), P())
    return jax.shard_map(
        on_device,
        mesh=mesh,
        in_specs=placed,
        out_specs=P("px", "py", None, None, None, None),
        check_vma=False,
    )
```

```python
import functools
import math

import jax
import jax.numpy as jnp
import ml_dtypes
import numpy as np
from jax import lax
from jax.experimental import pallas as pl
from jax.experimental.pallas import tpu as pltpu
from jax.sharding import PartitionSpec as P

F32, BF16 = jnp.float32, jnp.bfloat16
HIGHEST = lax.Precision.HIGHEST
LANES = 128
EX = EY = 4
MID_GROUP = 4
LAG = 5
MIB = 1024 * 1024
VMEM_LIMIT = 60 * MIB


def lobatto(count):
    return -np.cos(np.arange(count) * (np.pi / (count - 1)))


def interpolation(fine_count, coarse_count):
    fine, coarse = lobatto(fine_count), lobatto(coarse_count)
    out = np.ones((fine_count, coarse_count))
    for j in range(coarse_count):
        for m in range(coarse_count):
            if m != j:
                out[:, j] *= (fine - coarse[m]) / (coarse[j] - coarse[m])
    return out


def hartley(count):
    phase = np.outer(np.arange(count), np.arange(count)) % count
    angle = phase * (2.0 * np.pi / count)
    return np.cos(angle) + np.sin(angle)


def line_eigen(count):
    return 2.0 - 2.0 * np.cos(np.arange(count) * (2.0 * np.pi / count))


def split_np(values):
    values = np.asarray(values, np.float32)
    high = values.astype(ml_dtypes.bfloat16)
    low = (values - high.astype(np.float32)).astype(ml_dtypes.bfloat16)
    return high, low


def split(values):
    high = values.astype(BF16)
    return high, (values - high.astype(F32)).astype(BF16)


def dot(left, right):
    return jnp.dot(left, right, preferred_element_type=F32)


def exact_dot(left, right, contract=((1,), (0,))):
    return lax.dot_general(
        left, right, (contract, ((), ())), precision=HIGHEST, preferred_element_type=F32
    )


INTERP_FINE = interpolation(8, 4)
INTERP_MID = interpolation(4, 2)
INTERP_ALL = INTERP_FINE @ INTERP_MID


def kron3(m):
    return np.kron(np.kron(m, m), m)


def restrict_matrix():
    rows = np.zeros((80, 512))
    rows[:64] = kron3(INTERP_FINE).T
    rows[64:72] = kron3(INTERP_ALL).T
    high, low = split_np(rows)
    return np.concatenate([high, low], axis=0)


def prolong_matrix():
    fine = kron3(INTERP_FINE)
    coarse = np.zeros((512, 16))
    coarse[:, :8] = kron3(INTERP_ALL)
    fine_high, fine_low = split_np(fine)
    coarse_high, coarse_low = split_np(coarse)
    return np.concatenate(
        [fine_high, fine_high, fine_low, coarse_high, coarse_high, coarse_low], axis=1
    )


def vertex_matrices():
    out = np.zeros((2, 32, 128), np.float32)
    for ex in range(EX):
        for ey in range(EY):
            for i in (0, 1):
                for j in (0, 1):
                    for k in (0, 1):
                        column = (ex * EY + ey) * 8 + i * 4 + j * 2 + k
                        out[k, (ex + i) * 5 + ey + j, column] = 1.0
    return out


class Level:
    def __init__(self, n):
        self.n = n
        self.wide = n + 2
        self.core = n * n
        self.rim = 4 * n
        self.depth = self.core + self.rim
        self.modes = -(-(self.wide * self.wide) // 16) * 16
        self.planes = EX * n + 4

    def tables(self):
        n, wide = self.n, self.wide
        first = np.zeros((2 * self.modes, wide), np.float32)
        second = np.zeros((2 * self.modes, wide), np.float32)
        for half in (0, 1):
            for j in range(wide):
                for k in range(wide):
                    first[half * self.modes + j * wide + k, j] = 1.0
                    second[half * self.modes + j * wide + k, k] = 1.0
        inner = list(range(1, n + 1))
        points = [(b, c) for b in inner for c in inner]
        points += [(0, c) for c in inner] + [(n + 1, c) for c in inner]
        points += [(b, 0) for b in inner] + [(b, n + 1) for b in inner]
        pick_b = np.zeros((wide, 2 * self.depth), np.float32)
        pick_c = np.zeros((wide, 2 * self.depth), np.float32)
        for half in (0, 1):
            for column, (b, c) in enumerate(points):
                pick_b[b, half * self.depth + column] = 1.0
                pick_c[c, half * self.depth + column] = 1.0
        return (
            first,
            second,
            pick_b,
            pick_c,
            np.ascontiguousarray(pick_b[:, : self.core].T),
            np.ascontiguousarray(pick_c[:, : self.core].T),
        )


FINE, MID = Level(8), Level(4)

LAYER_ROWS = 640
X_ROWS = 648
Y_ROWS = 664
FACE_ROWS = 320
VERTEX_ROWS = 24


def plane_line(n, side):
    return (640 if n == 8 else 656) + side * n


def pack_kernel(
    residual,
    restrict_in,
    vertex_pick_in,
    hartley_in,
    x_up,
    x_down,
    y_up,
    y_down,
    middle,
    vertex,
    field,
    corners,
    restrict,
    vertex_pick,
    hartley_z,
    sems,
):
    moves = [(restrict_in, restrict)]
    moves += [(residual.at[ex], field.at[ex]) for ex in range(EX)]
    moves += [(vertex_pick_in, vertex_pick), (hartley_in, hartley_z)]
    copies = []
    for place, (source, target) in enumerate(moves):
        copies.append(pltpu.make_async_copy(source, target, sems.at[place]))
        copies[-1].start()
    copies[0].wait()
    for ex in range(EX):
        copies[1 + ex].wait()
        for pair in range(EY // 2):
            ey = 2 * pair
            values = jnp.concatenate(
                [field[ex, ey].reshape(512, LANES), field[ex, ey + 1].reshape(512, LANES)], axis=1
            )
            high, low = split(values)
            upper = dot(restrict[...], high)
            lower = dot(restrict[0:80, :], low)
            total = upper[0:80] + upper[80:160] + lower
            for h in (0, 1):
                part = total[:, h * LANES : (h + 1) * LANES]
                for i in range(4):
                    middle[ex, ey + h, i] = part[16 * i : 16 * i + 16]
                column = ex * EY + ey + h
                corners[8 * column : 8 * column + 8] = part[64:72]
    for out, ex, nodes, mids in ((x_up, EX - 1, (7, 6), (3, 2)), (x_down, 0, (0, 1), (0, 1))):
        for layer in (0, 1):
            for ey in range(EY):
                row = (layer * EY + ey) * 64
                out[row : row + 64] = field[ex, ey, nodes[layer]]
                row = 512 + (layer * EY + ey) * 16
                out[row : row + 16] = middle[ex, ey, mids[layer]]
    for out, ey, nodes, mids in ((y_up, EY - 1, (7, 6), (3, 2)), (y_down, 0, (0, 1), (0, 1))):
        for layer in (0, 1):
            for ex in range(EX):
                for a in range(8):
                    row = (layer * EX + ex) * 64 + a * 8
                    line = nodes[layer] * 8
                    out[row : row + 8] = field[ex, ey, a, line : line + 8]
                for a in range(4):
                    row = 512 + (layer * EX + ex) * 16 + a * 4
                    line = mids[layer] * 4
                    out[row : row + 4] = middle[ex, ey, a, line : line + 4]
    for out in (y_up, y_down):
        for n, base in ((8, 0), (4, 512)):
            core = n * n
            for row in [base + k * core for k in (1, 2, 3, 5, 6, 7)]:
                total = out[row - n : row] + out[row : row + n]
                out[row - n : row] = total
                out[row : row + n] = total
    copies[EX + 1].wait()
    copies[EX + 2].wait()
    values = corners[...]
    low = exact_dot(vertex_pick[0], values)
    high = exact_dot(vertex_pick[1], values)
    total = low + pltpu.roll(high, 1, 1)
    total = exact_dot(total, hartley_z[...])
    vertex[...] = total
    x_up[LAYER_ROWS:X_ROWS] = total[20:28]
    x_down[LAYER_ROWS:X_ROWS] = jnp.zeros((8, LANES), F32)


def pack(residual):
    x_halo = jax.ShapeDtypeStruct((X_ROWS, LANES), F32)
    y_halo = jax.ShapeDtypeStruct((LAYER_ROWS, LANES), F32)
    vmem = pl.BlockSpec(memory_space=pltpu.VMEM)
    return pl.pallas_call(
        pack_kernel,
        out_shape=[x_halo] * 2
        + [y_halo] * 2
        + [
            jax.ShapeDtypeStruct((EX, EY, 4, 16, LANES), F32),
            jax.ShapeDtypeStruct((32, LANES), F32),
        ],
        in_specs=[pl.BlockSpec(memory_space=pltpu.HBM)] * 4,
        out_specs=[vmem] * 6,
        scratch_shapes=[
            pltpu.VMEM((EX, EY, 8, 64, LANES), F32),
            pltpu.VMEM((128, LANES), F32),
            pltpu.VMEM((160, 512), BF16),
            pltpu.VMEM((2, 32, 128), F32),
            pltpu.VMEM((128, 128), F32),
            pltpu.SemaphoreType.DMA((EX + 3,)),
        ],
        compiler_params=pltpu.CompilerParams(vmem_limit_bytes=VMEM_LIMIT),
        cost_estimate=pl.CostEstimate(flops=10**9, bytes_accessed=8 * 10**6, transcendentals=0),
        name="pack",
    )(
        residual,
        jnp.asarray(restrict_matrix()),
        jnp.asarray(vertex_matrices()),
        jnp.asarray(hartley(128), F32),
    )


def join_kernel(x_low, x_high, y_up, y_down, vertex, after, up, down, summed):
    del after
    for out, source, ey, ends in ((up, y_up, EY - 1, True), (down, y_down, 0, False)):
        out[0:LAYER_ROWS] = source[...]
        for n, base in ((8, 0), (4, 512)):
            core = n * n
            nodes = (n - 1, n - 2) if ends else (0, 1)
            for layer in (0, 1):
                line = base + ey * core + nodes[layer] * n
                row = base + layer * EX * core
                out[row : row + n] += x_low[line : line + n]
                row += EX * core - n
                out[row : row + n] += x_high[line : line + n]
            line = base + (EY + ey) * core + nodes[0] * n
            for side, halo in ((0, x_low), (1, x_high)):
                row = plane_line(n, side)
                out[row : row + n] = halo[line : line + n]
    summed[...] = vertex[0:VERTEX_ROWS]
    summed[0:5] += x_low[LAYER_ROWS : LAYER_ROWS + 5]
    summed[20:24] = jnp.zeros((4, LANES), F32)


def join(x_low, x_high, y_up, y_down, vertex, after):
    vmem = pl.BlockSpec(memory_space=pltpu.VMEM)
    halo = jax.ShapeDtypeStruct((Y_ROWS, LANES), F32)
    return pl.pallas_call(
        join_kernel,
        out_shape=[halo, halo, jax.ShapeDtypeStruct((VERTEX_ROWS, LANES), F32)],
        in_specs=[vmem] * 5 + [pl.BlockSpec(memory_space=pl.ANY)],
        out_specs=[vmem] * 3,
        compiler_params=pltpu.CompilerParams(vmem_limit_bytes=VMEM_LIMIT),
        cost_estimate=pl.CostEstimate(flops=10**6, bytes_accessed=3 * 10**6, transcendentals=0),
        name="join",
    )(x_low, x_high, y_up, y_down, vertex, after)


def join_faces_kernel(x_low, x_high, y_up, y_down, up, down):
    for out, source, ey, ends in ((up, y_up, EY - 1, True), (down, y_down, 0, False)):
        out[...] = source[...]
        for n, base in ((8, 0), (4, 256)):
            core = n * n
            line = base + ey * core + (core - n if ends else 0)
            out[base : base + n] = 0.5 * (source[base : base + n] + x_low[line : line + n])
            row = base + EX * core - n
            out[row : row + n] = 0.5 * (source[row : row + n] + x_high[line : line + n])
            for ex in range(EX - 1):
                row = base + ex * core + core
                total = 0.5 * (source[row - n : row] + source[row : row + n])
                out[row - n : row] = total
                out[row : row + n] = total


def join_faces(x_low, x_high, y_up, y_down):
    vmem = pl.BlockSpec(memory_space=pltpu.VMEM)
    face = jax.ShapeDtypeStruct((FACE_ROWS, LANES), F32)
    return pl.pallas_call(
        join_faces_kernel,
        out_shape=[face, face],
        in_specs=[vmem] * 4,
        out_specs=[vmem] * 2,
        compiler_params=pltpu.CompilerParams(vmem_limit_bytes=VMEM_LIMIT),
        cost_estimate=pl.CostEstimate(flops=10**6, bytes_accessed=10**6, transcendentals=0),
        name="join_faces",
    )(x_low, x_high, y_up, y_down)


def spread_kernel(source, out):
    out[...] = jnp.broadcast_to(source[...][None], out.shape)


def spread(values, count):
    vmem = pl.BlockSpec(memory_space=pltpu.VMEM)
    return pl.pallas_call(
        spread_kernel,
        out_shape=jax.ShapeDtypeStruct((count,) + values.shape, F32),
        in_specs=[vmem],
        out_specs=vmem,
        compiler_params=pltpu.CompilerParams(vmem_limit_bytes=VMEM_LIMIT),
        cost_estimate=pl.CostEstimate(flops=10**6, bytes_accessed=2 * 10**6, transcendentals=0),
        name="spread",
    )(values)


def sum_lines(ref, lead, n, scale=None):
    count = ref.shape[-2] // n
    low_rows = lead + (pl.ds(0, count, stride=n), slice(None))
    high_rows = lead + (pl.ds(n - 1, count, stride=n), slice(None))
    low, high = ref[low_rows], ref[high_rows]
    new_low = low + pltpu.roll(high, 1, 1)
    new_high = high + pltpu.roll(low, LANES - 1, 1)
    if scale is not None:
        new_low, new_high = new_low * scale, new_high * scale
    ref[low_rows] = new_low
    ref[high_rows] = new_high


def assemble(level, planes, rims, sides, x_low, x_high, y_low, y_high):
    n, core = level.n, level.core
    last = EX * n + 3
    base = 0 if n == 8 else 512
    for ey in range(EY):
        row = base + ey * core
        planes[ey, 2] += x_low[row : row + core]
        planes[ey, last - 2] += x_high[row : row + core]
        for ex in range(EX - 1):
            left = 2 + ex * n + n - 1
            total = planes[ey, left] + planes[ey, left + 1]
            planes[ey, left] = total
            planes[ey, left + 1] = total
        row = base + (EY + ey) * core
        planes[ey, 0] = x_low[row : row + core]
        planes[ey, last] = x_high[row : row + core]
    for side, halo in ((0, y_low), (1, y_high)):
        for layer in (0, 1):
            kind = 2 * side + layer
            start = base + layer * EX * core
            sides[kind] = halo[start : start + EX * core]
    for plane in range(EX * n):
        row = plane * n
        planes[0, 2 + plane, 0:n] += sides[0, row : row + n]
        planes[EY - 1, 2 + plane, core - n : core] += sides[2, row : row + n]
    for side, plane in ((0, 0), (1, last)):
        row = plane_line(n, side)
        planes[0, plane, 0:n] += y_low[row : row + n]
        planes[EY - 1, plane, core - n : core] += y_high[row : row + n]
    for ey in range(EY - 1):
        for plane in [0, last] + list(range(2, 2 + EX * n)):
            total = planes[ey, plane, core - n : core] + planes[ey + 1, plane, 0:n]
            planes[ey, plane, core - n : core] = total
            planes[ey + 1, plane, 0:n] = total
    for ey in range(EY):
        for plane in [0, last] + list(range(2, 2 + EX * n)):
            sum_lines(planes, (ey, plane), n)
    for kind in (1, 3):
        sum_lines(sides, (kind,), n)
    for ey in range(EY):
        for plane in range(EX * n):
            at = 2 + plane
            row = plane * n
            low = planes[ey - 1, at, core - 2 * n : core - n] if ey else sides[1, row : row + n]
            high = planes[ey + 1, at, n : 2 * n] if ey < EY - 1 else sides[3, row : row + n]
            rims[ey, plane, 0:n] = low
            rims[ey, plane, n : 2 * n] = high
            rims[ey, plane, 2 * n : 3 * n] = pltpu.roll(
                planes[ey, at, pl.ds(n - 2, n, stride=n), :], 1, 1
            )
            rims[ey, plane, 3 * n : 4 * n] = pltpu.roll(
                planes[ey, at, pl.ds(1, n, stride=n), :], LANES - 1, 1
            )


def build_tables(level, tables, basis, eigen, forward, backward, inverse):
    first, second, pick_b, pick_c, core_b, core_c = tables
    modes, depth = level.modes, level.depth
    rows_b = exact_dot(first[0:modes], basis[1], ((1,), (1,)))
    rows_c = exact_dot(second[0:modes], basis[2], ((1,), (1,)))
    matrix = exact_dot(rows_b, pick_b[...]) * exact_dot(rows_c, pick_c[...])
    high, low = split(matrix)
    keep = lax.broadcasted_iota(jnp.int32, matrix.shape, 1) < depth
    forward[0:modes] = high
    forward[modes : 2 * modes] = jnp.where(keep, low.astype(F32), 0.0).astype(BF16)
    out_b = exact_dot(exact_dot(core_b[...], basis[1]), first[...], ((1,), (1,)))
    out_c = exact_dot(exact_dot(core_c[...], basis[2]), second[...], ((1,), (1,)))
    matrix = out_b * out_c
    high, low = split(matrix)
    keep = lax.broadcasted_iota(jnp.int32, matrix.shape, 1) < modes
    backward[0 : level.core] = high
    backward[level.core : 2 * level.core] = jnp.where(keep, low.astype(F32), 0.0).astype(BF16)
    wide = level.wide
    spread_b = jnp.broadcast_to(eigen[1:2, :], (LANES, wide))
    spread_c = jnp.broadcast_to(eigen[2:3, :], (LANES, wide))
    lines = exact_dot(first[0:modes], spread_b, ((1,), (1,)))
    lines += exact_dot(second[0:modes], spread_c, ((1,), (1,)))
    for i in range(wide):
        inverse[i] = 1.0 / (lines + eigen[0:1, i : i + 1])


def solve_pairs(
    level, start, group, planes, rims, coeff, forward, backward, inverse, scale, spectrum, hats, out
):
    n, wide, core, modes, depth = level.n, level.wide, level.core, level.modes, level.depth
    offsets = [0] + [2 + a for a in range(n)] + [n + 3]

    def contract(slot, load, nodes, row):
        held = [[load(h, e) for h in (0, 1)] for e in nodes]
        for i in range(wide):
            for h in (0, 1):
                total = coeff[nodes[0], i] * held[0][h]
                for position in range(1, len(nodes)):
                    total += coeff[nodes[position], i] * held[position][h]
                high, low = split(total)
                lanes = slice(h * LANES, (h + 1) * LANES)
                spectrum[slot, i, row : row + 16, lanes] = high
                spectrum[slot, i, depth + row : depth + row + 16, lanes] = low

    for slot in range(group):
        q = start + slot
        base, ey = q // 2 * n, q % 2 * 2
        for row in range(0, core, 16):
            contract(
                slot,
                lambda h, e, row=row: planes[ey + h, base + offsets[e], row : row + 16],
                list(range(wide)),
                row,
            )
        for row in range(0, level.rim, 16):
            contract(
                slot,
                lambda h, e, row=row: rims[ey + h, base + e - 1, row : row + 16],
                list(range(1, n + 1)),
                core + row,
            )
    waiting = []
    steps = [(slot, i) for slot in range(group) for i in range(wide)]
    for step in range(len(steps) + LAG):
        if step < len(steps):
            slot, i = steps[step]
            both = dot(forward[...], spectrum[slot, i])
            damp = inverse[i]
            hat = (both[0:modes] + both[modes : 2 * modes]) * jnp.concatenate([damp, damp], axis=1)
            waiting.append(jnp.concatenate(split(hat), axis=0))
        if step >= LAG:
            slot, i = steps[step - LAG]
            both = dot(backward[...], waiting[step - LAG])
            hats[slot, i] = both[0:core] + both[core : 2 * core]
    for slot in range(group):
        q = start + slot
        ex, ey = q // 2, q % 2 * 2
        for h in (0, 1):
            inv = 1.0 / scale[ex, pl.ds(ey + h, 1), :]
            lanes = slice(h * LANES, (h + 1) * LANES)
            for row in range(0, core, 16):
                held = [hats[slot, i, row : row + 16, lanes] for i in range(wide)]
                for a in range(n):
                    total = coeff[a + 1, 0] * held[0]
                    for i in range(1, wide):
                        total += coeff[a + 1, i] * held[i]
                    out[q, h, a, row : row + 16] = total * inv


def tables_kernel(fine_basis, fine_eigen, middle_basis, middle_eigen, after, *refs):
    del after
    fine_in, middle_in, outs = refs[:6], refs[6:12], refs[12:]
    build_tables(FINE, fine_in, fine_basis, fine_eigen, *outs[:3])
    build_tables(MID, middle_in, middle_basis, middle_eigen, *outs[3:6])
    outs[6][...] = fine_basis[0]
    outs[7][...] = middle_basis[0]


def solve_tables(fine_basis, fine_eigen, middle_basis, middle_eigen, after):
    vmem = pl.BlockSpec(memory_space=pltpu.VMEM)
    shapes = []
    for level in (FINE, MID):
        shapes += [
            jax.ShapeDtypeStruct((2 * level.modes, 2 * level.depth), BF16),
            jax.ShapeDtypeStruct((2 * level.core, 2 * level.modes), BF16),
            jax.ShapeDtypeStruct((level.wide, level.modes, LANES), F32),
        ]
    shapes += [jax.ShapeDtypeStruct((level.wide, level.wide), F32) for level in (FINE, MID)]
    return pl.pallas_call(
        tables_kernel,
        out_shape=shapes,
        in_specs=[vmem] * 4 + [pl.BlockSpec(memory_space=pl.ANY)] + [vmem] * 12,
        out_specs=[vmem] * 8,
        compiler_params=pltpu.CompilerParams(vmem_limit_bytes=VMEM_LIMIT),
        cost_estimate=pl.CostEstimate(flops=10**8, bytes_accessed=10**6, transcendentals=0),
        name="tables",
    )(
        fine_basis, fine_eigen, middle_basis, middle_eigen, after,
        *[jnp.asarray(t) for level in (FINE, MID) for t in level.tables()],
    )


def schwarz_kernel(
    residual,
    middle,
    scale,
    fine_coeff,
    middle_coeff,
    x_low,
    x_high,
    y_low,
    y_high,
    forward,
    backward,
    inverse,
    forward_m,
    backward_m,
    inverse_m,
    fine_out,
    middle_out,
    x_up,
    x_down,
    y_up,
    y_down,
    planes,
    rims,
    sides,
    spectrum,
    hats,
    planes_m,
    rims_m,
    sides_m,
    spectrum_m,
    hats_m,
    solved,
    in_sems,
    out_sems,
):
    copies = []
    for ex in range(EX):
        for ey in range(EY):
            copy = pltpu.make_async_copy(
                residual.at[ex, ey], planes.at[ey, pl.ds(2 + 8 * ex, 8)], in_sems.at[ex * EY + ey]
            )
            copy.start()
            copies.append(copy)
    for ex in range(EX):
        for ey in range(EY):
            planes_m[ey, 2 + 4 * ex : 6 + 4 * ex] = middle[ex, ey]
    assemble(MID, planes_m, rims_m, sides_m, x_low, x_high, y_low, y_high)

    def middle_step(step, carry):
        solve_pairs(
            MID, step * MID_GROUP, MID_GROUP, planes_m, rims_m, middle_coeff, forward_m, backward_m,
            inverse_m, scale, spectrum_m, hats_m, middle_out,
        )
        return carry

    lax.fori_loop(0, 8 // MID_GROUP, middle_step, 0)
    for copy in copies:
        copy.wait()
    assemble(FINE, planes, rims, sides, x_low, x_high, y_low, y_high)

    def fine_step(q, carry):
        solve_pairs(
            FINE, q, 1, planes, rims, fine_coeff, forward, backward,
            inverse, scale, spectrum, hats, solved,
        )
        pltpu.make_async_copy(solved.at[q], fine_out.at[q], out_sems.at[q]).start()
        return carry

    lax.fori_loop(0, 8, fine_step, 0)
    for n, source, base in ((8, solved, 0), (4, middle_out, 256)):
        core = n * n
        for out, ex, node in ((x_up, EX - 1, n - 1), (x_down, 0, 0)):
            for ey in range(EY):
                row = base + ey * core
                out[row : row + core] = source[2 * ex + ey // 2, ey % 2, node]
        for out, ey, node in ((y_up, EY - 1, n - 1), (y_down, 0, 0)):
            for ex in range(EX):
                for a in range(n):
                    row = base + (ex * n + a) * n
                    out[row : row + n] = source[
                        2 * ex + ey // 2, ey % 2, a, node * n : node * n + n
                    ]
    for q in range(8):
        pltpu.make_async_copy(solved.at[q], fine_out.at[q], out_sems.at[q]).wait()


def schwarz(residual, middle, scale, halos, tables):
    vmem = pl.BlockSpec(memory_space=pltpu.VMEM)
    smem = pl.BlockSpec(memory_space=pltpu.SMEM)
    hbm = pl.BlockSpec(memory_space=pltpu.HBM)
    face = jax.ShapeDtypeStruct((FACE_ROWS, LANES), F32)

    def scratch(level, group):
        return [
            pltpu.VMEM((EY, level.planes, level.core, LANES), F32),
            pltpu.VMEM((EY, EX * level.n, level.rim, LANES), F32),
            pltpu.VMEM((4, EX * level.core, LANES), F32),
            pltpu.VMEM((group, level.wide, 2 * level.depth, 2 * LANES), BF16),
            pltpu.VMEM((group, level.wide, level.core, 2 * LANES), F32),
        ]

    return pl.pallas_call(
        schwarz_kernel,
        out_shape=[
            jax.ShapeDtypeStruct((8, 2, 8, 64, LANES), F32),
            jax.ShapeDtypeStruct((8, 2, 4, 16, LANES), F32),
        ]
        + [face] * 4,
        in_specs=[hbm, vmem, vmem, smem, smem] + [vmem] * 10,
        out_specs=[hbm] + [vmem] * 5,
        scratch_shapes=scratch(FINE, 1)
        + scratch(MID, MID_GROUP)
        + [
            pltpu.VMEM((8, 2, 8, 64, LANES), F32),
            pltpu.SemaphoreType.DMA((16,)),
            pltpu.SemaphoreType.DMA((8,)),
        ],
        compiler_params=pltpu.CompilerParams(vmem_limit_bytes=VMEM_LIMIT),
        cost_estimate=pl.CostEstimate(
            flops=10**11, bytes_accessed=12 * 10**6, transcendentals=0
        ),
        name="schwarz",
    )(residual, middle, scale, *tables[6:], *halos, *tables[:6])


def coarse_kernel(rows_x, gathered, table, out, held, part):
    own_x, own_y = lax.axis_index("px"), lax.axis_index("py")
    high, low = split(table[0:64])
    forward_y = jnp.concatenate([high, low], axis=0)[:, 0:80]

    def y_step(p, carry):
        slabs = []
        for lx in range(4):
            pieces = []
            for ly in range(5):
                row = p * (16 * VERTEX_ROWS) + lx * 5 + ly
                pieces.append(gathered[pl.ds(row, 16, stride=VERTEX_ROWS), :])
            slabs.append(jnp.concatenate(pieces, axis=0))
        for half in (0, 2):
            high, low = split(jnp.concatenate([slabs[half], slabs[half + 1]], axis=1))
            both = dot(forward_y, high)
            total = both[0:64] + both[64:128] + dot(forward_y[0:64], low)
            held[4 * p + half] = total[:, 0:LANES]
            held[4 * p + half + 1] = total[:, LANES : 2 * LANES]
        return carry

    lax.fori_loop(0, 8, y_step, 0)
    angle = 2.0 * np.pi / 32
    eigen_x = line_eigen(32)

    def x_step(chunk, carry):
        rows = pl.ds(pl.multiple_of(chunk * 8, 8), 8)
        values = [held[x, rows, :] for x in range(32)]
        even = [values[0]] + [values[x] + values[32 - x] for x in range(1, 16)] + [values[16]]
        odd = [None] + [values[x] - values[32 - x] for x in range(1, 16)]
        base = table[pl.ds(pl.multiple_of(64 + chunk * 8, 8), 8), :]
        totals = [None] * 5
        for k in range(17):
            cosine = even[0]
            for x in range(1, 17):
                cosine = cosine + float(np.cos(angle * (k * x % 32))) * even[x]
            modes = [(k, cosine)]
            if 0 < k < 16:
                sine = float(np.sin(angle * k)) * odd[1]
                for x in range(2, 16):
                    sine = sine + float(np.sin(angle * (k * x % 32))) * odd[x]
                modes = [(k, cosine + sine), (32 - k, cosine - sine)]
            damp = 1.0 / (base + float(24.0 * eigen_x[k]))
            for kx, value in modes:
                value = value * damp
                for lx in range(5):
                    term = rows_x[lax.rem(own_x * 4 + lx, 32), kx] * value
                    totals[lx] = term if totals[lx] is None else totals[lx] + term
        for lx in range(5):
            part[lx, rows, :] = totals[lx]
        return carry

    lax.fori_loop(0, 8, x_step, 0)
    own_rows = table[pl.ds(pl.multiple_of(256 + own_y * 8, 8), 8), :][:, 0:64]
    solved = jnp.concatenate([exact_dot(own_rows, part[lx]) for lx in range(5)], axis=0)
    out[...] = exact_dot(solved, table[128:256]) * (1.0 / (32 * 64 * 128))


def coarse_table():
    table_y = hartley(64)
    out = np.zeros((384, 128), np.float32)
    for q in range(16):
        for ly in range(5):
            out[0:64, ly * 16 + q] = table_y[:, (4 * q + ly) % 64]
            out[256 + 8 * q + ly, 0:64] = table_y[(4 * q + ly) % 64]
    out[64:128] = 24.0 * (line_eigen(64)[:, None] + line_eigen(128)[None, :]) + 0.5
    out[128:256] = hartley(128)
    return out


def coarse(gathered):
    vmem = pl.BlockSpec(memory_space=pltpu.VMEM)
    smem = pl.BlockSpec(memory_space=pltpu.SMEM)
    return pl.pallas_call(
        coarse_kernel,
        out_shape=jax.ShapeDtypeStruct((40, LANES), F32),
        in_specs=[smem, vmem, vmem],
        out_specs=vmem,
        scratch_shapes=[
            pltpu.VMEM((32, 64, LANES), F32),
            pltpu.VMEM((5, 64, LANES), F32),
        ],
        compiler_params=pltpu.CompilerParams(vmem_limit_bytes=16 * MIB),
        cost_estimate=pl.CostEstimate(
            flops=2 * 10**9, bytes_accessed=4 * 10**6, transcendentals=0
        ),
        name="coarse",
    )(jnp.asarray(hartley(32), F32), gathered, jnp.asarray(coarse_table()))


def average_faces(level, field, sides, x_low, x_high, y_low, y_high):
    n, core = level.n, level.core
    base = 0 if n == 8 else 256

    def at(ex, ey):
        return 2 * ex + ey // 2, ey % 2

    for ey in range(EY):
        row = base + ey * core
        q, h = at(0, ey)
        field[q, h, 0] = 0.5 * (field[q, h, 0] + x_low[row : row + core])
        q, h = at(EX - 1, ey)
        field[q, h, n - 1] = 0.5 * (field[q, h, n - 1] + x_high[row : row + core])
        for ex in range(EX - 1):
            q, h = at(ex, ey)
            total = 0.5 * (field[q, h, n - 1] + field[q + 2, h, 0])
            field[q, h, n - 1] = total
            field[q + 2, h, 0] = total
    for side, halo in ((0, y_low), (1, y_high)):
        sides[side] = halo[base : base + EX * core]
    for ex in range(EX):
        for a in range(n):
            row = (ex * n + a) * n
            q, h = at(ex, 0)
            field[q, h, a, 0:n] = 0.5 * (field[q, h, a, 0:n] + sides[0, row : row + n])
            q, h = at(ex, EY - 1)
            field[q, h, a, core - n : core] = 0.5 * (
                field[q, h, a, core - n : core] + sides[1, row : row + n]
            )
            for ey in range(EY - 1):
                q, h = at(ex, ey)
                p, g = at(ex, ey + 1)
                total = 0.5 * (field[q, h, a, core - n : core] + field[p, g, a, 0:n])
                field[q, h, a, core - n : core] = total
                field[p, g, a, 0:n] = total


def finish_kernel(
    fine, middle, coarse_part, prolong, x_low, x_high, y_low, y_high,
    out, field, sides, field_m, sides_m, corner, result, in_sems, out_sems,
):
    copies = []
    for q in range(8):
        copy = pltpu.make_async_copy(fine.at[q], field.at[q], in_sems.at[q])
        copy.start()
        copies.append(copy)
    field_m[...] = middle[...]
    average_faces(MID, field_m, sides_m, x_low, x_high, y_low, y_high)
    near = coarse_part[...]
    far = pltpu.roll(near, LANES - 1, 1)
    for q in range(8):
        for h in (0, 1):
            ex, ey = q // 2, (q % 2) * 2 + h
            corner[q, h, 8:16] = jnp.zeros((8, LANES), F32)
            for i in (0, 1):
                for j in (0, 1):
                    row = (ex + i) * 8 + ey + j
                    place = i * 4 + j * 2
                    corner[q, h, place : place + 1] = near[row : row + 1]
                    corner[q, h, place + 1 : place + 2] = far[row : row + 1]
    for copy in copies:
        copy.wait()
    average_faces(FINE, field, sides, x_low, x_high, y_low, y_high)

    def step(q, carry):
        for h in (0, 1):
            for a in range(4):
                sum_lines(field_m, (q, h, a), 4, 0.5)
            for a in range(8):
                sum_lines(field, (q, h, a), 8, 0.5)
        level = jnp.concatenate(
            [field_m[q, 0].reshape(64, LANES), field_m[q, 1].reshape(64, LANES)], axis=1
        )
        high, low = split(level)
        ends = jnp.concatenate([corner[q, 0], corner[q, 1]], axis=1)
        ends_high, ends_low = split(ends)
        stacked = jnp.concatenate([high, low, high, ends_high, ends_low, ends_high], axis=0)
        total = dot(prolong[...], stacked)
        for h in (0, 1):
            part = total[:, h * LANES : (h + 1) * LANES]
            result[q, h] = field[q, h] + part.reshape(8, 64, LANES)
        pltpu.make_async_copy(result.at[q], out.at[q], out_sems.at[q]).start()
        return carry

    lax.fori_loop(0, 8, step, 0)
    for q in range(8):
        pltpu.make_async_copy(result.at[q], out.at[q], out_sems.at[q]).wait()


def finish(fine, middle, coarse_part, halos):
    vmem = pl.BlockSpec(memory_space=pltpu.VMEM)
    hbm = pl.BlockSpec(memory_space=pl.ANY)
    return pl.pallas_call(
        finish_kernel,
        out_shape=jax.ShapeDtypeStruct((8, 2, 8, 64, LANES), F32),
        in_specs=[hbm] + [vmem] * 7,
        out_specs=hbm,
        scratch_shapes=[
            pltpu.VMEM((8, 2, 8, 64, LANES), F32),
            pltpu.VMEM((2, EX * 64, LANES), F32),
            pltpu.VMEM((8, 2, 4, 16, LANES), F32),
            pltpu.VMEM((2, EX * 16, LANES), F32),
            pltpu.VMEM((8, 2, 16, LANES), F32),
            pltpu.VMEM((8, 2, 8, 64, LANES), F32),
            pltpu.SemaphoreType.DMA((8,)),
            pltpu.SemaphoreType.DMA((8,)),
        ],
        compiler_params=pltpu.CompilerParams(vmem_limit_bytes=16 * MIB),
        cost_estimate=pl.CostEstimate(
            flops=2 * 10**9, bytes_accessed=8 * 10**6, transcendentals=0
        ),
        name="finish",
    )(fine, middle, coarse_part, jnp.asarray(prolong_matrix()), *halos)


def shift(values, axis, step):
    count = lax.axis_size(axis)
    return lax.ppermute(values, axis, [(i, (i + step) % count) for i in range(count)])


def on_device(residual, scale, fine_basis, fine_eigen, middle_basis, middle_eigen):
    shape = residual.shape
    residual = residual.reshape(EX, EY, 8, 64, LANES)
    x_up, x_down, y_up, y_down, middle, vertex = pack(residual)
    x_halos = shift(x_up, "px", 1), shift(x_down, "px", -1)
    tables = solve_tables(fine_basis, fine_eigen, middle_basis, middle_eigen, vertex)
    y_up, y_down, vertex = join(*x_halos, y_up, y_down, vertex, tables[-1])
    halos = x_halos + (shift(y_up, "py", 1), shift(y_down, "py", -1))
    devices = lax.axis_size("px") * lax.axis_size("py")
    gathered = lax.all_to_all(spread(vertex, devices), ("px", "py"), 0, 0)
    gathered = gathered.reshape(devices * VERTEX_ROWS, LANES)
    fine_solved, middle_solved, x_up, x_down, y_up, y_down = schwarz(
        residual, middle, scale, halos, tables
    )
    x_halos = shift(x_up, "px", 1), shift(x_down, "px", -1)
    y_up, y_down = join_faces(*x_halos, y_up, y_down)
    halos = x_halos + (shift(y_up, "py", 1), shift(y_down, "py", -1))
    coarse_part = coarse(gathered)
    return finish(fine_solved, middle_solved, coarse_part, halos).reshape(shape)


def solution(mesh):
    placed = (P("px", "py", None, None, None, None), P("px", "py", None), P(), P(), P(), P())
    return jax.shard_map(
        on_device,
        mesh=mesh,
        in_specs=placed,
        out_specs=P("px", "py", None, None, None, None),
        check_vma=False,
    )
```

```python
import functools
import math

import jax
import jax.numpy as jnp
import ml_dtypes
import numpy as np
from jax import lax
from jax.experimental import pallas as pl
from jax.experimental.pallas import tpu as pltpu
from jax.sharding import PartitionSpec as P

F32, BF16 = jnp.float32, jnp.bfloat16
HIGHEST = lax.Precision.HIGHEST
LANES = 128
EX = EY = 4
MID_GROUP = 4
LAG = 5
MIB = 1024 * 1024
VMEM_LIMIT = 60 * MIB


def lobatto(count):
    return -np.cos(np.arange(count) * (np.pi / (count - 1)))


def interpolation(fine_count, coarse_count):
    fine, coarse = lobatto(fine_count), lobatto(coarse_count)
    out = np.ones((fine_count, coarse_count))
    for j in range(coarse_count):
        for m in range(coarse_count):
            if m != j:
                out[:, j] *= (fine - coarse[m]) / (coarse[j] - coarse[m])
    return out


def hartley(count):
    phase = np.outer(np.arange(count), np.arange(count)) % count
    angle = phase * (2.0 * np.pi / count)
    return np.cos(angle) + np.sin(angle)


def line_eigen(count):
    return 2.0 - 2.0 * np.cos(np.arange(count) * (2.0 * np.pi / count))


def split_np(values):
    values = np.asarray(values, np.float32)
    high = values.astype(ml_dtypes.bfloat16)
    low = (values - high.astype(np.float32)).astype(ml_dtypes.bfloat16)
    return high, low


def split(values):
    high = values.astype(BF16)
    return high, (values - high.astype(F32)).astype(BF16)


def dot(left, right):
    return jnp.dot(left, right, preferred_element_type=F32)


def exact_dot(left, right, contract=((1,), (0,))):
    return lax.dot_general(
        left, right, (contract, ((), ())), precision=HIGHEST, preferred_element_type=F32
    )


INTERP_FINE = interpolation(8, 4)
INTERP_MID = interpolation(4, 2)
INTERP_ALL = INTERP_FINE @ INTERP_MID


def kron3(m):
    return np.kron(np.kron(m, m), m)


def restrict_matrix():
    rows = np.zeros((80, 512))
    rows[:64] = kron3(INTERP_FINE).T
    rows[64:72] = kron3(INTERP_ALL).T
    high, low = split_np(rows)
    return np.concatenate([high, low], axis=0)


def prolong_matrix():
    fine = kron3(INTERP_FINE)
    coarse = np.zeros((512, 16))
    coarse[:, :8] = kron3(INTERP_ALL)
    fine_high, fine_low = split_np(fine)
    coarse_high, coarse_low = split_np(coarse)
    return np.concatenate(
        [fine_high, fine_high, fine_low, coarse_high, coarse_high, coarse_low], axis=1
    )


def vertex_matrices():
    out = np.zeros((2, 32, 128), np.float32)
    for ex in range(EX):
        for ey in range(EY):
            for i in (0, 1):
                for j in (0, 1):
                    for k in (0, 1):
                        column = (ex * EY + ey) * 8 + i * 4 + j * 2 + k
                        out[k, (ex + i) * 5 + ey + j, column] = 1.0
    return out


class Level:
    def __init__(self, n):
        self.n = n
        self.wide = n + 2
        self.core = n * n
        self.rim = 4 * n
        self.depth = self.core + self.rim
        self.modes = -(-(self.wide * self.wide) // 16) * 16
        self.planes = EX * n + 4

    def tables(self):
        n, wide = self.n, self.wide
        first = np.zeros((2 * self.modes, wide), np.float32)
        second = np.zeros((2 * self.modes, wide), np.float32)
        for half in (0, 1):
            for j in range(wide):
                for k in range(wide):
                    first[half * self.modes + j * wide + k, j] = 1.0
                    second[half * self.modes + j * wide + k, k] = 1.0
        inner = list(range(1, n + 1))
        points = [(b, c) for b in inner for c in inner]
        points += [(0, c) for c in inner] + [(n + 1, c) for c in inner]
        points += [(b, 0) for b in inner] + [(b, n + 1) for b in inner]
        pick_b = np.zeros((wide, 2 * self.depth), np.float32)
        pick_c = np.zeros((wide, 2 * self.depth), np.float32)
        for half in (0, 1):
            for column, (b, c) in enumerate(points):
                pick_b[b, half * self.depth + column] = 1.0
                pick_c[c, half * self.depth + column] = 1.0
        return (
            first,
            second,
            pick_b,
            pick_c,
            np.ascontiguousarray(pick_b[:, : self.core].T),
            np.ascontiguousarray(pick_c[:, : self.core].T),
        )


FINE, MID = Level(8), Level(4)

LAYER_ROWS = 640
X_ROWS = 648
FACE_ROWS = 320
VERTEX_ROWS = 24
EDGE_ROWS = 72
EDGE_FACE_ROWS = 24


def edge_row(n, side, kind):
    return (0 if n == 8 else 48) + (side * 3 + kind) * n


def edge_face_row(n, side):
    return (0 if n == 8 else 16) + side * n


class Either:
    def __init__(self, flag, yes, no):
        self.flag, self.yes, self.no = flag, yes, no

    def __getitem__(self, index):
        return jnp.where(self.flag, self.yes[index], self.no[index])


def is_even(axis):
    return lax.rem(lax.axis_index(axis), 2) == 0


def received(axis, first, second):
    flag = is_even(axis)
    return Either(flag, second, first), Either(flag, first, second)


def for_partners(axis, first, second, write):
    @pl.when(is_even(axis))
    def _():
        write(first, second)

    @pl.when(jnp.logical_not(is_even(axis)))
    def _():
        write(second, first)


def pack_kernel(
    residual,
    restrict_in,
    vertex_pick_in,
    hartley_in,
    x_first,
    x_second,
    y_first,
    y_second,
    middle,
    vertex,
    field,
    corners,
    restrict,
    vertex_pick,
    hartley_z,
    sems,
):
    moves = [(restrict_in, restrict)]
    moves += [(residual.at[ex], field.at[ex]) for ex in range(EX)]
    moves += [(vertex_pick_in, vertex_pick), (hartley_in, hartley_z)]
    copies = []
    for place, (source, target) in enumerate(moves):
        copies.append(pltpu.make_async_copy(source, target, sems.at[place]))
        copies[-1].start()
    copies[0].wait()
    for ex in range(EX):
        copies[1 + ex].wait()
        for pair in range(EY // 2):
            ey = 2 * pair
            values = jnp.concatenate(
                [field[ex, ey].reshape(512, LANES), field[ex, ey + 1].reshape(512, LANES)], axis=1
            )
            high, low = split(values)
            upper = dot(restrict[...], high)
            lower = dot(restrict[0:80, :], low)
            total = upper[0:80] + upper[80:160] + lower
            for h in (0, 1):
                part = total[:, h * LANES : (h + 1) * LANES]
                for i in range(4):
                    middle[ex, ey + h, i] = part[16 * i : 16 * i + 16]
                column = ex * EY + ey + h
                corners[8 * column : 8 * column + 8] = part[64:72]
    copies[EX + 1].wait()
    copies[EX + 2].wait()
    values = corners[...]
    near = exact_dot(vertex_pick[0], values)
    far = exact_dot(vertex_pick[1], values)
    total = exact_dot(near + pltpu.roll(far, 1, 1), hartley_z[...])
    vertex[...] = total

    def write_x(x_up, x_down):
        for out, ex, nodes, mids in ((x_up, EX - 1, (7, 6), (3, 2)), (x_down, 0, (0, 1), (0, 1))):
            for layer in (0, 1):
                for ey in range(EY):
                    row = (layer * EY + ey) * 64
                    out[row : row + 64] = field[ex, ey, nodes[layer]]
                    row = 512 + (layer * EY + ey) * 16
                    out[row : row + 16] = middle[ex, ey, mids[layer]]
        x_up[LAYER_ROWS:X_ROWS] = vertex[20:28]
        x_down[LAYER_ROWS:X_ROWS] = jnp.zeros((8, LANES), F32)

    for_partners("px", x_first, x_second, write_x)
    def write_y(y_up, y_down):
        for out, ey, nodes, mids in ((y_up, EY - 1, (7, 6), (3, 2)), (y_down, 0, (0, 1), (0, 1))):
            for layer in (0, 1):
                for ex in range(EX):
                    for a in range(8):
                        row = (layer * EX + ex) * 64 + a * 8
                        line = nodes[layer] * 8
                        out[row : row + 8] = field[ex, ey, a, line : line + 8]
                    for a in range(4):
                        row = 512 + (layer * EX + ex) * 16 + a * 4
                        line = mids[layer] * 4
                        out[row : row + 4] = middle[ex, ey, a, line : line + 4]
            for n, base in ((8, 0), (4, 512)):
                core = n * n
                for row in [base + k * core for k in (1, 2, 3, 5, 6, 7)]:
                    total = out[row - n : row] + out[row : row + n]
                    out[row - n : row] = total
                    out[row : row + n] = total

    for_partners("py", y_first, y_second, write_y)


def pack(residual):
    x_halo = jax.ShapeDtypeStruct((X_ROWS, LANES), F32)
    y_halo = jax.ShapeDtypeStruct((LAYER_ROWS, LANES), F32)
    vmem = pl.BlockSpec(memory_space=pltpu.VMEM)
    return pl.pallas_call(
        pack_kernel,
        out_shape=[x_halo] * 2
        + [y_halo] * 2
        + [
            jax.ShapeDtypeStruct((EX, EY, 4, 16, LANES), F32),
            jax.ShapeDtypeStruct((32, LANES), F32),
        ],
        in_specs=[pl.BlockSpec(memory_space=pltpu.HBM)] * 4,
        out_specs=[vmem] * 6,
        scratch_shapes=[
            pltpu.VMEM((EX, EY, 8, 64, LANES), F32),
            pltpu.VMEM((128, LANES), F32),
            pltpu.VMEM((160, 512), BF16),
            pltpu.VMEM((2, 32, 128), F32),
            pltpu.VMEM((128, 128), F32),
            pltpu.SemaphoreType.DMA((EX + 3,)),
        ],
        compiler_params=pltpu.CompilerParams(vmem_limit_bytes=VMEM_LIMIT),
        cost_estimate=pl.CostEstimate(flops=10**9, bytes_accessed=8 * 10**6, transcendentals=0),
        name="pack",
    )(
        residual,
        jnp.asarray(restrict_matrix()),
        jnp.asarray(vertex_matrices()),
        jnp.asarray(hartley(128), F32),
    )


def join_kernel(x_first, x_second, vertex, after, first, second, summed):
    del after
    x_low, x_high = received("px", x_first, x_second)

    def write(up, down):
        for out, ey, ends in ((up, EY - 1, True), (down, 0, False)):
            for n, base in ((8, 0), (4, 512)):
                face, inner = (n - 1, n - 2) if ends else (0, 1)
                for kind, (layer, node) in enumerate(((0, face), (0, inner), (1, face))):
                    line = base + (layer * EY + ey) * n * n + node * n
                    for side, halo in ((0, x_low), (1, x_high)):
                        row = edge_row(n, side, kind)
                        out[row : row + n] = halo[line : line + n]

    for_partners("py", first, second, write)
    summed[...] = vertex[0:VERTEX_ROWS]
    summed[0:5] += x_low[LAYER_ROWS : LAYER_ROWS + 5]
    summed[20:24] = jnp.zeros((4, LANES), F32)


def join(x_halos, vertex, after):
    vmem = pl.BlockSpec(memory_space=pltpu.VMEM)
    edge = jax.ShapeDtypeStruct((EDGE_ROWS, LANES), F32)
    return pl.pallas_call(
        join_kernel,
        out_shape=[edge, edge, jax.ShapeDtypeStruct((VERTEX_ROWS, LANES), F32)],
        in_specs=[vmem] * 3 + [pl.BlockSpec(memory_space=pl.ANY)],
        out_specs=[vmem] * 3,
        compiler_params=pltpu.CompilerParams(vmem_limit_bytes=8 * MIB),
        cost_estimate=pl.CostEstimate(flops=10**6, bytes_accessed=10**6, transcendentals=0),
        name="join",
    )(*x_halos, vertex, after)


def join_faces_kernel(x_first, x_second, first, second):
    x_low, x_high = received("px", x_first, x_second)

    def write(up, down):
        for out, ey, ends in ((up, EY - 1, True), (down, 0, False)):
            for n, base in ((8, 0), (4, 256)):
                core = n * n
                line = base + ey * core + (core - n if ends else 0)
                for side, halo in ((0, x_low), (1, x_high)):
                    row = edge_face_row(n, side)
                    out[row : row + n] = halo[line : line + n]

    for_partners("py", first, second, write)


def join_faces(x_halos):
    vmem = pl.BlockSpec(memory_space=pltpu.VMEM)
    edge = jax.ShapeDtypeStruct((EDGE_FACE_ROWS, LANES), F32)
    return pl.pallas_call(
        join_faces_kernel,
        out_shape=[edge, edge],
        in_specs=[vmem] * 2,
        out_specs=[vmem] * 2,
        compiler_params=pltpu.CompilerParams(vmem_limit_bytes=8 * MIB),
        cost_estimate=pl.CostEstimate(flops=10**6, bytes_accessed=10**6, transcendentals=0),
        name="join_faces",
    )(*x_halos)


def spread_kernel(source, out):
    out[...] = jnp.broadcast_to(source[...][None], out.shape)


def spread(values, count):
    vmem = pl.BlockSpec(memory_space=pltpu.VMEM)
    return pl.pallas_call(
        spread_kernel,
        out_shape=jax.ShapeDtypeStruct((count,) + values.shape, F32),
        in_specs=[vmem],
        out_specs=vmem,
        compiler_params=pltpu.CompilerParams(vmem_limit_bytes=VMEM_LIMIT),
        cost_estimate=pl.CostEstimate(flops=10**6, bytes_accessed=2 * 10**6, transcendentals=0),
        name="spread",
    )(values)


def sum_lines(ref, lead, n, scale=None):
    count = ref.shape[-2] // n
    low_rows = lead + (pl.ds(0, count, stride=n), slice(None))
    high_rows = lead + (pl.ds(n - 1, count, stride=n), slice(None))
    low, high = ref[low_rows], ref[high_rows]
    new_low = low + pltpu.roll(high, 1, 1)
    new_high = high + pltpu.roll(low, LANES - 1, 1)
    if scale is not None:
        new_low, new_high = new_low * scale, new_high * scale
    ref[low_rows] = new_low
    ref[high_rows] = new_high


def assemble(level, planes, rims, sides, x_low, x_high, y_low, y_high, edges):
    n, core = level.n, level.core
    last = EX * n + 3
    base = 0 if n == 8 else 512
    for ey in range(EY):
        row = base + ey * core
        planes[ey, 2] += x_low[row : row + core]
        planes[ey, last - 2] += x_high[row : row + core]
        for ex in range(EX - 1):
            left = 2 + ex * n + n - 1
            total = planes[ey, left] + planes[ey, left + 1]
            planes[ey, left] = total
            planes[ey, left + 1] = total
        row = base + (EY + ey) * core
        planes[ey, 0] = x_low[row : row + core]
        planes[ey, last] = x_high[row : row + core]
    for side, halo in ((0, y_low), (1, y_high)):
        for layer in (0, 1):
            kind = 2 * side + layer
            start = base + layer * EX * core
            sides[kind] = halo[start : start + EX * core]
            row = edge_row(n, 0, layer)
            sides[kind, 0:n] += edges[side][row : row + n]
            row = edge_row(n, 1, layer)
            sides[kind, EX * core - n : EX * core] += edges[side][row : row + n]
    for plane in range(EX * n):
        row = plane * n
        planes[0, 2 + plane, 0:n] += sides[0, row : row + n]
        planes[EY - 1, 2 + plane, core - n : core] += sides[2, row : row + n]
    for side, plane in ((0, 0), (1, last)):
        row = edge_row(n, side, 2)
        planes[0, plane, 0:n] += edges[0][row : row + n]
        planes[EY - 1, plane, core - n : core] += edges[1][row : row + n]
    for ey in range(EY - 1):
        for plane in [0, last] + list(range(2, 2 + EX * n)):
            total = planes[ey, plane, core - n : core] + planes[ey + 1, plane, 0:n]
            planes[ey, plane, core - n : core] = total
            planes[ey + 1, plane, 0:n] = total
    for ey in range(EY):
        for plane in [0, last] + list(range(2, 2 + EX * n)):
            sum_lines(planes, (ey, plane), n)
    for kind in (1, 3):
        sum_lines(sides, (kind,), n)
    for ey in range(EY):
        for plane in range(EX * n):
            at = 2 + plane
            row = plane * n
            low = planes[ey - 1, at, core - 2 * n : core - n] if ey else sides[1, row : row + n]
            high = planes[ey + 1, at, n : 2 * n] if ey < EY - 1 else sides[3, row : row + n]
            rims[ey, plane, 0:n] = low
            rims[ey, plane, n : 2 * n] = high
            rims[ey, plane, 2 * n : 3 * n] = pltpu.roll(
                planes[ey, at, pl.ds(n - 2, n, stride=n), :], 1, 1
            )
            rims[ey, plane, 3 * n : 4 * n] = pltpu.roll(
                planes[ey, at, pl.ds(1, n, stride=n), :], LANES - 1, 1
            )


def build_tables(level, tables, basis, eigen, forward, backward, lines_out):
    first, second, pick_b, pick_c, core_b, core_c = tables
    modes, depth = level.modes, level.depth
    rows_b = exact_dot(first[0:modes], basis[1], ((1,), (1,)))
    rows_c = exact_dot(second[0:modes], basis[2], ((1,), (1,)))
    matrix = exact_dot(rows_b, pick_b[...]) * exact_dot(rows_c, pick_c[...])
    high, low = split(matrix)
    keep = lax.broadcasted_iota(jnp.int32, matrix.shape, 1) < depth
    forward[0:modes] = high
    forward[modes : 2 * modes] = jnp.where(keep, low.astype(F32), 0.0).astype(BF16)
    out_b = exact_dot(exact_dot(core_b[...], basis[1]), first[...], ((1,), (1,)))
    out_c = exact_dot(exact_dot(core_c[...], basis[2]), second[...], ((1,), (1,)))
    matrix = out_b * out_c
    high, low = split(matrix)
    keep = lax.broadcasted_iota(jnp.int32, matrix.shape, 1) < modes
    backward[0 : level.core] = high
    backward[level.core : 2 * level.core] = jnp.where(keep, low.astype(F32), 0.0).astype(BF16)
    wide = level.wide
    spread_b = jnp.broadcast_to(eigen[1:2, :], (LANES, wide))
    spread_c = jnp.broadcast_to(eigen[2:3, :], (LANES, wide))
    lines = exact_dot(first[0:modes], spread_b, ((1,), (1,)))
    lines += exact_dot(second[0:modes], spread_c, ((1,), (1,)))
    lines_out[...] = lines


def first_steps(level, q, planes, rims, coeff, spectrum):
    n, wide, core, depth = level.n, level.wide, level.core, level.depth
    offsets = [0] + [2 + a for a in range(n)] + [n + 3]
    base, ey = q // 2 * n, q % 2 * 2

    def contract(load, nodes, row):
        held = [[load(h, e) for h in (0, 1)] for e in nodes]
        for i in range(wide):
            for h in (0, 1):
                total = coeff[nodes[0], i] * held[0][h]
                for position in range(1, len(nodes)):
                    total += coeff[nodes[position], i] * held[position][h]
                high, low = split(total)
                lanes = slice(h * LANES, (h + 1) * LANES)
                spectrum[i, row : row + 16, lanes] = high
                spectrum[i, depth + row : depth + row + 16, lanes] = low

    def inner(row):
        load = lambda h, e: planes[ey + h, base + offsets[e], row : row + 16]
        contract(load, list(range(wide)), row)

    def outer(row):
        load = lambda h, e: rims[ey + h, base + e - 1, row : row + 16]
        contract(load, list(range(1, n + 1)), core + row)

    steps = [functools.partial(inner, row) for row in range(0, core, 16)]
    return steps + [functools.partial(outer, row) for row in range(0, level.rim, 16)]


def last_steps(level, q, hats, coeff, scale, out):
    n, wide, core = level.n, level.wide, level.core
    ex, ey = q // 2, q % 2 * 2

    def back(h, row):
        inv = 1.0 / scale[ex, pl.ds(ey + h, 1), :]
        lanes = slice(h * LANES, (h + 1) * LANES)
        held = [hats[i, row : row + 16, lanes] for i in range(wide)]
        for a in range(n):
            total = coeff[a + 1, 0] * held[0]
            for i in range(1, wide):
                total += coeff[a + 1, i] * held[i]
            out[q, h, a, row : row + 16] = total * inv

    return [functools.partial(back, h, row) for h in (0, 1) for row in range(0, core, 16)]


def products(level, slots, forward, backward, inverse, lag):
    core, modes = level.core, level.modes
    waiting = []
    steps = [(spectrum, hats, i) for spectrum, hats in slots for i in range(level.wide)]
    for step in range(len(steps) + lag):
        if step < len(steps):
            spectrum, _, i = steps[step]
            both = dot(forward[...], spectrum[i])
            damp = inverse[i]
            hat = (both[0:modes] + both[modes : 2 * modes]) * jnp.concatenate([damp, damp], axis=1)
            waiting.append(jnp.concatenate(split(hat), axis=0))
        if step >= lag:
            _, hats, i = steps[step - lag]
            both = dot(backward[...], waiting[step - lag])
            hats[i] = both[0:core] + both[core : 2 * core]


def tables_kernel(
    fine_basis, fine_eigen, middle_basis, middle_eigen, after, *refs
):
    del after
    fine_in, middle_in, outs = refs[:6], refs[6:12], refs[12:]
    build_tables(FINE, fine_in, fine_basis, fine_eigen, *outs[:3])
    build_tables(MID, middle_in, middle_basis, middle_eigen, *outs[3:6])
    outs[6][...] = fine_basis[0]
    outs[7][...] = middle_basis[0]


def solve_tables(fine_basis, fine_eigen, middle_basis, middle_eigen, after):
    vmem = pl.BlockSpec(memory_space=pltpu.VMEM)
    shapes = []
    for level in (FINE, MID):
        shapes += [
            jax.ShapeDtypeStruct((2 * level.modes, 2 * level.depth), BF16),
            jax.ShapeDtypeStruct((2 * level.core, 2 * level.modes), BF16),
            jax.ShapeDtypeStruct((level.modes, LANES), F32),
        ]
    shapes += [jax.ShapeDtypeStruct((level.wide, level.wide), F32) for level in (FINE, MID)]
    return pl.pallas_call(
        tables_kernel,
        out_shape=shapes,
        in_specs=[vmem] * 4 + [pl.BlockSpec(memory_space=pl.ANY)] + [vmem] * 12,
        out_specs=[vmem] * 8,
        compiler_params=pltpu.CompilerParams(vmem_limit_bytes=VMEM_LIMIT),
        cost_estimate=pl.CostEstimate(flops=10**8, bytes_accessed=10**6, transcendentals=0),
        name="tables",
    )(
        fine_basis, fine_eigen, middle_basis, middle_eigen, after,
        *[jnp.asarray(t) for level in (FINE, MID) for t in level.tables()],
    )


def schwarz_kernel(
    residual,
    middle,
    scale,
    fine_coeff,
    middle_coeff,
    x_first,
    x_second,
    y_first,
    y_second,
    edge_first,
    edge_second,
    forward,
    backward,
    lines,
    forward_m,
    backward_m,
    lines_m,
    fine_eigen,
    middle_eigen,
    fine_out,
    middle_out,
    face_first,
    face_second,
    line_first,
    line_second,
    planes,
    rims,
    sides,
    spectrum,
    hats,
    planes_m,
    rims_m,
    sides_m,
    spectrum_m,
    hats_m,
    solved,
    inverse,
    inverse_m,
    in_sems,
    out_sems,
):
    x_low, x_high = received("px", x_first, x_second)
    y_low, y_high = received("py", y_first, y_second)
    edges = received("py", edge_first, edge_second)
    copies = []
    for ex in range(EX):
        for ey in range(EY):
            copy = pltpu.make_async_copy(
                residual.at[ex, ey], planes.at[ey, pl.ds(2 + 8 * ex, 8)], in_sems.at[ex * EY + ey]
            )
            copy.start()
            copies.append(copy)
    for ex in range(EX):
        for ey in range(EY):
            planes_m[ey, 2 + 4 * ex : 6 + 4 * ex] = middle[ex, ey]
    assemble(MID, planes_m, rims_m, sides_m, x_low, x_high, y_low, y_high, edges)

    for level, inverse_out, lines_in, eigen in (
        (FINE, inverse, lines, fine_eigen),
        (MID, inverse_m, lines_m, middle_eigen),
    ):
        for i in range(level.wide):
            inverse_out[i] = 1.0 / (lines_in[...] + eigen[0, i])

    def middle_step(step, carry):
        pairs = [MID_GROUP * step + k for k in range(MID_GROUP)]
        for k, q in enumerate(pairs):
            for run in first_steps(MID, q, planes_m, rims_m, middle_coeff, spectrum_m.at[k]):
                run()
        slots = [(spectrum_m.at[k], hats_m.at[k]) for k in range(MID_GROUP)]
        products(MID, slots, forward_m, backward_m, inverse_m, LAG)
        for k, q in enumerate(pairs):
            for run in last_steps(MID, q, hats_m.at[k], middle_coeff, scale, middle_out):
                run()
        return carry

    lax.fori_loop(0, 8 // MID_GROUP, middle_step, 0)
    for copy in copies:
        copy.wait()
    assemble(FINE, planes, rims, sides, x_low, x_high, y_low, y_high, edges)

    def fine_step(q, carry):
        for run in first_steps(FINE, q, planes, rims, fine_coeff, spectrum):
            run()
        products(FINE, [(spectrum, hats)], forward, backward, inverse, LAG)
        for run in last_steps(FINE, q, hats, fine_coeff, scale, solved):
            run()
        pltpu.make_async_copy(solved.at[q], fine_out.at[q], out_sems.at[q]).start()
        return carry

    lax.fori_loop(0, 8, fine_step, 0)

    def write_x(x_up, x_down):
        for n, source, base in ((8, solved, 0), (4, middle_out, 256)):
            for out, ex, node in ((x_up, EX - 1, n - 1), (x_down, 0, 0)):
                for ey in range(EY):
                    row = base + ey * n * n
                    out[row : row + n * n] = source[2 * ex + ey // 2, ey % 2, node]

    for_partners("px", face_first, face_second, write_x)

    def write_y(y_up, y_down):
        for n, source, base in ((8, solved, 0), (4, middle_out, 256)):
            core = n * n
            for out, ey, node in ((y_up, EY - 1, n - 1), (y_down, 0, 0)):
                for ex in range(EX):
                    for a in range(n):
                        row = base + (ex * n + a) * n
                        out[row : row + n] = source[
                            2 * ex + ey // 2, ey % 2, a, node * n : node * n + n
                        ]
                for ex in range(1, EX):
                    row = base + ex * core
                    total = 0.5 * (out[row - n : row] + out[row : row + n])
                    out[row - n : row] = total
                    out[row : row + n] = total

    for_partners("py", line_first, line_second, write_y)
    for q in range(8):
        pltpu.make_async_copy(solved.at[q], fine_out.at[q], out_sems.at[q]).wait()


def schwarz(residual, middle, scale, fine_eigen, middle_eigen, halos, tables):
    vmem = pl.BlockSpec(memory_space=pltpu.VMEM)
    smem = pl.BlockSpec(memory_space=pltpu.SMEM)
    hbm = pl.BlockSpec(memory_space=pltpu.HBM)
    face = jax.ShapeDtypeStruct((FACE_ROWS, LANES), F32)

    def scratch(level, *group):
        return [
            pltpu.VMEM((EY, level.planes, level.core, LANES), F32),
            pltpu.VMEM((EY, EX * level.n, level.rim, LANES), F32),
            pltpu.VMEM((4, EX * level.core, LANES), F32),
            pltpu.VMEM(group + (level.wide, 2 * level.depth, 2 * LANES), BF16),
            pltpu.VMEM(group + (level.wide, level.core, 2 * LANES), F32),
        ]

    return pl.pallas_call(
        schwarz_kernel,
        out_shape=[
            jax.ShapeDtypeStruct((8, 2, 8, 64, LANES), F32),
            jax.ShapeDtypeStruct((8, 2, 4, 16, LANES), F32),
        ]
        + [face] * 4,
        in_specs=[hbm, vmem, vmem, smem, smem] + [vmem] * 12 + [smem] * 2,
        out_specs=[hbm] + [vmem] * 5,
        scratch_shapes=scratch(FINE)
        + scratch(MID, MID_GROUP)
        + [
            pltpu.VMEM((8, 2, 8, 64, LANES), F32),
            pltpu.VMEM((FINE.wide, FINE.modes, LANES), F32),
            pltpu.VMEM((MID.wide, MID.modes, LANES), F32),
            pltpu.SemaphoreType.DMA((16,)),
            pltpu.SemaphoreType.DMA((8,)),
        ],
        compiler_params=pltpu.CompilerParams(vmem_limit_bytes=VMEM_LIMIT),
        cost_estimate=pl.CostEstimate(
            flops=10**11, bytes_accessed=12 * 10**6, transcendentals=0
        ),
        name="schwarz",
    )(residual, middle, scale, *tables[6:], *halos, *tables[:6], fine_eigen, middle_eigen)


def coarse_kernel(rows_x, gathered, table, out, held, part):
    own_x, own_y = lax.axis_index("px"), lax.axis_index("py")
    high, low = split(table[0:64])
    forward_y = jnp.concatenate([high, low], axis=0)[:, 0:80]

    def y_step(p, carry):
        slabs = []
        for lx in range(4):
            pieces = []
            for ly in range(5):
                row = p * (16 * VERTEX_ROWS) + lx * 5 + ly
                pieces.append(gathered[pl.ds(row, 16, stride=VERTEX_ROWS), :])
            slabs.append(jnp.concatenate(pieces, axis=0))
        for half in (0, 2):
            high, low = split(jnp.concatenate([slabs[half], slabs[half + 1]], axis=1))
            both = dot(forward_y, high)
            total = both[0:64] + both[64:128] + dot(forward_y[0:64], low)
            held[4 * p + half] = total[:, 0:LANES]
            held[4 * p + half + 1] = total[:, LANES : 2 * LANES]
        return carry

    lax.fori_loop(0, 8, y_step, 0, unroll=4)
    angle = 2.0 * np.pi / 32
    eigen_x = line_eigen(32)

    def x_step(chunk, carry):
        rows = pl.ds(pl.multiple_of(chunk * 8, 8), 8)
        values = [held[x, rows, :] for x in range(32)]
        even = [values[0]] + [values[x] + values[32 - x] for x in range(1, 16)] + [values[16]]
        odd = [None] + [values[x] - values[32 - x] for x in range(1, 16)]
        base = table[pl.ds(pl.multiple_of(64 + chunk * 8, 8), 8), :]
        totals = [None] * 5
        for k in range(17):
            cosine = even[0]
            for x in range(1, 17):
                cosine = cosine + float(np.cos(angle * (k * x % 32))) * even[x]
            modes = [(k, cosine)]
            if 0 < k < 16:
                sine = float(np.sin(angle * k)) * odd[1]
                for x in range(2, 16):
                    sine = sine + float(np.sin(angle * (k * x % 32))) * odd[x]
                modes = [(k, cosine + sine), (32 - k, cosine - sine)]
            damp = 1.0 / (base + float(24.0 * eigen_x[k]))
            for kx, value in modes:
                value = value * damp
                for lx in range(5):
                    term = rows_x[lax.rem(own_x * 4 + lx, 32), kx] * value
                    totals[lx] = term if totals[lx] is None else totals[lx] + term
        for lx in range(5):
            part[lx, rows, :] = totals[lx]
        return carry

    lax.fori_loop(0, 8, x_step, 0)
    own_rows = table[pl.ds(pl.multiple_of(256 + own_y * 8, 8), 8), :][:, 0:64]
    solved = jnp.concatenate([exact_dot(own_rows, part[lx]) for lx in range(5)], axis=0)
    out[...] = exact_dot(solved, table[128:256]) * (1.0 / (32 * 64 * 128))


def coarse_table():
    table_y = hartley(64)
    out = np.zeros((384, 128), np.float32)
    for q in range(16):
        for ly in range(5):
            out[0:64, ly * 16 + q] = table_y[:, (4 * q + ly) % 64]
            out[256 + 8 * q + ly, 0:64] = table_y[(4 * q + ly) % 64]
    out[64:128] = 24.0 * (line_eigen(64)[:, None] + line_eigen(128)[None, :]) + 0.5
    out[128:256] = hartley(128)
    return out


def coarse(gathered):
    vmem = pl.BlockSpec(memory_space=pltpu.VMEM)
    smem = pl.BlockSpec(memory_space=pltpu.SMEM)
    return pl.pallas_call(
        coarse_kernel,
        out_shape=jax.ShapeDtypeStruct((40, LANES), F32),
        in_specs=[smem, vmem, vmem],
        out_specs=vmem,
        scratch_shapes=[
            pltpu.VMEM((32, 64, LANES), F32),
            pltpu.VMEM((5, 64, LANES), F32),
        ],
        compiler_params=pltpu.CompilerParams(vmem_limit_bytes=16 * MIB),
        cost_estimate=pl.CostEstimate(
            flops=2 * 10**9, bytes_accessed=4 * 10**6, transcendentals=0
        ),
        name="coarse",
    )(jnp.asarray(hartley(32), F32), gathered, jnp.asarray(coarse_table()))


def average_faces(level, field, sides, x_low, x_high, y_low, y_high, edges):
    n, core = level.n, level.core
    base = 0 if n == 8 else 256

    def at(ex, ey):
        return 2 * ex + ey // 2, ey % 2

    for ey in range(EY):
        row = base + ey * core
        q, h = at(0, ey)
        field[q, h, 0] = 0.5 * (field[q, h, 0] + x_low[row : row + core])
        q, h = at(EX - 1, ey)
        field[q, h, n - 1] = 0.5 * (field[q, h, n - 1] + x_high[row : row + core])
        for ex in range(EX - 1):
            q, h = at(ex, ey)
            total = 0.5 * (field[q, h, n - 1] + field[q + 2, h, 0])
            field[q, h, n - 1] = total
            field[q + 2, h, 0] = total
    for side, halo in ((0, y_low), (1, y_high)):
        sides[side] = halo[base : base + EX * core]
        row = edge_face_row(n, 0)
        sides[side, 0:n] = 0.5 * (sides[side, 0:n] + edges[side][row : row + n])
        row, end = edge_face_row(n, 1), EX * core
        sides[side, end - n : end] = 0.5 * (sides[side, end - n : end] + edges[side][row : row + n])
    for ex in range(EX):
        for a in range(n):
            row = (ex * n + a) * n
            q, h = at(ex, 0)
            field[q, h, a, 0:n] = 0.5 * (field[q, h, a, 0:n] + sides[0, row : row + n])
            q, h = at(ex, EY - 1)
            field[q, h, a, core - n : core] = 0.5 * (
                field[q, h, a, core - n : core] + sides[1, row : row + n]
            )
            for ey in range(EY - 1):
                q, h = at(ex, ey)
                p, g = at(ex, ey + 1)
                total = 0.5 * (field[q, h, a, core - n : core] + field[p, g, a, 0:n])
                field[q, h, a, core - n : core] = total
                field[p, g, a, 0:n] = total


def finish_kernel(
    fine, middle, coarse_part, prolong, x_first, x_second, y_first, y_second, edge_first, edge_second,
    out, field, sides, field_m, sides_m, corner, result, in_sems, out_sems,
):
    copies = []
    for q in range(8):
        copy = pltpu.make_async_copy(fine.at[q], field.at[q], in_sems.at[q])
        copy.start()
        copies.append(copy)
    x_low, x_high = received("px", x_first, x_second)
    y_low, y_high = received("py", y_first, y_second)
    edges = received("py", edge_first, edge_second)
    field_m[...] = middle[...]
    average_faces(MID, field_m, sides_m, x_low, x_high, y_low, y_high, edges)
    near = coarse_part[...]
    far = pltpu.roll(near, LANES - 1, 1)
    for q in range(8):
        for h in (0, 1):
            ex, ey = q // 2, (q % 2) * 2 + h
            corner[q, h, 8:16] = jnp.zeros((8, LANES), F32)
            for i in (0, 1):
                for j in (0, 1):
                    row = (ex + i) * 8 + ey + j
                    place = i * 4 + j * 2
                    corner[q, h, place : place + 1] = near[row : row + 1]
                    corner[q, h, place + 1 : place + 2] = far[row : row + 1]
    for copy in copies:
        copy.wait()
    average_faces(FINE, field, sides, x_low, x_high, y_low, y_high, edges)

    def step(q, carry):
        for h in (0, 1):
            for a in range(4):
                sum_lines(field_m, (q, h, a), 4, 0.5)
            for a in range(8):
                sum_lines(field, (q, h, a), 8, 0.5)
        level = jnp.concatenate(
            [field_m[q, 0].reshape(64, LANES), field_m[q, 1].reshape(64, LANES)], axis=1
        )
        high, low = split(level)
        ends = jnp.concatenate([corner[q, 0], corner[q, 1]], axis=1)
        ends_high, ends_low = split(ends)
        stacked = jnp.concatenate([high, low, high, ends_high, ends_low, ends_high], axis=0)
        total = dot(prolong[...], stacked)
        for h in (0, 1):
            part = total[:, h * LANES : (h + 1) * LANES]
            result[q, h] = field[q, h] + part.reshape(8, 64, LANES)
        pltpu.make_async_copy(result.at[q], out.at[q], out_sems.at[q]).start()
        return carry

    lax.fori_loop(0, 8, step, 0, unroll=4)
    for q in range(8):
        pltpu.make_async_copy(result.at[q], out.at[q], out_sems.at[q]).wait()


def finish(fine, middle, coarse_part, halos):
    vmem = pl.BlockSpec(memory_space=pltpu.VMEM)
    hbm = pl.BlockSpec(memory_space=pl.ANY)
    return pl.pallas_call(
        finish_kernel,
        out_shape=jax.ShapeDtypeStruct((8, 2, 8, 64, LANES), F32),
        in_specs=[hbm] + [vmem] * 9,
        out_specs=hbm,
        scratch_shapes=[
            pltpu.VMEM((8, 2, 8, 64, LANES), F32),
            pltpu.VMEM((2, EX * 64, LANES), F32),
            pltpu.VMEM((8, 2, 4, 16, LANES), F32),
            pltpu.VMEM((2, EX * 16, LANES), F32),
            pltpu.VMEM((8, 2, 16, LANES), F32),
            pltpu.VMEM((8, 2, 8, 64, LANES), F32),
            pltpu.SemaphoreType.DMA((8,)),
            pltpu.SemaphoreType.DMA((8,)),
        ],
        compiler_params=pltpu.CompilerParams(vmem_limit_bytes=16 * MIB),
        cost_estimate=pl.CostEstimate(
            flops=2 * 10**9, bytes_accessed=8 * 10**6, transcendentals=0
        ),
        name="finish",
    )(fine, middle, coarse_part, jnp.asarray(prolong_matrix()), *halos)


def swap(first, second, axis):
    count = lax.axis_size(axis)
    pairs = [(i, i + 1 - 2 * (i % 2)) for i in range(count)]
    others = [(i, (i - 1 + 2 * (i % 2)) % count) for i in range(count)]
    return lax.ppermute(first, axis, pairs), lax.ppermute(second, axis, others)


def on_device(residual, scale, fine_basis, fine_eigen, middle_basis, middle_eigen):
    shape = residual.shape
    devices = lax.axis_size("px") * lax.axis_size("py")
    residual = residual.reshape(EX, EY, 8, 64, LANES)
    x_first, x_second, y_first, y_second, middle, vertex = pack(residual)
    x_halos = swap(x_first, x_second, "px")
    halos = x_halos + swap(y_first, y_second, "py")
    tables = solve_tables(fine_basis, fine_eigen, middle_basis, middle_eigen, vertex)
    edge_first, edge_second, vertex = join(x_halos, vertex, tables[7])
    halos += swap(edge_first, edge_second, "py")
    gathered = lax.all_to_all(spread(vertex, devices), ("px", "py"), 0, 0)
    gathered = gathered.reshape(devices * VERTEX_ROWS, LANES)
    fine_solved, middle_solved, x_first, x_second, y_first, y_second = schwarz(
        residual, middle, scale, fine_eigen, middle_eigen, halos, tables
    )
    x_halos = swap(x_first, x_second, "px")
    halos = x_halos + swap(y_first, y_second, "py")
    halos += swap(*join_faces(x_halos), "py")
    coarse_part = coarse(gathered)
    return finish(fine_solved, middle_solved, coarse_part, halos).reshape(shape)


def solution(mesh):
    placed = (P("px", "py", None, None, None, None), P("px", "py", None), P(), P(), P(), P())
    return jax.shard_map(
        on_device,
        mesh=mesh,
        in_specs=placed,
        out_specs=P("px", "py", None, None, None, None),
        check_vma=False,
    )
```

```python
import functools
import math

import jax
import jax.numpy as jnp
import ml_dtypes
import numpy as np
from jax import lax
from jax.experimental import pallas as pl
from jax.experimental.pallas import tpu as pltpu
from jax.sharding import PartitionSpec as P

F32, BF16 = jnp.float32, jnp.bfloat16
HIGHEST = lax.Precision.HIGHEST
LANES = 128
EX = EY = 4
MID_GROUP = 4
LAG = 5
MIB = 1024 * 1024
VMEM_LIMIT = 60 * MIB


def lobatto(count):
    return -np.cos(np.arange(count) * (np.pi / (count - 1)))


def interpolation(fine_count, coarse_count):
    fine, coarse = lobatto(fine_count), lobatto(coarse_count)
    out = np.ones((fine_count, coarse_count))
    for j in range(coarse_count):
        for m in range(coarse_count):
            if m != j:
                out[:, j] *= (fine - coarse[m]) / (coarse[j] - coarse[m])
    return out


def hartley(count):
    phase = np.outer(np.arange(count), np.arange(count)) % count
    angle = phase * (2.0 * np.pi / count)
    return np.cos(angle) + np.sin(angle)


def line_eigen(count):
    return 2.0 - 2.0 * np.cos(np.arange(count) * (2.0 * np.pi / count))


def split_np(values):
    values = np.asarray(values, np.float32)
    high = values.astype(ml_dtypes.bfloat16)
    low = (values - high.astype(np.float32)).astype(ml_dtypes.bfloat16)
    return high, low


def split(values):
    high = values.astype(BF16)
    return high, (values - high.astype(F32)).astype(BF16)


def dot(left, right):
    return jnp.dot(left, right, preferred_element_type=F32)


def exact_dot(left, right, contract=((1,), (0,))):
    return lax.dot_general(
        left, right, (contract, ((), ())), precision=HIGHEST, preferred_element_type=F32
    )


INTERP_FINE = interpolation(8, 4)
INTERP_MID = interpolation(4, 2)
INTERP_ALL = INTERP_FINE @ INTERP_MID


def kron3(m):
    return np.kron(np.kron(m, m), m)


def restrict_matrix():
    rows = np.zeros((80, 512))
    rows[:64] = kron3(INTERP_FINE).T
    rows[64:72] = kron3(INTERP_ALL).T
    high, low = split_np(rows)
    return np.concatenate([high, low], axis=0)


def prolong_matrix():
    fine = kron3(INTERP_FINE)
    coarse = np.zeros((512, 16))
    coarse[:, :8] = kron3(INTERP_ALL)
    fine_high, fine_low = split_np(fine)
    coarse_high, coarse_low = split_np(coarse)
    return np.concatenate(
        [fine_high, fine_high, fine_low, coarse_high, coarse_high, coarse_low], axis=1
    )


def vertex_matrices():
    out = np.zeros((2, 32, 128), np.float32)
    for ex in range(EX):
        for ey in range(EY):
            for i in (0, 1):
                for j in (0, 1):
                    for k in (0, 1):
                        column = (ex * EY + ey) * 8 + i * 4 + j * 2 + k
                        out[k, (ex + i) * 5 + ey + j, column] = 1.0
    return out


class Level:
    def __init__(self, n):
        self.n = n
        self.wide = n + 2
        self.core = n * n
        self.rim = 4 * n
        self.depth = self.core + self.rim
        self.modes = -(-(self.wide * self.wide) // 16) * 16
        self.planes = EX * n + 4

    def tables(self):
        n, wide = self.n, self.wide
        first = np.zeros((2 * self.modes, wide), np.float32)
        second = np.zeros((2 * self.modes, wide), np.float32)
        for half in (0, 1):
            for j in range(wide):
                for k in range(wide):
                    first[half * self.modes + j * wide + k, j] = 1.0
                    second[half * self.modes + j * wide + k, k] = 1.0
        inner = list(range(1, n + 1))
        points = [(b, c) for b in inner for c in inner]
        points += [(0, c) for c in inner] + [(n + 1, c) for c in inner]
        points += [(b, 0) for b in inner] + [(b, n + 1) for b in inner]
        pick_b = np.zeros((wide, 2 * self.depth), np.float32)
        pick_c = np.zeros((wide, 2 * self.depth), np.float32)
        for half in (0, 1):
            for column, (b, c) in enumerate(points):
                pick_b[b, half * self.depth + column] = 1.0
                pick_c[c, half * self.depth + column] = 1.0
        return (
            first,
            second,
            pick_b,
            pick_c,
            np.ascontiguousarray(pick_b[:, : self.core].T),
            np.ascontiguousarray(pick_c[:, : self.core].T),
        )


FINE, MID = Level(8), Level(4)

LAYER_ROWS = 640
X_ROWS = 648
FACE_ROWS = 320
VERTEX_ROWS = 24
EDGE_ROWS = 72
EDGE_FACE_ROWS = 24


def edge_row(n, side, kind):
    return (0 if n == 8 else 48) + (side * 3 + kind) * n


def edge_face_row(n, side):
    return (0 if n == 8 else 16) + side * n


class Either:
    def __init__(self, flag, yes, no):
        self.flag, self.yes, self.no = flag, yes, no

    def __getitem__(self, index):
        return jnp.where(self.flag, self.yes[index], self.no[index])


def is_even(axis):
    return lax.rem(lax.axis_index(axis), 2) == 0


def received(axis, first, second):
    flag = is_even(axis)
    return Either(flag, second, first), Either(flag, first, second)


def for_partners(axis, first, second, write):
    @pl.when(is_even(axis))
    def _():
        write(first, second)

    @pl.when(jnp.logical_not(is_even(axis)))
    def _():
        write(second, first)


def pack_kernel(
    residual,
    restrict_in,
    vertex_pick_in,
    hartley_in,
    x_first,
    x_second,
    y_first,
    y_second,
    middle,
    vertex,
    field,
    corners,
    restrict,
    vertex_pick,
    hartley_z,
    sems,
):
    moves = [(restrict_in, restrict)]
    moves += [(residual.at[ex], field.at[ex]) for ex in range(EX)]
    moves += [(vertex_pick_in, vertex_pick), (hartley_in, hartley_z)]
    copies = []
    for place, (source, target) in enumerate(moves):
        copies.append(pltpu.make_async_copy(source, target, sems.at[place]))
        copies[-1].start()
    copies[0].wait()
    for ex in range(EX):
        copies[1 + ex].wait()
        for pair in range(EY // 2):
            ey = 2 * pair
            values = jnp.concatenate(
                [field[ex, ey].reshape(512, LANES), field[ex, ey + 1].reshape(512, LANES)], axis=1
            )
            high, low = split(values)
            upper = dot(restrict[...], high)
            lower = dot(restrict[0:80, :], low)
            total = upper[0:80] + upper[80:160] + lower
            for h in (0, 1):
                part = total[:, h * LANES : (h + 1) * LANES]
                for i in range(4):
                    middle[ex, ey + h, i] = part[16 * i : 16 * i + 16]
                column = ex * EY + ey + h
                corners[8 * column : 8 * column + 8] = part[64:72]
    copies[EX + 1].wait()
    copies[EX + 2].wait()
    values = corners[...]
    near = exact_dot(vertex_pick[0], values)
    far = exact_dot(vertex_pick[1], values)
    total = exact_dot(near + pltpu.roll(far, 1, 1), hartley_z[...])
    vertex[...] = total

    def write_x(x_up, x_down):
        for out, ex, nodes, mids in ((x_up, EX - 1, (7, 6), (3, 2)), (x_down, 0, (0, 1), (0, 1))):
            for layer in (0, 1):
                for ey in range(EY):
                    row = (layer * EY + ey) * 64
                    out[row : row + 64] = field[ex, ey, nodes[layer]]
                    row = 512 + (layer * EY + ey) * 16
                    out[row : row + 16] = middle[ex, ey, mids[layer]]
        x_up[LAYER_ROWS:X_ROWS] = vertex[20:28]
        x_down[LAYER_ROWS:X_ROWS] = jnp.zeros((8, LANES), F32)

    for_partners("px", x_first, x_second, write_x)
    def write_y(y_up, y_down):
        for out, ey, nodes, mids in ((y_up, EY - 1, (7, 6), (3, 2)), (y_down, 0, (0, 1), (0, 1))):
            for layer in (0, 1):
                for ex in range(EX):
                    for a in range(8):
                        row = (layer * EX + ex) * 64 + a * 8
                        line = nodes[layer] * 8
                        out[row : row + 8] = field[ex, ey, a, line : line + 8]
                    for a in range(4):
                        row = 512 + (layer * EX + ex) * 16 + a * 4
                        line = mids[layer] * 4
                        out[row : row + 4] = middle[ex, ey, a, line : line + 4]
            for n, base in ((8, 0), (4, 512)):
                core = n * n
                for row in [base + k * core for k in (1, 2, 3, 5, 6, 7)]:
                    total = out[row - n : row] + out[row : row + n]
                    out[row - n : row] = total
                    out[row : row + n] = total

    for_partners("py", y_first, y_second, write_y)


def pack(residual):
    x_halo = jax.ShapeDtypeStruct((X_ROWS, LANES), F32)
    y_halo = jax.ShapeDtypeStruct((LAYER_ROWS, LANES), F32)
    vmem = pl.BlockSpec(memory_space=pltpu.VMEM)
    return pl.pallas_call(
        pack_kernel,
        out_shape=[x_halo] * 2
        + [y_halo] * 2
        + [
            jax.ShapeDtypeStruct((EX, EY, 4, 16, LANES), F32),
            jax.ShapeDtypeStruct((32, LANES), F32),
        ],
        in_specs=[pl.BlockSpec(memory_space=pltpu.HBM)] * 4,
        out_specs=[vmem] * 6,
        scratch_shapes=[
            pltpu.VMEM((EX, EY, 8, 64, LANES), F32),
            pltpu.VMEM((128, LANES), F32),
            pltpu.VMEM((160, 512), BF16),
            pltpu.VMEM((2, 32, 128), F32),
            pltpu.VMEM((128, 128), F32),
            pltpu.SemaphoreType.DMA((EX + 3,)),
        ],
        compiler_params=pltpu.CompilerParams(vmem_limit_bytes=VMEM_LIMIT),
        cost_estimate=pl.CostEstimate(flops=10**9, bytes_accessed=8 * 10**6, transcendentals=0),
        name="pack",
    )(
        residual,
        jnp.asarray(restrict_matrix()),
        jnp.asarray(vertex_matrices()),
        jnp.asarray(hartley(128), F32),
    )


def join_kernel(x_first, x_second, vertex, after, first, second, summed):
    del after
    x_low, x_high = received("px", x_first, x_second)

    def write(up, down):
        for out, ey, ends in ((up, EY - 1, True), (down, 0, False)):
            for n, base in ((8, 0), (4, 512)):
                face, inner = (n - 1, n - 2) if ends else (0, 1)
                for kind, (layer, node) in enumerate(((0, face), (0, inner), (1, face))):
                    line = base + (layer * EY + ey) * n * n + node * n
                    for side, halo in ((0, x_low), (1, x_high)):
                        row = edge_row(n, side, kind)
                        out[row : row + n] = halo[line : line + n]

    for_partners("py", first, second, write)
    total = vertex[0:8] + jnp.concatenate(
        [x_low[LAYER_ROWS : LAYER_ROWS + 5], jnp.zeros((3, LANES), F32)], axis=0
    )
    last = jnp.concatenate([vertex[16:20], jnp.zeros((4, LANES), F32)], axis=0)
    total = jnp.concatenate([total, vertex[8:16], last], axis=0)
    summed[...] = jnp.broadcast_to(total[None], summed.shape)


def join(x_halos, vertex, after, devices):
    vmem = pl.BlockSpec(memory_space=pltpu.VMEM)
    edge = jax.ShapeDtypeStruct((EDGE_ROWS, LANES), F32)
    return pl.pallas_call(
        join_kernel,
        out_shape=[edge, edge, jax.ShapeDtypeStruct((devices, VERTEX_ROWS, LANES), F32)],
        in_specs=[vmem] * 3 + [pl.BlockSpec(memory_space=pl.ANY)],
        out_specs=[vmem] * 3,
        compiler_params=pltpu.CompilerParams(vmem_limit_bytes=8 * MIB),
        cost_estimate=pl.CostEstimate(flops=10**6, bytes_accessed=10**6, transcendentals=0),
        name="join",
    )(*x_halos, vertex, after)


def join_faces_kernel(x_first, x_second, first, second):
    x_low, x_high = received("px", x_first, x_second)

    def write(up, down):
        for out, ey, ends in ((up, EY - 1, True), (down, 0, False)):
            for n, base in ((8, 0), (4, 256)):
                core = n * n
                line = base + ey * core + (core - n if ends else 0)
                for side, halo in ((0, x_low), (1, x_high)):
                    row = edge_face_row(n, side)
                    out[row : row + n] = halo[line : line + n]

    for_partners("py", first, second, write)


def join_faces(x_halos):
    vmem = pl.BlockSpec(memory_space=pltpu.VMEM)
    edge = jax.ShapeDtypeStruct((EDGE_FACE_ROWS, LANES), F32)
    return pl.pallas_call(
        join_faces_kernel,
        out_shape=[edge, edge],
        in_specs=[vmem] * 2,
        out_specs=[vmem] * 2,
        compiler_params=pltpu.CompilerParams(vmem_limit_bytes=8 * MIB),
        cost_estimate=pl.CostEstimate(flops=10**6, bytes_accessed=10**6, transcendentals=0),
        name="join_faces",
    )(*x_halos)


def sum_lines(ref, lead, n, scale=None):
    count = ref.shape[-2] // n
    low_rows = lead + (pl.ds(0, count, stride=n), slice(None))
    high_rows = lead + (pl.ds(n - 1, count, stride=n), slice(None))
    low, high = ref[low_rows], ref[high_rows]
    new_low = low + pltpu.roll(high, 1, 1)
    new_high = high + pltpu.roll(low, LANES - 1, 1)
    if scale is not None:
        new_low, new_high = new_low * scale, new_high * scale
    ref[low_rows] = new_low
    ref[high_rows] = new_high


def assemble(level, planes, rims, sides, x_low, x_high, y_low, y_high, edges):
    n, core = level.n, level.core
    last = EX * n + 3
    base = 0 if n == 8 else 512
    for ey in range(EY):
        row = base + ey * core
        planes[ey, 2] += x_low[row : row + core]
        planes[ey, last - 2] += x_high[row : row + core]
        for ex in range(EX - 1):
            left = 2 + ex * n + n - 1
            total = planes[ey, left] + planes[ey, left + 1]
            planes[ey, left] = total
            planes[ey, left + 1] = total
        row = base + (EY + ey) * core
        planes[ey, 0] = x_low[row : row + core]
        planes[ey, last] = x_high[row : row + core]
    for side, halo in ((0, y_low), (1, y_high)):
        for layer in (0, 1):
            kind = 2 * side + layer
            start = base + layer * EX * core
            sides[kind] = halo[start : start + EX * core]
            row = edge_row(n, 0, layer)
            sides[kind, 0:n] += edges[side][row : row + n]
            row = edge_row(n, 1, layer)
            sides[kind, EX * core - n : EX * core] += edges[side][row : row + n]
    for plane in range(EX * n):
        row = plane * n
        planes[0, 2 + plane, 0:n] += sides[0, row : row + n]
        planes[EY - 1, 2 + plane, core - n : core] += sides[2, row : row + n]
    for side, plane in ((0, 0), (1, last)):
        row = edge_row(n, side, 2)
        planes[0, plane, 0:n] += edges[0][row : row + n]
        planes[EY - 1, plane, core - n : core] += edges[1][row : row + n]
    for ey in range(EY - 1):
        for plane in [0, last] + list(range(2, 2 + EX * n)):
            total = planes[ey, plane, core - n : core] + planes[ey + 1, plane, 0:n]
            planes[ey, plane, core - n : core] = total
            planes[ey + 1, plane, 0:n] = total
    for ey in range(EY):
        for plane in [0, last] + list(range(2, 2 + EX * n)):
            sum_lines(planes, (ey, plane), n)
    for kind in (1, 3):
        sum_lines(sides, (kind,), n)
    for ey in range(EY):
        for plane in range(EX * n):
            at = 2 + plane
            row = plane * n
            low = planes[ey - 1, at, core - 2 * n : core - n] if ey else sides[1, row : row + n]
            high = planes[ey + 1, at, n : 2 * n] if ey < EY - 1 else sides[3, row : row + n]
            rims[ey, plane, 0:n] = low
            rims[ey, plane, n : 2 * n] = high
            rims[ey, plane, 2 * n : 3 * n] = pltpu.roll(
                planes[ey, at, pl.ds(n - 2, n, stride=n), :], 1, 1
            )
            rims[ey, plane, 3 * n : 4 * n] = pltpu.roll(
                planes[ey, at, pl.ds(1, n, stride=n), :], LANES - 1, 1
            )


def build_tables(level, tables, basis, eigen, forward, backward, lines_out):
    first, second, pick_b, pick_c, core_b, core_c = tables
    modes, depth = level.modes, level.depth
    rows_b = exact_dot(first[0:modes], basis[1], ((1,), (1,)))
    rows_c = exact_dot(second[0:modes], basis[2], ((1,), (1,)))
    matrix = exact_dot(rows_b, pick_b[...]) * exact_dot(rows_c, pick_c[...])
    high, low = split(matrix)
    keep = lax.broadcasted_iota(jnp.int32, matrix.shape, 1) < depth
    forward[0:modes] = high
    forward[modes : 2 * modes] = jnp.where(keep, low.astype(F32), 0.0).astype(BF16)
    out_b = exact_dot(exact_dot(core_b[...], basis[1]), first[...], ((1,), (1,)))
    out_c = exact_dot(exact_dot(core_c[...], basis[2]), second[...], ((1,), (1,)))
    matrix = out_b * out_c
    high, low = split(matrix)
    keep = lax.broadcasted_iota(jnp.int32, matrix.shape, 1) < modes
    backward[0 : level.core] = high
    backward[level.core : 2 * level.core] = jnp.where(keep, low.astype(F32), 0.0).astype(BF16)
    wide = level.wide
    spread_b = jnp.broadcast_to(eigen[1:2, :], (LANES, wide))
    spread_c = jnp.broadcast_to(eigen[2:3, :], (LANES, wide))
    lines = exact_dot(first[0:modes], spread_b, ((1,), (1,)))
    lines += exact_dot(second[0:modes], spread_c, ((1,), (1,)))
    lines_out[...] = lines


def first_steps(level, q, planes, rims, coeff, spectrum):
    n, wide, core, depth = level.n, level.wide, level.core, level.depth
    offsets = [0] + [2 + a for a in range(n)] + [n + 3]
    base, ey = q // 2 * n, q % 2 * 2

    def contract(load, nodes, row):
        held = [[load(h, e) for h in (0, 1)] for e in nodes]
        for i in range(wide):
            for h in (0, 1):
                total = coeff[nodes[0], i] * held[0][h]
                for position in range(1, len(nodes)):
                    total += coeff[nodes[position], i] * held[position][h]
                high, low = split(total)
                lanes = slice(h * LANES, (h + 1) * LANES)
                spectrum[i, row : row + 16, lanes] = high
                spectrum[i, depth + row : depth + row + 16, lanes] = low

    def inner(row):
        load = lambda h, e: planes[ey + h, base + offsets[e], row : row + 16]
        contract(load, list(range(wide)), row)

    def outer(row):
        load = lambda h, e: rims[ey + h, base + e - 1, row : row + 16]
        contract(load, list(range(1, n + 1)), core + row)

    steps = [functools.partial(inner, row) for row in range(0, core, 16)]
    return steps + [functools.partial(outer, row) for row in range(0, level.rim, 16)]


def last_steps(level, q, hats, coeff, scale, out):
    n, wide, core = level.n, level.wide, level.core
    ex, ey = q // 2, q % 2 * 2

    def back(h, row):
        inv = 1.0 / scale[ex, pl.ds(ey + h, 1), :]
        lanes = slice(h * LANES, (h + 1) * LANES)
        held = [hats[i, row : row + 16, lanes] for i in range(wide)]
        for a in range(n):
            total = coeff[a + 1, 0] * held[0]
            for i in range(1, wide):
                total += coeff[a + 1, i] * held[i]
            out[q, h, a, row : row + 16] = total * inv

    return [functools.partial(back, h, row) for h in (0, 1) for row in range(0, core, 16)]


def products(level, slots, forward, backward, inverse, lag):
    core, modes = level.core, level.modes
    waiting = []
    steps = [(spectrum, hats, i) for spectrum, hats in slots for i in range(level.wide)]
    for step in range(len(steps) + lag):
        if step < len(steps):
            spectrum, _, i = steps[step]
            both = dot(forward[...], spectrum[i])
            damp = inverse[i]
            hat = (both[0:modes] + both[modes : 2 * modes]) * jnp.concatenate([damp, damp], axis=1)
            waiting.append(jnp.concatenate(split(hat), axis=0))
        if step >= lag:
            _, hats, i = steps[step - lag]
            both = dot(backward[...], waiting[step - lag])
            hats[i] = both[0:core] + both[core : 2 * core]


def tables_kernel(
    fine_basis, fine_eigen, middle_basis, middle_eigen, after, *refs
):
    del after
    fine_in, middle_in, outs = refs[:6], refs[6:12], refs[12:]
    build_tables(FINE, fine_in, fine_basis, fine_eigen, *outs[:3])
    build_tables(MID, middle_in, middle_basis, middle_eigen, *outs[3:6])
    outs[6][...] = fine_basis[0]
    outs[7][...] = middle_basis[0]


def solve_tables(fine_basis, fine_eigen, middle_basis, middle_eigen, after):
    vmem = pl.BlockSpec(memory_space=pltpu.VMEM)
    shapes = []
    for level in (FINE, MID):
        shapes += [
            jax.ShapeDtypeStruct((2 * level.modes, 2 * level.depth), BF16),
            jax.ShapeDtypeStruct((2 * level.core, 2 * level.modes), BF16),
            jax.ShapeDtypeStruct((level.modes, LANES), F32),
        ]
    shapes += [jax.ShapeDtypeStruct((level.wide, level.wide), F32) for level in (FINE, MID)]
    return pl.pallas_call(
        tables_kernel,
        out_shape=shapes,
        in_specs=[vmem] * 4 + [pl.BlockSpec(memory_space=pl.ANY)] + [vmem] * 12,
        out_specs=[vmem] * 8,
        compiler_params=pltpu.CompilerParams(vmem_limit_bytes=VMEM_LIMIT),
        cost_estimate=pl.CostEstimate(flops=10**8, bytes_accessed=10**6, transcendentals=0),
        name="tables",
    )(
        fine_basis, fine_eigen, middle_basis, middle_eigen, after,
        *[jnp.asarray(t) for level in (FINE, MID) for t in level.tables()],
    )


def schwarz_kernel(
    residual,
    middle,
    scale,
    fine_coeff,
    middle_coeff,
    x_first,
    x_second,
    y_first,
    y_second,
    edge_first,
    edge_second,
    forward,
    backward,
    lines,
    forward_m,
    backward_m,
    lines_m,
    fine_eigen,
    middle_eigen,
    fine_out,
    middle_out,
    face_first,
    face_second,
    line_first,
    line_second,
    planes,
    rims,
    sides,
    spectrum,
    hats,
    planes_m,
    rims_m,
    sides_m,
    spectrum_m,
    hats_m,
    solved,
    inverse,
    inverse_m,
    in_sems,
    out_sems,
):
    x_low, x_high = received("px", x_first, x_second)
    y_low, y_high = received("py", y_first, y_second)
    edges = received("py", edge_first, edge_second)
    copies = []
    for ex in range(EX):
        for ey in range(EY):
            copy = pltpu.make_async_copy(
                residual.at[ex, ey], planes.at[ey, pl.ds(2 + 8 * ex, 8)], in_sems.at[ex * EY + ey]
            )
            copy.start()
            copies.append(copy)
    for ex in range(EX):
        for ey in range(EY):
            planes_m[ey, 2 + 4 * ex : 6 + 4 * ex] = middle[ex, ey]
    assemble(MID, planes_m, rims_m, sides_m, x_low, x_high, y_low, y_high, edges)

    for level, inverse_out, lines_in, eigen in (
        (FINE, inverse, lines, fine_eigen),
        (MID, inverse_m, lines_m, middle_eigen),
    ):
        for i in range(level.wide):
            inverse_out[i] = 1.0 / (lines_in[...] + eigen[0, i])

    def middle_step(step, carry):
        pairs = [MID_GROUP * step + k for k in range(MID_GROUP)]
        for k, q in enumerate(pairs):
            for run in first_steps(MID, q, planes_m, rims_m, middle_coeff, spectrum_m.at[k]):
                run()
        slots = [(spectrum_m.at[k], hats_m.at[k]) for k in range(MID_GROUP)]
        products(MID, slots, forward_m, backward_m, inverse_m, LAG)
        for k, q in enumerate(pairs):
            for run in last_steps(MID, q, hats_m.at[k], middle_coeff, scale, middle_out):
                run()
        return carry

    lax.fori_loop(0, 8 // MID_GROUP, middle_step, 0)
    for copy in copies:
        copy.wait()
    assemble(FINE, planes, rims, sides, x_low, x_high, y_low, y_high, edges)

    def fine_step(q, carry):
        for run in first_steps(FINE, q, planes, rims, fine_coeff, spectrum):
            run()
        products(FINE, [(spectrum, hats)], forward, backward, inverse, LAG)
        for run in last_steps(FINE, q, hats, fine_coeff, scale, solved):
            run()
        pltpu.make_async_copy(solved.at[q], fine_out.at[q], out_sems.at[q]).start()
        return carry

    lax.fori_loop(0, 8, fine_step, 0)

    def write_x(x_up, x_down):
        for n, source, base in ((8, solved, 0), (4, middle_out, 256)):
            for out, ex, node in ((x_up, EX - 1, n - 1), (x_down, 0, 0)):
                for ey in range(EY):
                    row = base + ey * n * n
                    out[row : row + n * n] = source[2 * ex + ey // 2, ey % 2, node]

    for_partners("px", face_first, face_second, write_x)

    def write_y(y_up, y_down):
        for n, source, base in ((8, solved, 0), (4, middle_out, 256)):
            core = n * n
            for out, ey, node in ((y_up, EY - 1, n - 1), (y_down, 0, 0)):
                for ex in range(EX):
                    for a in range(n):
                        row = base + (ex * n + a) * n
                        out[row : row + n] = source[
                            2 * ex + ey // 2, ey % 2, a, node * n : node * n + n
                        ]
                for ex in range(1, EX):
                    row = base + ex * core
                    total = 0.5 * (out[row - n : row] + out[row : row + n])
                    out[row - n : row] = total
                    out[row : row + n] = total

    for_partners("py", line_first, line_second, write_y)
    for q in range(8):
        pltpu.make_async_copy(solved.at[q], fine_out.at[q], out_sems.at[q]).wait()


def schwarz(residual, middle, scale, fine_eigen, middle_eigen, halos, tables):
    vmem = pl.BlockSpec(memory_space=pltpu.VMEM)
    smem = pl.BlockSpec(memory_space=pltpu.SMEM)
    hbm = pl.BlockSpec(memory_space=pltpu.HBM)
    face = jax.ShapeDtypeStruct((FACE_ROWS, LANES), F32)

    def scratch(level, *group):
        return [
            pltpu.VMEM((EY, level.planes, level.core, LANES), F32),
            pltpu.VMEM((EY, EX * level.n, level.rim, LANES), F32),
            pltpu.VMEM((4, EX * level.core, LANES), F32),
            pltpu.VMEM(group + (level.wide, 2 * level.depth, 2 * LANES), BF16),
            pltpu.VMEM(group + (level.wide, level.core, 2 * LANES), F32),
        ]

    return pl.pallas_call(
        schwarz_kernel,
        out_shape=[
            jax.ShapeDtypeStruct((8, 2, 8, 64, LANES), F32),
            jax.ShapeDtypeStruct((8, 2, 4, 16, LANES), F32),
        ]
        + [face] * 4,
        in_specs=[hbm, vmem, vmem, smem, smem] + [vmem] * 12 + [smem] * 2,
        out_specs=[hbm] + [vmem] * 5,
        scratch_shapes=scratch(FINE)
        + scratch(MID, MID_GROUP)
        + [
            pltpu.VMEM((8, 2, 8, 64, LANES), F32),
            pltpu.VMEM((FINE.wide, FINE.modes, LANES), F32),
            pltpu.VMEM((MID.wide, MID.modes, LANES), F32),
            pltpu.SemaphoreType.DMA((16,)),
            pltpu.SemaphoreType.DMA((8,)),
        ],
        compiler_params=pltpu.CompilerParams(vmem_limit_bytes=VMEM_LIMIT),
        cost_estimate=pl.CostEstimate(
            flops=10**11, bytes_accessed=12 * 10**6, transcendentals=0
        ),
        name="schwarz",
    )(residual, middle, scale, *tables[6:], *halos, *tables[:6], fine_eigen, middle_eigen)


def coarse_kernel(rows_x, gathered, table, out, held, part):
    own_x, own_y = lax.axis_index("px"), lax.axis_index("py")
    high, low = split(table[0:64])
    forward_y = jnp.concatenate([high, low], axis=0)[:, 0:80]

    def y_step(p, carry):
        slabs = []
        for lx in range(4):
            pieces = []
            for ly in range(5):
                row = p * (16 * VERTEX_ROWS) + lx * 5 + ly
                pieces.append(gathered[pl.ds(row, 16, stride=VERTEX_ROWS), :])
            slabs.append(jnp.concatenate(pieces, axis=0))
        for half in (0, 2):
            high, low = split(jnp.concatenate([slabs[half], slabs[half + 1]], axis=1))
            both = dot(forward_y, high)
            total = both[0:64] + both[64:128] + dot(forward_y[0:64], low)
            held[4 * p + half] = total[:, 0:LANES]
            held[4 * p + half + 1] = total[:, LANES : 2 * LANES]
        return carry

    lax.fori_loop(0, 8, y_step, 0, unroll=4)
    angle = 2.0 * np.pi / 32
    eigen_x = line_eigen(32)

    def x_step(chunk, carry):
        rows = pl.ds(pl.multiple_of(chunk * 8, 8), 8)
        values = [held[x, rows, :] for x in range(32)]
        even = [values[0]] + [values[x] + values[32 - x] for x in range(1, 16)] + [values[16]]
        odd = [None] + [values[x] - values[32 - x] for x in range(1, 16)]
        base = table[pl.ds(pl.multiple_of(64 + chunk * 8, 8), 8), :]
        totals = [None] * 5

        def series(wave, terms, k, start):
            total = None
            for x in range(start, len(terms), 2):
                value = float(wave(angle * (k * x % 32))) * terms[x]
                total = value if total is None else total + value
            return total

        def add(k, cosine, sine):
            damp = 1.0 / (base + float(24.0 * eigen_x[k]))
            modes = [(k, cosine)]
            if sine is not None:
                modes = [(k, cosine + sine), (32 - k, cosine - sine)]
            for kx, value in modes:
                value = value * damp
                for lx in range(5):
                    term = rows_x[lax.rem(own_x * 4 + lx, 32), kx] * value
                    totals[lx] = term if totals[lx] is None else totals[lx] + term

        for k in range(9):
            cos_a, cos_b = series(np.cos, even, k, 0), series(np.cos, even, k, 1)
            sin_a = sin_b = None
            if k > 0:
                sin_a, sin_b = series(np.sin, odd, k, 2), series(np.sin, odd, k, 1)
            add(k, cos_a + cos_b, None if k == 0 else sin_a + sin_b)
            if k < 8:
                add(16 - k, cos_a - cos_b, None if k == 0 else sin_b - sin_a)
        for lx in range(5):
            part[lx, rows, :] = totals[lx]
        return carry

    lax.fori_loop(0, 8, x_step, 0)
    own_rows = table[pl.ds(pl.multiple_of(256 + own_y * 8, 8), 8), :][:, 0:64]
    solved = jnp.concatenate([exact_dot(own_rows, part[lx]) for lx in range(5)], axis=0)
    out[...] = exact_dot(solved, table[128:256]) * (1.0 / (32 * 64 * 128))


def coarse_table():
    table_y = hartley(64)
    out = np.zeros((384, 128), np.float32)
    for q in range(16):
        for ly in range(5):
            out[0:64, ly * 16 + q] = table_y[:, (4 * q + ly) % 64]
            out[256 + 8 * q + ly, 0:64] = table_y[(4 * q + ly) % 64]
    out[64:128] = 24.0 * (line_eigen(64)[:, None] + line_eigen(128)[None, :]) + 0.5
    out[128:256] = hartley(128)
    return out


def coarse(gathered):
    vmem = pl.BlockSpec(memory_space=pltpu.VMEM)
    smem = pl.BlockSpec(memory_space=pltpu.SMEM)
    return pl.pallas_call(
        coarse_kernel,
        out_shape=jax.ShapeDtypeStruct((40, LANES), F32),
        in_specs=[smem, vmem, vmem],
        out_specs=vmem,
        scratch_shapes=[
            pltpu.VMEM((32, 64, LANES), F32),
            pltpu.VMEM((5, 64, LANES), F32),
        ],
        compiler_params=pltpu.CompilerParams(vmem_limit_bytes=16 * MIB),
        cost_estimate=pl.CostEstimate(
            flops=2 * 10**9, bytes_accessed=4 * 10**6, transcendentals=0
        ),
        name="coarse",
    )(jnp.asarray(hartley(32), F32), gathered, jnp.asarray(coarse_table()))


def average_faces(level, field, sides, x_low, x_high, y_low, y_high, edges):
    n, core = level.n, level.core
    base = 0 if n == 8 else 256

    def at(ex, ey):
        return 2 * ex + ey // 2, ey % 2

    for ey in range(EY):
        row = base + ey * core
        q, h = at(0, ey)
        field[q, h, 0] = 0.5 * (field[q, h, 0] + x_low[row : row + core])
        q, h = at(EX - 1, ey)
        field[q, h, n - 1] = 0.5 * (field[q, h, n - 1] + x_high[row : row + core])
        for ex in range(EX - 1):
            q, h = at(ex, ey)
            total = 0.5 * (field[q, h, n - 1] + field[q + 2, h, 0])
            field[q, h, n - 1] = total
            field[q + 2, h, 0] = total
    for side, halo in ((0, y_low), (1, y_high)):
        sides[side] = halo[base : base + EX * core]
        row = edge_face_row(n, 0)
        sides[side, 0:n] = 0.5 * (sides[side, 0:n] + edges[side][row : row + n])
        row, end = edge_face_row(n, 1), EX * core
        sides[side, end - n : end] = 0.5 * (sides[side, end - n : end] + edges[side][row : row + n])
    for ex in range(EX):
        for a in range(n):
            row = (ex * n + a) * n
            q, h = at(ex, 0)
            field[q, h, a, 0:n] = 0.5 * (field[q, h, a, 0:n] + sides[0, row : row + n])
            q, h = at(ex, EY - 1)
            field[q, h, a, core - n : core] = 0.5 * (
                field[q, h, a, core - n : core] + sides[1, row : row + n]
            )
            for ey in range(EY - 1):
                q, h = at(ex, ey)
                p, g = at(ex, ey + 1)
                total = 0.5 * (field[q, h, a, core - n : core] + field[p, g, a, 0:n])
                field[q, h, a, core - n : core] = total
                field[p, g, a, 0:n] = total


def finish_kernel(
    fine, middle, coarse_part, prolong, x_first, x_second, y_first, y_second, edge_first, edge_second,
    out, field, sides, field_m, sides_m, corner, result, in_sems, out_sems,
):
    copies = []
    for q in range(8):
        copy = pltpu.make_async_copy(fine.at[q], field.at[q], in_sems.at[q])
        copy.start()
        copies.append(copy)
    x_low, x_high = received("px", x_first, x_second)
    y_low, y_high = received("py", y_first, y_second)
    edges = received("py", edge_first, edge_second)
    field_m[...] = middle[...]
    average_faces(MID, field_m, sides_m, x_low, x_high, y_low, y_high, edges)
    near = coarse_part[...]
    far = pltpu.roll(near, LANES - 1, 1)
    for q in range(8):
        for h in (0, 1):
            ex, ey = q // 2, (q % 2) * 2 + h
            corner[q, h, 8:16] = jnp.zeros((8, LANES), F32)
            for i in (0, 1):
                for j in (0, 1):
                    row = (ex + i) * 8 + ey + j
                    place = i * 4 + j * 2
                    corner[q, h, place : place + 1] = near[row : row + 1]
                    corner[q, h, place + 1 : place + 2] = far[row : row + 1]
    for copy in copies:
        copy.wait()
    average_faces(FINE, field, sides, x_low, x_high, y_low, y_high, edges)

    def step(q, carry):
        for h in (0, 1):
            for a in range(4):
                sum_lines(field_m, (q, h, a), 4, 0.5)
            for a in range(8):
                sum_lines(field, (q, h, a), 8, 0.5)
        level = jnp.concatenate(
            [field_m[q, 0].reshape(64, LANES), field_m[q, 1].reshape(64, LANES)], axis=1
        )
        high, low = split(level)
        ends = jnp.concatenate([corner[q, 0], corner[q, 1]], axis=1)
        ends_high, ends_low = split(ends)
        stacked = jnp.concatenate([high, low, high, ends_high, ends_low, ends_high], axis=0)
        total = dot(prolong[...], stacked)
        for h in (0, 1):
            part = total[:, h * LANES : (h + 1) * LANES]
            result[q, h] = field[q, h] + part.reshape(8, 64, LANES)
        pltpu.make_async_copy(result.at[q], out.at[q], out_sems.at[q]).start()
        return carry

    lax.fori_loop(0, 8, step, 0, unroll=4)
    for q in range(8):
        pltpu.make_async_copy(result.at[q], out.at[q], out_sems.at[q]).wait()


def finish(fine, middle, coarse_part, halos):
    vmem = pl.BlockSpec(memory_space=pltpu.VMEM)
    hbm = pl.BlockSpec(memory_space=pl.ANY)
    return pl.pallas_call(
        finish_kernel,
        out_shape=jax.ShapeDtypeStruct((8, 2, 8, 64, LANES), F32),
        in_specs=[hbm] + [vmem] * 9,
        out_specs=hbm,
        scratch_shapes=[
            pltpu.VMEM((8, 2, 8, 64, LANES), F32),
            pltpu.VMEM((2, EX * 64, LANES), F32),
            pltpu.VMEM((8, 2, 4, 16, LANES), F32),
            pltpu.VMEM((2, EX * 16, LANES), F32),
            pltpu.VMEM((8, 2, 16, LANES), F32),
            pltpu.VMEM((8, 2, 8, 64, LANES), F32),
            pltpu.SemaphoreType.DMA((8,)),
            pltpu.SemaphoreType.DMA((8,)),
        ],
        compiler_params=pltpu.CompilerParams(vmem_limit_bytes=16 * MIB),
        cost_estimate=pl.CostEstimate(
            flops=2 * 10**9, bytes_accessed=8 * 10**6, transcendentals=0
        ),
        name="finish",
    )(fine, middle, coarse_part, jnp.asarray(prolong_matrix()), *halos)


def swap(first, second, axis):
    count = lax.axis_size(axis)
    pairs = [(i, i + 1 - 2 * (i % 2)) for i in range(count)]
    others = [(i, (i - 1 + 2 * (i % 2)) % count) for i in range(count)]
    return lax.ppermute(first, axis, pairs), lax.ppermute(second, axis, others)


def on_device(residual, scale, fine_basis, fine_eigen, middle_basis, middle_eigen):
    shape = residual.shape
    devices = lax.axis_size("px") * lax.axis_size("py")
    residual = residual.reshape(EX, EY, 8, 64, LANES)
    x_first, x_second, y_first, y_second, middle, vertex = pack(residual)
    x_halos = swap(x_first, x_second, "px")
    halos = x_halos + swap(y_first, y_second, "py")
    tables = solve_tables(fine_basis, fine_eigen, middle_basis, middle_eigen, vertex)
    edge_first, edge_second, vertex = join(x_halos, vertex, tables[7], devices)
    halos += swap(edge_first, edge_second, "py")
    gathered = lax.all_to_all(vertex, ("px", "py"), 0, 0)
    gathered = gathered.reshape(devices * VERTEX_ROWS, LANES)
    fine_solved, middle_solved, x_first, x_second, y_first, y_second = schwarz(
        residual, middle, scale, fine_eigen, middle_eigen, halos, tables
    )
    x_halos = swap(x_first, x_second, "px")
    halos = x_halos + swap(y_first, y_second, "py")
    halos += swap(*join_faces(x_halos), "py")
    coarse_part = coarse(gathered)
    return finish(fine_solved, middle_solved, coarse_part, halos).reshape(shape)


def solution(mesh):
    placed = (P("px", "py", None, None, None, None), P("px", "py", None), P(), P(), P(), P())
    return jax.shard_map(
        on_device,
        mesh=mesh,
        in_specs=placed,
        out_specs=P("px", "py", None, None, None, None),
        check_vma=False,
    )
```

```python
import functools
import math

import jax
import jax.numpy as jnp
import ml_dtypes
import numpy as np
from jax import lax
from jax.experimental import pallas as pl
from jax.experimental.pallas import tpu as pltpu
from jax.sharding import PartitionSpec as P

F32, BF16 = jnp.float32, jnp.bfloat16
HIGHEST = lax.Precision.HIGHEST
LANES = 128
EX = EY = 4
MID_GROUP = 4
LAG = 5
MIB = 1024 * 1024
VMEM_LIMIT = 60 * MIB


def lobatto(count):
    return -np.cos(np.arange(count) * (np.pi / (count - 1)))


def interpolation(fine_count, coarse_count):
    fine, coarse = lobatto(fine_count), lobatto(coarse_count)
    out = np.ones((fine_count, coarse_count))
    for j in range(coarse_count):
        for m in range(coarse_count):
            if m != j:
                out[:, j] *= (fine - coarse[m]) / (coarse[j] - coarse[m])
    return out


def hartley(count):
    phase = np.outer(np.arange(count), np.arange(count)) % count
    angle = phase * (2.0 * np.pi / count)
    return np.cos(angle) + np.sin(angle)


def line_eigen(count):
    return 2.0 - 2.0 * np.cos(np.arange(count) * (2.0 * np.pi / count))


def split_np(values):
    values = np.asarray(values, np.float32)
    high = values.astype(ml_dtypes.bfloat16)
    low = (values - high.astype(np.float32)).astype(ml_dtypes.bfloat16)
    return high, low


def split(values):
    high = values.astype(BF16)
    return high, (values - high.astype(F32)).astype(BF16)


def dot(left, right):
    return jnp.dot(left, right, preferred_element_type=F32)


def exact_dot(left, right, contract=((1,), (0,))):
    return lax.dot_general(
        left, right, (contract, ((), ())), precision=HIGHEST, preferred_element_type=F32
    )


INTERP_FINE = interpolation(8, 4)
INTERP_MID = interpolation(4, 2)
INTERP_ALL = INTERP_FINE @ INTERP_MID


def kron3(m):
    return np.kron(np.kron(m, m), m)


def restrict_matrix():
    rows = np.zeros((80, 512))
    rows[:64] = kron3(INTERP_FINE).T
    rows[64:72] = kron3(INTERP_ALL).T
    high, low = split_np(rows)
    return np.concatenate([high, low], axis=0)


def prolong_matrix():
    fine = kron3(INTERP_FINE)
    coarse = np.zeros((512, 16))
    coarse[:, :8] = kron3(INTERP_ALL)
    fine_high, fine_low = split_np(fine)
    coarse_high, coarse_low = split_np(coarse)
    return np.concatenate(
        [fine_high, fine_high, fine_low, coarse_high, coarse_high, coarse_low], axis=1
    )


def vertex_matrices():
    out = np.zeros((2, 32, 128), np.float32)
    for ex in range(EX):
        for ey in range(EY):
            for i in (0, 1):
                for j in (0, 1):
                    for k in (0, 1):
                        column = (ex * EY + ey) * 8 + i * 4 + j * 2 + k
                        out[k, (ex + i) * 5 + ey + j, column] = 1.0
    return out


class Level:
    def __init__(self, n):
        self.n = n
        self.wide = n + 2
        self.core = n * n
        self.rim = 4 * n
        self.depth = self.core + self.rim
        self.modes = -(-(self.wide * self.wide) // 16) * 16
        self.planes = EX * n + 4

    def tables(self):
        n, wide = self.n, self.wide
        first = np.zeros((2 * self.modes, wide), np.float32)
        second = np.zeros((2 * self.modes, wide), np.float32)
        for half in (0, 1):
            for j in range(wide):
                for k in range(wide):
                    first[half * self.modes + j * wide + k, j] = 1.0
                    second[half * self.modes + j * wide + k, k] = 1.0
        inner = list(range(1, n + 1))
        points = [(b, c) for b in inner for c in inner]
        points += [(0, c) for c in inner] + [(n + 1, c) for c in inner]
        points += [(b, 0) for b in inner] + [(b, n + 1) for b in inner]
        pick_b = np.zeros((wide, 2 * self.depth), np.float32)
        pick_c = np.zeros((wide, 2 * self.depth), np.float32)
        for half in (0, 1):
            for column, (b, c) in enumerate(points):
                pick_b[b, half * self.depth + column] = 1.0
                pick_c[c, half * self.depth + column] = 1.0
        return (
            first,
            second,
            pick_b,
            pick_c,
            np.ascontiguousarray(pick_b[:, : self.core].T),
            np.ascontiguousarray(pick_c[:, : self.core].T),
        )


FINE, MID = Level(8), Level(4)

LAYER_ROWS = 640
X_ROWS = 648
FACE_ROWS = 320
VERTEX_ROWS = 24
EDGE_ROWS = 72
EDGE_FACE_ROWS = 24


def edge_row(n, side, kind):
    return (0 if n == 8 else 48) + (side * 3 + kind) * n


def edge_face_row(n, side):
    return (0 if n == 8 else 16) + side * n


class Either:
    def __init__(self, flag, yes, no):
        self.flag, self.yes, self.no = flag, yes, no

    def __getitem__(self, index):
        return jnp.where(self.flag, self.yes[index], self.no[index])


def is_even(axis):
    return lax.rem(lax.axis_index(axis), 2) == 0


def received(axis, first, second):
    flag = is_even(axis)
    return Either(flag, second, first), Either(flag, first, second)


def for_partners(axis, first, second, write):
    @pl.when(is_even(axis))
    def _():
        write(first, second)

    @pl.when(jnp.logical_not(is_even(axis)))
    def _():
        write(second, first)


def pack_kernel(
    residual,
    restrict_in,
    vertex_pick_in,
    hartley_in,
    x_first,
    x_second,
    y_first,
    y_second,
    middle,
    vertex,
    field,
    corners,
    restrict,
    vertex_pick,
    hartley_z,
    sems,
):
    moves = [(restrict_in, restrict)]
    moves += [(residual.at[ex], field.at[ex]) for ex in range(EX)]
    moves += [(vertex_pick_in, vertex_pick), (hartley_in, hartley_z)]
    copies = []
    for place, (source, target) in enumerate(moves):
        copies.append(pltpu.make_async_copy(source, target, sems.at[place]))
        copies[-1].start()
    copies[0].wait()
    for ex in range(EX):
        copies[1 + ex].wait()
        for pair in range(EY // 2):
            ey = 2 * pair
            values = jnp.concatenate(
                [field[ex, ey].reshape(512, LANES), field[ex, ey + 1].reshape(512, LANES)], axis=1
            )
            high, low = split(values)
            upper = dot(restrict[...], high)
            lower = dot(restrict[0:80, :], low)
            total = upper[0:80] + upper[80:160] + lower
            for h in (0, 1):
                part = total[:, h * LANES : (h + 1) * LANES]
                for i in range(4):
                    middle[ex, ey + h, i] = part[16 * i : 16 * i + 16]
                column = ex * EY + ey + h
                corners[8 * column : 8 * column + 8] = part[64:72]
    copies[EX + 1].wait()
    copies[EX + 2].wait()
    values = corners[...]
    near = exact_dot(vertex_pick[0], values)
    far = exact_dot(vertex_pick[1], values)
    total = exact_dot(near + pltpu.roll(far, 1, 1), hartley_z[...])
    vertex[...] = total

    def write_x(x_up, x_down):
        for out, ex, nodes, mids in ((x_up, EX - 1, (7, 6), (3, 2)), (x_down, 0, (0, 1), (0, 1))):
            for layer in (0, 1):
                for ey in range(EY):
                    row = (layer * EY + ey) * 64
                    out[row : row + 64] = field[ex, ey, nodes[layer]]
                    row = 512 + (layer * EY + ey) * 16
                    out[row : row + 16] = middle[ex, ey, mids[layer]]
        x_up[LAYER_ROWS:X_ROWS] = vertex[20:28]
        x_down[LAYER_ROWS:X_ROWS] = jnp.zeros((8, LANES), F32)

    for_partners("px", x_first, x_second, write_x)
    def write_y(y_up, y_down):
        for out, ey, nodes, mids in ((y_up, EY - 1, (7, 6), (3, 2)), (y_down, 0, (0, 1), (0, 1))):
            for layer in (0, 1):
                for ex in range(EX):
                    for a in range(8):
                        row = (layer * EX + ex) * 64 + a * 8
                        line = nodes[layer] * 8
                        out[row : row + 8] = field[ex, ey, a, line : line + 8]
                    for a in range(4):
                        row = 512 + (layer * EX + ex) * 16 + a * 4
                        line = mids[layer] * 4
                        out[row : row + 4] = middle[ex, ey, a, line : line + 4]
            for n, base in ((8, 0), (4, 512)):
                core = n * n
                for row in [base + k * core for k in (1, 2, 3, 5, 6, 7)]:
                    total = out[row - n : row] + out[row : row + n]
                    out[row - n : row] = total
                    out[row : row + n] = total

    for_partners("py", y_first, y_second, write_y)


def pack(residual):
    x_halo = jax.ShapeDtypeStruct((X_ROWS, LANES), F32)
    y_halo = jax.ShapeDtypeStruct((LAYER_ROWS, LANES), F32)
    vmem = pl.BlockSpec(memory_space=pltpu.VMEM)
    return pl.pallas_call(
        pack_kernel,
        out_shape=[x_halo] * 2
        + [y_halo] * 2
        + [
            jax.ShapeDtypeStruct((EX, EY, 4, 16, LANES), F32),
            jax.ShapeDtypeStruct((32, LANES), F32),
        ],
        in_specs=[pl.BlockSpec(memory_space=pltpu.HBM)] * 4,
        out_specs=[vmem] * 6,
        scratch_shapes=[
            pltpu.VMEM((EX, EY, 8, 64, LANES), F32),
            pltpu.VMEM((128, LANES), F32),
            pltpu.VMEM((160, 512), BF16),
            pltpu.VMEM((2, 32, 128), F32),
            pltpu.VMEM((128, 128), F32),
            pltpu.SemaphoreType.DMA((EX + 3,)),
        ],
        compiler_params=pltpu.CompilerParams(vmem_limit_bytes=VMEM_LIMIT),
        cost_estimate=pl.CostEstimate(flops=10**9, bytes_accessed=8 * 10**6, transcendentals=0),
        name="pack",
    )(
        residual,
        jnp.asarray(restrict_matrix()),
        jnp.asarray(vertex_matrices()),
        jnp.asarray(hartley(128), F32),
    )


def join_kernel(x_first, x_second, vertex, after, first, second, summed):
    del after
    x_low, x_high = received("px", x_first, x_second)

    def write(up, down):
        for out, ey, ends in ((up, EY - 1, True), (down, 0, False)):
            for n, base in ((8, 0), (4, 512)):
                face, inner = (n - 1, n - 2) if ends else (0, 1)
                for kind, (layer, node) in enumerate(((0, face), (0, inner), (1, face))):
                    line = base + (layer * EY + ey) * n * n + node * n
                    for side, halo in ((0, x_low), (1, x_high)):
                        row = edge_row(n, side, kind)
                        out[row : row + n] = halo[line : line + n]

    for_partners("py", first, second, write)
    total = vertex[0:8] + jnp.concatenate(
        [x_low[LAYER_ROWS : LAYER_ROWS + 5], jnp.zeros((3, LANES), F32)], axis=0
    )
    last = jnp.concatenate([vertex[16:20], jnp.zeros((4, LANES), F32)], axis=0)
    total = jnp.concatenate([total, vertex[8:16], last], axis=0)
    summed[...] = jnp.broadcast_to(total[None], summed.shape)


def join(x_halos, vertex, after, devices):
    vmem = pl.BlockSpec(memory_space=pltpu.VMEM)
    edge = jax.ShapeDtypeStruct((EDGE_ROWS, LANES), F32)
    return pl.pallas_call(
        join_kernel,
        out_shape=[edge, edge, jax.ShapeDtypeStruct((devices, VERTEX_ROWS, LANES), F32)],
        in_specs=[vmem] * 3 + [pl.BlockSpec(memory_space=pl.ANY)],
        out_specs=[vmem] * 3,
        compiler_params=pltpu.CompilerParams(vmem_limit_bytes=8 * MIB),
        cost_estimate=pl.CostEstimate(flops=10**6, bytes_accessed=10**6, transcendentals=0),
        name="join",
    )(*x_halos, vertex, after)


def join_faces_kernel(x_first, x_second, first, second):
    x_low, x_high = received("px", x_first, x_second)

    def write(up, down):
        for out, ey, ends in ((up, EY - 1, True), (down, 0, False)):
            for n, base in ((8, 0), (4, 256)):
                core = n * n
                line = base + ey * core + (core - n if ends else 0)
                for side, halo in ((0, x_low), (1, x_high)):
                    row = edge_face_row(n, side)
                    out[row : row + n] = halo[line : line + n]

    for_partners("py", first, second, write)


def join_faces(x_halos):
    vmem = pl.BlockSpec(memory_space=pltpu.VMEM)
    edge = jax.ShapeDtypeStruct((EDGE_FACE_ROWS, LANES), F32)
    return pl.pallas_call(
        join_faces_kernel,
        out_shape=[edge, edge],
        in_specs=[vmem] * 2,
        out_specs=[vmem] * 2,
        compiler_params=pltpu.CompilerParams(vmem_limit_bytes=8 * MIB),
        cost_estimate=pl.CostEstimate(flops=10**6, bytes_accessed=10**6, transcendentals=0),
        name="join_faces",
    )(*x_halos)


def sum_lines(ref, lead, n, scale=None):
    count = ref.shape[-2] // n
    low_rows = lead + (pl.ds(0, count, stride=n), slice(None))
    high_rows = lead + (pl.ds(n - 1, count, stride=n), slice(None))
    low, high = ref[low_rows], ref[high_rows]
    new_low = low + pltpu.roll(high, 1, 1)
    new_high = high + pltpu.roll(low, LANES - 1, 1)
    if scale is not None:
        new_low, new_high = new_low * scale, new_high * scale
    ref[low_rows] = new_low
    ref[high_rows] = new_high


def assemble(level, planes, rims, sides, x_low, x_high, y_low, y_high, edges):
    n, core = level.n, level.core
    last = EX * n + 3
    base = 0 if n == 8 else 512
    for ey in range(EY):
        row = base + ey * core
        planes[ey, 2] += x_low[row : row + core]
        planes[ey, last - 2] += x_high[row : row + core]
        for ex in range(EX - 1):
            left = 2 + ex * n + n - 1
            total = planes[ey, left] + planes[ey, left + 1]
            planes[ey, left] = total
            planes[ey, left + 1] = total
        row = base + (EY + ey) * core
        planes[ey, 0] = x_low[row : row + core]
        planes[ey, last] = x_high[row : row + core]
    for side, halo in ((0, y_low), (1, y_high)):
        for layer in (0, 1):
            kind = 2 * side + layer
            start = base + layer * EX * core
            sides[kind] = halo[start : start + EX * core]
            row = edge_row(n, 0, layer)
            sides[kind, 0:n] += edges[side][row : row + n]
            row = edge_row(n, 1, layer)
            sides[kind, EX * core - n : EX * core] += edges[side][row : row + n]
    for plane in range(EX * n):
        row = plane * n
        planes[0, 2 + plane, 0:n] += sides[0, row : row + n]
        planes[EY - 1, 2 + plane, core - n : core] += sides[2, row : row + n]
    for side, plane in ((0, 0), (1, last)):
        row = edge_row(n, side, 2)
        planes[0, plane, 0:n] += edges[0][row : row + n]
        planes[EY - 1, plane, core - n : core] += edges[1][row : row + n]
    for ey in range(EY - 1):
        for plane in [0, last] + list(range(2, 2 + EX * n)):
            total = planes[ey, plane, core - n : core] + planes[ey + 1, plane, 0:n]
            planes[ey, plane, core - n : core] = total
            planes[ey + 1, plane, 0:n] = total
    for ey in range(EY):
        for plane in [0, last] + list(range(2, 2 + EX * n)):
            sum_lines(planes, (ey, plane), n)
    for kind in (1, 3):
        sum_lines(sides, (kind,), n)
    for ey in range(EY):
        for plane in range(EX * n):
            at = 2 + plane
            row = plane * n
            low = planes[ey - 1, at, core - 2 * n : core - n] if ey else sides[1, row : row + n]
            high = planes[ey + 1, at, n : 2 * n] if ey < EY - 1 else sides[3, row : row + n]
            rims[ey, plane, 0:n] = low
            rims[ey, plane, n : 2 * n] = high
            rims[ey, plane, 2 * n : 3 * n] = pltpu.roll(
                planes[ey, at, pl.ds(n - 2, n, stride=n), :], 1, 1
            )
            rims[ey, plane, 3 * n : 4 * n] = pltpu.roll(
                planes[ey, at, pl.ds(1, n, stride=n), :], LANES - 1, 1
            )


def build_tables(level, tables, basis, eigen, forward, backward, lines_out):
    first, second, pick_b, pick_c, core_b, core_c = tables
    modes, depth = level.modes, level.depth
    rows_b = exact_dot(first[0:modes], basis[1], ((1,), (1,)))
    rows_c = exact_dot(second[0:modes], basis[2], ((1,), (1,)))
    matrix = exact_dot(rows_b, pick_b[...]) * exact_dot(rows_c, pick_c[...])
    high, low = split(matrix)
    keep = lax.broadcasted_iota(jnp.int32, matrix.shape, 1) < depth
    forward[0:modes] = high
    forward[modes : 2 * modes] = jnp.where(keep, low.astype(F32), 0.0).astype(BF16)
    out_b = exact_dot(exact_dot(core_b[...], basis[1]), first[...], ((1,), (1,)))
    out_c = exact_dot(exact_dot(core_c[...], basis[2]), second[...], ((1,), (1,)))
    matrix = out_b * out_c
    high, low = split(matrix)
    keep = lax.broadcasted_iota(jnp.int32, matrix.shape, 1) < modes
    backward[0 : level.core] = high
    backward[level.core : 2 * level.core] = jnp.where(keep, low.astype(F32), 0.0).astype(BF16)
    wide = level.wide
    spread_b = jnp.broadcast_to(eigen[1:2, :], (LANES, wide))
    spread_c = jnp.broadcast_to(eigen[2:3, :], (LANES, wide))
    lines = exact_dot(first[0:modes], spread_b, ((1,), (1,)))
    lines += exact_dot(second[0:modes], spread_c, ((1,), (1,)))
    lines_out[...] = lines


def first_steps(level, q, planes, rims, coeff, spectrum):
    n, wide, core, depth = level.n, level.wide, level.core, level.depth
    offsets = [0] + [2 + a for a in range(n)] + [n + 3]
    base, ey = q // 2 * n, q % 2 * 2

    def contract(load, nodes, row):
        held = [[load(h, e) for h in (0, 1)] for e in nodes]
        for i in range(wide):
            for h in (0, 1):
                total = coeff[nodes[0], i] * held[0][h]
                for position in range(1, len(nodes)):
                    total += coeff[nodes[position], i] * held[position][h]
                high, low = split(total)
                lanes = slice(h * LANES, (h + 1) * LANES)
                spectrum[i, row : row + 16, lanes] = high
                spectrum[i, depth + row : depth + row + 16, lanes] = low

    def inner(row):
        load = lambda h, e: planes[ey + h, base + offsets[e], row : row + 16]
        contract(load, list(range(wide)), row)

    def outer(row):
        load = lambda h, e: rims[ey + h, base + e - 1, row : row + 16]
        contract(load, list(range(1, n + 1)), core + row)

    steps = [functools.partial(inner, row) for row in range(0, core, 16)]
    return steps + [functools.partial(outer, row) for row in range(0, level.rim, 16)]


def last_steps(level, q, hats, coeff, scale, out):
    n, wide, core = level.n, level.wide, level.core
    ex, ey = q // 2, q % 2 * 2

    def back(h, row):
        inv = 1.0 / scale[ex, pl.ds(ey + h, 1), :]
        lanes = slice(h * LANES, (h + 1) * LANES)
        held = [hats[i, row : row + 16, lanes] for i in range(wide)]
        for a in range(n):
            total = coeff[a + 1, 0] * held[0]
            for i in range(1, wide):
                total += coeff[a + 1, i] * held[i]
            out[q, h, a, row : row + 16] = total * inv

    return [functools.partial(back, h, row) for h in (0, 1) for row in range(0, core, 16)]


def products(level, slots, forward, backward, inverse, waiting, lag):
    core, modes = level.core, level.modes
    places = waiting.shape[0]
    steps = [(spectrum, hats, i) for spectrum, hats in slots for i in range(level.wide)]
    for step in range(len(steps) + lag):
        if step < len(steps):
            spectrum, _, i = steps[step]
            both = dot(forward[...], spectrum[i])
            damp = inverse[i]
            hat = (both[0:modes] + both[modes : 2 * modes]) * jnp.concatenate([damp, damp], axis=1)
            high, low = split(hat)
            waiting[step % places, 0:modes] = high
            waiting[step % places, modes : 2 * modes] = low
        if step >= lag:
            _, hats, i = steps[step - lag]
            both = dot(backward[...], waiting[(step - lag) % places, 0 : 2 * modes])
            hats[i] = both[0:core] + both[core : 2 * core]


def tables_kernel(
    fine_basis, fine_eigen, middle_basis, middle_eigen, after, *refs
):
    del after
    fine_in, middle_in, outs = refs[:6], refs[6:12], refs[12:]
    build_tables(FINE, fine_in, fine_basis, fine_eigen, *outs[:3])
    build_tables(MID, middle_in, middle_basis, middle_eigen, *outs[3:6])
    outs[6][...] = fine_basis[0]
    outs[7][...] = middle_basis[0]


def solve_tables(fine_basis, fine_eigen, middle_basis, middle_eigen, after):
    vmem = pl.BlockSpec(memory_space=pltpu.VMEM)
    shapes = []
    for level in (FINE, MID):
        shapes += [
            jax.ShapeDtypeStruct((2 * level.modes, 2 * level.depth), BF16),
            jax.ShapeDtypeStruct((2 * level.core, 2 * level.modes), BF16),
            jax.ShapeDtypeStruct((level.modes, LANES), F32),
        ]
    shapes += [jax.ShapeDtypeStruct((level.wide, level.wide), F32) for level in (FINE, MID)]
    return pl.pallas_call(
        tables_kernel,
        out_shape=shapes,
        in_specs=[vmem] * 4 + [pl.BlockSpec(memory_space=pl.ANY)] + [vmem] * 12,
        out_specs=[vmem] * 8,
        compiler_params=pltpu.CompilerParams(vmem_limit_bytes=VMEM_LIMIT),
        cost_estimate=pl.CostEstimate(flops=10**8, bytes_accessed=10**6, transcendentals=0),
        name="tables",
    )(
        fine_basis, fine_eigen, middle_basis, middle_eigen, after,
        *[jnp.asarray(t) for level in (FINE, MID) for t in level.tables()],
    )


def schwarz_kernel(
    residual,
    middle,
    scale,
    fine_coeff,
    middle_coeff,
    x_first,
    x_second,
    y_first,
    y_second,
    edge_first,
    edge_second,
    forward,
    backward,
    lines,
    forward_m,
    backward_m,
    lines_m,
    fine_eigen,
    middle_eigen,
    fine_out,
    middle_out,
    face_first,
    face_second,
    line_first,
    line_second,
    planes,
    rims,
    sides,
    spectrum,
    hats,
    planes_m,
    rims_m,
    sides_m,
    spectrum_m,
    hats_m,
    solved,
    inverse,
    inverse_m,
    waiting,
    in_sems,
    out_sems,
):
    x_low, x_high = received("px", x_first, x_second)
    y_low, y_high = received("py", y_first, y_second)
    edges = received("py", edge_first, edge_second)
    copies = []
    for ex in range(EX):
        for ey in range(EY):
            copy = pltpu.make_async_copy(
                residual.at[ex, ey], planes.at[ey, pl.ds(2 + 8 * ex, 8)], in_sems.at[ex * EY + ey]
            )
            copy.start()
            copies.append(copy)
    for ex in range(EX):
        for ey in range(EY):
            planes_m[ey, 2 + 4 * ex : 6 + 4 * ex] = middle[ex, ey]
    assemble(MID, planes_m, rims_m, sides_m, x_low, x_high, y_low, y_high, edges)

    for level, inverse_out, lines_in, eigen in (
        (FINE, inverse, lines, fine_eigen),
        (MID, inverse_m, lines_m, middle_eigen),
    ):
        for i in range(level.wide):
            inverse_out[i] = 1.0 / (lines_in[...] + eigen[0, i])

    def middle_step(step, carry):
        pairs = [MID_GROUP * step + k for k in range(MID_GROUP)]
        for k, q in enumerate(pairs):
            for run in first_steps(MID, q, planes_m, rims_m, middle_coeff, spectrum_m.at[k]):
                run()
        slots = [(spectrum_m.at[k], hats_m.at[k]) for k in range(MID_GROUP)]
        products(MID, slots, forward_m, backward_m, inverse_m, waiting, LAG)
        for k, q in enumerate(pairs):
            for run in last_steps(MID, q, hats_m.at[k], middle_coeff, scale, middle_out):
                run()
        return carry

    lax.fori_loop(0, 8 // MID_GROUP, middle_step, 0)
    for copy in copies:
        copy.wait()
    assemble(FINE, planes, rims, sides, x_low, x_high, y_low, y_high, edges)

    def fine_step(q, carry):
        for run in first_steps(FINE, q, planes, rims, fine_coeff, spectrum):
            run()
        products(FINE, [(spectrum, hats)], forward, backward, inverse, waiting, LAG)
        for run in last_steps(FINE, q, hats, fine_coeff, scale, solved):
            run()
        pltpu.make_async_copy(solved.at[q], fine_out.at[q], out_sems.at[q]).start()
        return carry

    lax.fori_loop(0, 8, fine_step, 0)

    def write_x(x_up, x_down):
        for n, source, base in ((8, solved, 0), (4, middle_out, 256)):
            for out, ex, node in ((x_up, EX - 1, n - 1), (x_down, 0, 0)):
                for ey in range(EY):
                    row = base + ey * n * n
                    out[row : row + n * n] = source[2 * ex + ey // 2, ey % 2, node]

    for_partners("px", face_first, face_second, write_x)

    def write_y(y_up, y_down):
        for n, source, base in ((8, solved, 0), (4, middle_out, 256)):
            core = n * n
            for out, ey, node in ((y_up, EY - 1, n - 1), (y_down, 0, 0)):
                for ex in range(EX):
                    for a in range(n):
                        row = base + (ex * n + a) * n
                        out[row : row + n] = source[
                            2 * ex + ey // 2, ey % 2, a, node * n : node * n + n
                        ]
                for ex in range(1, EX):
                    row = base + ex * core
                    total = 0.5 * (out[row - n : row] + out[row : row + n])
                    out[row - n : row] = total
                    out[row : row + n] = total

    for_partners("py", line_first, line_second, write_y)
    for q in range(8):
        pltpu.make_async_copy(solved.at[q], fine_out.at[q], out_sems.at[q]).wait()


def schwarz(residual, middle, scale, fine_eigen, middle_eigen, halos, tables):
    vmem = pl.BlockSpec(memory_space=pltpu.VMEM)
    smem = pl.BlockSpec(memory_space=pltpu.SMEM)
    hbm = pl.BlockSpec(memory_space=pltpu.HBM)
    face = jax.ShapeDtypeStruct((FACE_ROWS, LANES), F32)

    def scratch(level, *group):
        return [
            pltpu.VMEM((EY, level.planes, level.core, LANES), F32),
            pltpu.VMEM((EY, EX * level.n, level.rim, LANES), F32),
            pltpu.VMEM((4, EX * level.core, LANES), F32),
            pltpu.VMEM(group + (level.wide, 2 * level.depth, 2 * LANES), BF16),
            pltpu.VMEM(group + (level.wide, level.core, 2 * LANES), F32),
        ]

    return pl.pallas_call(
        schwarz_kernel,
        out_shape=[
            jax.ShapeDtypeStruct((8, 2, 8, 64, LANES), F32),
            jax.ShapeDtypeStruct((8, 2, 4, 16, LANES), F32),
        ]
        + [face] * 4,
        in_specs=[hbm, vmem, vmem, smem, smem] + [vmem] * 12 + [smem] * 2,
        out_specs=[hbm] + [vmem] * 5,
        scratch_shapes=scratch(FINE)
        + scratch(MID, MID_GROUP)
        + [
            pltpu.VMEM((8, 2, 8, 64, LANES), F32),
            pltpu.VMEM((FINE.wide, FINE.modes, LANES), F32),
            pltpu.VMEM((MID.wide, MID.modes, LANES), F32),
            pltpu.VMEM((10, 2 * FINE.modes, 2 * LANES), BF16),
            pltpu.SemaphoreType.DMA((16,)),
            pltpu.SemaphoreType.DMA((8,)),
        ],
        compiler_params=pltpu.CompilerParams(vmem_limit_bytes=VMEM_LIMIT),
        cost_estimate=pl.CostEstimate(
            flops=10**11, bytes_accessed=12 * 10**6, transcendentals=0
        ),
        name="schwarz",
    )(residual, middle, scale, *tables[6:], *halos, *tables[:6], fine_eigen, middle_eigen)


def coarse_kernel(rows_x, gathered, table, out, held, part):
    own_x, own_y = lax.axis_index("px"), lax.axis_index("py")
    high, low = split(table[0:64])
    forward_y = jnp.concatenate([high, low], axis=0)[:, 0:80]

    def y_step(p, carry):
        slabs = []
        for lx in range(4):
            pieces = []
            for ly in range(5):
                row = p * (16 * VERTEX_ROWS) + lx * 5 + ly
                pieces.append(gathered[pl.ds(row, 16, stride=VERTEX_ROWS), :])
            slabs.append(jnp.concatenate(pieces, axis=0))
        for half in (0, 2):
            high, low = split(jnp.concatenate([slabs[half], slabs[half + 1]], axis=1))
            both = dot(forward_y, high)
            total = both[0:64] + both[64:128] + dot(forward_y[0:64], low)
            held[4 * p + half] = total[:, 0:LANES]
            held[4 * p + half + 1] = total[:, LANES : 2 * LANES]
        return carry

    lax.fori_loop(0, 8, y_step, 0, unroll=4)
    angle = 2.0 * np.pi / 32
    eigen_x = line_eigen(32)

    def x_step(chunk, carry):
        rows = pl.ds(pl.multiple_of(chunk * 8, 8), 8)
        values = [held[x, rows, :] for x in range(32)]
        even = [values[0]] + [values[x] + values[32 - x] for x in range(1, 16)] + [values[16]]
        odd = [None] + [values[x] - values[32 - x] for x in range(1, 16)]
        base = table[pl.ds(pl.multiple_of(64 + chunk * 8, 8), 8), :]
        totals = [None] * 5

        def series(wave, terms, k, start):
            total = None
            for x in range(start, len(terms), 2):
                value = float(wave(angle * (k * x % 32))) * terms[x]
                total = value if total is None else total + value
            return total

        def add(k, cosine, sine):
            damp = 1.0 / (base + float(24.0 * eigen_x[k]))
            modes = [(k, cosine)]
            if sine is not None:
                modes = [(k, cosine + sine), (32 - k, cosine - sine)]
            for kx, value in modes:
                value = value * damp
                for lx in range(5):
                    term = rows_x[lax.rem(own_x * 4 + lx, 32), kx] * value
                    totals[lx] = term if totals[lx] is None else totals[lx] + term

        for k in range(9):
            cos_a, cos_b = series(np.cos, even, k, 0), series(np.cos, even, k, 1)
            sin_a = sin_b = None
            if k > 0:
                sin_a, sin_b = series(np.sin, odd, k, 2), series(np.sin, odd, k, 1)
            add(k, cos_a + cos_b, None if k == 0 else sin_a + sin_b)
            if k < 8:
                add(16 - k, cos_a - cos_b, None if k == 0 else sin_b - sin_a)
        for lx in range(5):
            part[lx, rows, :] = totals[lx]
        return carry

    lax.fori_loop(0, 8, x_step, 0)
    own_rows = table[pl.ds(pl.multiple_of(256 + own_y * 8, 8), 8), :][:, 0:64]
    solved = jnp.concatenate([exact_dot(own_rows, part[lx]) for lx in range(5)], axis=0)
    out[...] = exact_dot(solved, table[128:256]) * (1.0 / (32 * 64 * 128))


def coarse_table():
    table_y = hartley(64)
    out = np.zeros((384, 128), np.float32)
    for q in range(16):
        for ly in range(5):
            out[0:64, ly * 16 + q] = table_y[:, (4 * q + ly) % 64]
            out[256 + 8 * q + ly, 0:64] = table_y[(4 * q + ly) % 64]
    out[64:128] = 24.0 * (line_eigen(64)[:, None] + line_eigen(128)[None, :]) + 0.5
    out[128:256] = hartley(128)
    return out


def coarse(gathered):
    vmem = pl.BlockSpec(memory_space=pltpu.VMEM)
    smem = pl.BlockSpec(memory_space=pltpu.SMEM)
    return pl.pallas_call(
        coarse_kernel,
        out_shape=jax.ShapeDtypeStruct((40, LANES), F32),
        in_specs=[smem, vmem, vmem],
        out_specs=vmem,
        scratch_shapes=[
            pltpu.VMEM((32, 64, LANES), F32),
            pltpu.VMEM((5, 64, LANES), F32),
        ],
        compiler_params=pltpu.CompilerParams(vmem_limit_bytes=16 * MIB),
        cost_estimate=pl.CostEstimate(
            flops=2 * 10**9, bytes_accessed=4 * 10**6, transcendentals=0
        ),
        name="coarse",
    )(jnp.asarray(hartley(32), F32), gathered, jnp.asarray(coarse_table()))


def average_faces(level, field, sides, x_low, x_high, y_low, y_high, edges):
    n, core = level.n, level.core
    base = 0 if n == 8 else 256

    def at(ex, ey):
        return 2 * ex + ey // 2, ey % 2

    for ey in range(EY):
        row = base + ey * core
        q, h = at(0, ey)
        field[q, h, 0] = 0.5 * (field[q, h, 0] + x_low[row : row + core])
        q, h = at(EX - 1, ey)
        field[q, h, n - 1] = 0.5 * (field[q, h, n - 1] + x_high[row : row + core])
        for ex in range(EX - 1):
            q, h = at(ex, ey)
            total = 0.5 * (field[q, h, n - 1] + field[q + 2, h, 0])
            field[q, h, n - 1] = total
            field[q + 2, h, 0] = total
    for side, halo in ((0, y_low), (1, y_high)):
        sides[side] = halo[base : base + EX * core]
        row = edge_face_row(n, 0)
        sides[side, 0:n] = 0.5 * (sides[side, 0:n] + edges[side][row : row + n])
        row, end = edge_face_row(n, 1), EX * core
        sides[side, end - n : end] = 0.5 * (sides[side, end - n : end] + edges[side][row : row + n])
    for ex in range(EX):
        for a in range(n):
            row = (ex * n + a) * n
            q, h = at(ex, 0)
            field[q, h, a, 0:n] = 0.5 * (field[q, h, a, 0:n] + sides[0, row : row + n])
            q, h = at(ex, EY - 1)
            field[q, h, a, core - n : core] = 0.5 * (
                field[q, h, a, core - n : core] + sides[1, row : row + n]
            )
            for ey in range(EY - 1):
                q, h = at(ex, ey)
                p, g = at(ex, ey + 1)
                total = 0.5 * (field[q, h, a, core - n : core] + field[p, g, a, 0:n])
                field[q, h, a, core - n : core] = total
                field[p, g, a, 0:n] = total


def finish_kernel(
    fine, middle, coarse_part, prolong, x_first, x_second, y_first, y_second, edge_first, edge_second,
    out, field, sides, field_m, sides_m, corner, result, in_sems, out_sems,
):
    copies = []
    for q in range(8):
        copy = pltpu.make_async_copy(fine.at[q], field.at[q], in_sems.at[q])
        copy.start()
        copies.append(copy)
    x_low, x_high = received("px", x_first, x_second)
    y_low, y_high = received("py", y_first, y_second)
    edges = received("py", edge_first, edge_second)
    field_m[...] = middle[...]
    average_faces(MID, field_m, sides_m, x_low, x_high, y_low, y_high, edges)
    near = coarse_part[...]
    far = pltpu.roll(near, LANES - 1, 1)
    for q in range(8):
        for h in (0, 1):
            ex, ey = q // 2, (q % 2) * 2 + h
            corner[q, h, 8:16] = jnp.zeros((8, LANES), F32)
            for i in (0, 1):
                for j in (0, 1):
                    row = (ex + i) * 8 + ey + j
                    place = i * 4 + j * 2
                    corner[q, h, place : place + 1] = near[row : row + 1]
                    corner[q, h, place + 1 : place + 2] = far[row : row + 1]
    for copy in copies:
        copy.wait()
    average_faces(FINE, field, sides, x_low, x_high, y_low, y_high, edges)

    def step(q, carry):
        for h in (0, 1):
            for a in range(4):
                sum_lines(field_m, (q, h, a), 4, 0.5)
            for a in range(8):
                sum_lines(field, (q, h, a), 8, 0.5)
        level = jnp.concatenate(
            [field_m[q, 0].reshape(64, LANES), field_m[q, 1].reshape(64, LANES)], axis=1
        )
        high, low = split(level)
        ends = jnp.concatenate([corner[q, 0], corner[q, 1]], axis=1)
        ends_high, ends_low = split(ends)
        stacked = jnp.concatenate([high, low, high, ends_high, ends_low, ends_high], axis=0)
        total = dot(prolong[...], stacked)
        for h in (0, 1):
            part = total[:, h * LANES : (h + 1) * LANES]
            result[q, h] = field[q, h] + part.reshape(8, 64, LANES)
        pltpu.make_async_copy(result.at[q], out.at[q], out_sems.at[q]).start()
        return carry

    lax.fori_loop(0, 8, step, 0, unroll=4)
    for q in range(8):
        pltpu.make_async_copy(result.at[q], out.at[q], out_sems.at[q]).wait()


def finish(fine, middle, coarse_part, halos):
    vmem = pl.BlockSpec(memory_space=pltpu.VMEM)
    hbm = pl.BlockSpec(memory_space=pl.ANY)
    return pl.pallas_call(
        finish_kernel,
        out_shape=jax.ShapeDtypeStruct((8, 2, 8, 64, LANES), F32),
        in_specs=[hbm] + [vmem] * 9,
        out_specs=hbm,
        scratch_shapes=[
            pltpu.VMEM((8, 2, 8, 64, LANES), F32),
            pltpu.VMEM((2, EX * 64, LANES), F32),
            pltpu.VMEM((8, 2, 4, 16, LANES), F32),
            pltpu.VMEM((2, EX * 16, LANES), F32),
            pltpu.VMEM((8, 2, 16, LANES), F32),
            pltpu.VMEM((8, 2, 8, 64, LANES), F32),
            pltpu.SemaphoreType.DMA((8,)),
            pltpu.SemaphoreType.DMA((8,)),
        ],
        compiler_params=pltpu.CompilerParams(vmem_limit_bytes=16 * MIB),
        cost_estimate=pl.CostEstimate(
            flops=2 * 10**9, bytes_accessed=8 * 10**6, transcendentals=0
        ),
        name="finish",
    )(fine, middle, coarse_part, jnp.asarray(prolong_matrix()), *halos)


def swap(first, second, axis):
    count = lax.axis_size(axis)
    pairs = [(i, i + 1 - 2 * (i % 2)) for i in range(count)]
    others = [(i, (i - 1 + 2 * (i % 2)) % count) for i in range(count)]
    return lax.ppermute(first, axis, pairs), lax.ppermute(second, axis, others)


def on_device(residual, scale, fine_basis, fine_eigen, middle_basis, middle_eigen):
    shape = residual.shape
    devices = lax.axis_size("px") * lax.axis_size("py")
    residual = residual.reshape(EX, EY, 8, 64, LANES)
    x_first, x_second, y_first, y_second, middle, vertex = pack(residual)
    x_halos = swap(x_first, x_second, "px")
    halos = x_halos + swap(y_first, y_second, "py")
    tables = solve_tables(fine_basis, fine_eigen, middle_basis, middle_eigen, vertex)
    edge_first, edge_second, vertex = join(x_halos, vertex, tables[7], devices)
    halos += swap(edge_first, edge_second, "py")
    gathered = lax.all_to_all(vertex, ("px", "py"), 0, 0)
    gathered = gathered.reshape(devices * VERTEX_ROWS, LANES)
    fine_solved, middle_solved, x_first, x_second, y_first, y_second = schwarz(
        residual, middle, scale, fine_eigen, middle_eigen, halos, tables
    )
    x_halos = swap(x_first, x_second, "px")
    halos = x_halos + swap(y_first, y_second, "py")
    halos += swap(*join_faces(x_halos), "py")
    coarse_part = coarse(gathered)
    return finish(fine_solved, middle_solved, coarse_part, halos).reshape(shape)


def solution(mesh):
    placed = (P("px", "py", None, None, None, None), P("px", "py", None), P(), P(), P(), P())
    return jax.shard_map(
        on_device,
        mesh=mesh,
        in_specs=placed,
        out_specs=P("px", "py", None, None, None, None),
        check_vma=False,
    )
```
